32 devices in a mesh: dom: 8 (over y, x, core), sub: 4 (over z).
Axes of the slice: x: 2, y: 2, z: 4, core: 2. Of those that a mesh axis runs over, the one named last changes fastest.
Arguments:
- features: float32 [16384, 602], P(('dom', 'sub')), may hold values from -6 to 6
- hub_features: float32 [256, 602], replicated, may hold values from -6 to 6
- low_lists: int32 [8192, 4], P(('dom', 'sub')), may hold values from 0 to 1791
- low_masks: int32 [8192, 4], P(('dom', 'sub')), may hold values 0 or 1
- high_lists: int32 [8192, 32], P(('dom', 'sub')), may hold values from 0 to 1791
- high_masks: int32 [8192, 32], P(('dom', 'sub')), may hold values 0 or 1
- hub_lists: int32 [32, 256, 16], P(('dom', 'sub')), may hold values from 0 to 1791
- hub_masks: int32 [32, 256, 16], P(('dom', 'sub')), may hold values 0 or 1
- send_rows: int32 [32, 32, 32], P(('dom', 'sub')), may hold values from 0 to 511
- labels: int32 [16384], P(('dom', 'sub')), may hold values from 0 to 40
- train_mask: int32 [16384], P(('dom', 'sub')), may hold values from 0 to 1
- stale_rows: float32 [2, 32768, 256], P(None, ('dom', 'sub')), may hold values from -4 to 4
- weight_one: float32 [1204, 256], replicated, may hold values from -2 to 2
- weight_two: float32 [512, 256], replicated, may hold values from -2 to 2
- weight_three: float32 [512, 41], replicated, may hold values from -2 to 2
- biases: float32 [553], replicated, may hold values from -1.5 to 1.5
- mean_one: float32 [1204, 256], replicated, may hold values from -0.0004272461 to 0.0004272461
- mean_two: float32 [512, 256], replicated, may hold values from -0.0004272461 to 0.0004272461
- mean_three: float32 [512, 41], replicated, may hold values from -0.0004272461 to 0.0004272461
- mean_biases: float32 [553], replicated, may hold values from -0.0017089844 to 0.0017089844
- square_one: float32 [1204, 256], replicated, may hold values from 8.676018e-10 to 3.4704073e-09
- square_two: float32 [512, 256], replicated, may hold values from 8.676018e-10 to 3.4704073e-09
- square_three: float32 [512, 41], replicated, may hold values from 8.676018e-10 to 3.4704073e-09
- square_biases: float32 [553], replicated, may hold values from 1.3881629e-08 to 5.5526517e-08
Outputs:
- grad_norm: float32 [], replicated
- loss_sum: float32 [], replicated
- train_count: float32 [], replicated
- new_one: float32 [1204, 256], replicated
- new_two: float32 [512, 256], replicated
- new_three: float32 [512, 41], replicated
- new_biases: float32 [553], replicated
- moment_one: float32 [1204, 256], replicated
- moment_two: float32 [512, 256], replicated
- moment_three: float32 [512, 41], replicated
- moment_biases: float32 [553], replicated
- second_one: float32 [1204, 256], replicated
- second_two: float32 [512, 256], replicated
- second_three: float32 [512, 41], replicated
- second_biases: float32 [553], replicated
- copy_one: bfloat16 [1204, 256], replicated
- copy_two: bfloat16 [512, 256], replicated
- copy_three: bfloat16 [512, 41], replicated
- copy_biases: bfloat16 [553], replicated
- new_stale: float32 [2, 32768, 256], P(None, ('dom', 'sub'))
The draws below stay inside these ranges and needn't reach their ends.
Inputs may be any that keep to these rules, and one draw needn't show every extreme that they name: `low_lists`: rows of a device's table, as laid out in the reference program. `send_rows`: rows of the sending device's own nodes.
All inputs are finite; a program needn't handle non-finite values. No bound on the sum of `low_masks` or of `high_masks` or of `hub_masks` on one device may be relied on, other than what follows from the above.
Results may differ from the reference program's by a relative error of at most 0.001.
Values sent between devices are 32-bit elements; how exact they have to be, the bound alone decides.
A program may use at most 128 MiB of HBM per device.

```python
import math
import jax
import jax.numpy as jnp
from jax import lax

F_IN = 602
HID = 256
CLS = 41
NLOW = 256
NHIGH = 256
K_LOW = 4
K_HIGH = 32
HUBS = 256
KH = 16
STEP = 5
NODE_DEV = 512
BLK = 32
NODES = 16384
HALO = 1024
TABLE = 1792
DEVICES = 32


def draw_train_mask(key, part):
    key = jax.random.fold_in(key, 3)
    ticket = jax.random.randint(key, (NODES,), 0, 1000)
    limit = 200 + 400 * jnp.arange(NODES, dtype=jnp.int32) // NODES
    return (ticket < limit).astype(jnp.int32)


def halves_weight(key, row_total, col_total):
    values = jnp.clip(jax.random.normal(key, (row_total, col_total), jnp.float32), -6.0, 6.0)
    factor = jnp.where(jnp.arange(row_total) >= row_total // 2, 2.0, 1.0).astype(jnp.float32)[:, None]
    return values * factor * row_total ** (-0.5)


def draw_weight_one(key, part):
    key = jax.random.fold_in(key, 5)
    return halves_weight(key, 2 * F_IN, HID)


def draw_weight_two(key, part):
    key = jax.random.fold_in(key, 7)
    return halves_weight(key, 2 * HID, HID)


def draw_weight_three(key, part):
    key = jax.random.fold_in(key, 11)
    return halves_weight(key, 2 * HID, CLS)


def with_ends(values, rng, smallest, top_value):
    extent = values.shape
    index_at = [jax.random.randint(jax.random.fold_in(rng, axis), (), 0, extent[axis]) for axis in range(len(extent))]
    values = values.at[tuple(index_at)].set(smallest)
    longest = extent.index(max(extent))
    index_at[longest] = (index_at[longest] + 1) % extent[longest]
    return values.at[tuple(index_at)].set(top_value)


def shard_levels(stream_key, shape, pieces, low, largest):
    level, own = 1.0, jax.random.fold_in(stream_key, 6)
    for position, blocks in pieces:
        draws = jnp.exp(jax.random.uniform(jax.random.fold_in(own, position), (blocks,), jnp.float32, low / len(pieces), largest / len(pieces)))
        level = level * jnp.repeat(draws, shape[position] // blocks).reshape([-1 if axis == position else 1 for axis in range(len(shape))])
    return level


def bell_draw(rng, shape, scale, most, split=(), held_as=jnp.bfloat16):
    drawn = scale * jax.random.normal(rng, shape, jnp.float32)
    if split:
        drawn = drawn * shard_levels(rng, shape, split, -0.22, 0.18)
    return jnp.clip(drawn, -most, most).astype(held_as)


def setup_inputs(seed: int = 0) -> dict:
    streams_of = jax.random.split(jax.random.key(seed), 25)
    return {
        "features": bell_draw(streams_of[0], (NODES, F_IN), 1.0, 6.0, ((0, 32),), jnp.float32),
        "hub_features": bell_draw(streams_of[1], (HUBS, F_IN), 1.0, 6.0, (), jnp.float32),
        "low_lists": with_ends(jax.random.randint(streams_of[2], (DEVICES * NLOW, K_LOW), 0, TABLE), jax.random.fold_in(streams_of[2], 1), 0, TABLE - 1).astype(jnp.int32),
        "low_masks": with_ends((jax.random.randint(streams_of[3], (DEVICES * NLOW, K_LOW), 0, 2) < 1).astype(jnp.int32), jax.random.fold_in(streams_of[3], 1), 0, 1),
        "high_lists": with_ends(jax.random.randint(streams_of[4], (DEVICES * NHIGH, K_HIGH), 0, TABLE), jax.random.fold_in(streams_of[4], 1), 0, TABLE - 1).astype(jnp.int32),
        "high_masks": with_ends((jax.random.randint(streams_of[5], (DEVICES * NHIGH, K_HIGH), 0, 4) < 3).astype(jnp.int32), jax.random.fold_in(streams_of[5], 1), 0, 1),
        "hub_lists": with_ends(jax.random.randint(streams_of[6], (DEVICES, HUBS, KH), 0, TABLE), jax.random.fold_in(streams_of[6], 1), 0, TABLE - 1).astype(jnp.int32),
        "hub_masks": with_ends((jax.random.randint(streams_of[7], (DEVICES, HUBS, KH), 0, 2) < 1).astype(jnp.int32), jax.random.fold_in(streams_of[7], 1), 0, 1),
        "send_rows": with_ends(jax.random.randint(streams_of[8], (DEVICES, DEVICES, BLK), 0, NODE_DEV), jax.random.fold_in(streams_of[8], 1), 0, NODE_DEV - 1).astype(jnp.int32),
        "labels": with_ends(jax.random.randint(streams_of[9], (NODES,), 0, CLS), jax.random.fold_in(streams_of[9], 1), 0, CLS - 1).astype(jnp.int32),
        "train_mask": draw_train_mask(jax.random.fold_in(streams_of[24], 71), 0),
        "stale_rows": bell_draw(streams_of[11], (2, DEVICES * HALO, HID), 0.5, 4.0, ((1, 32),), jnp.float32),
        "weight_one": draw_weight_one(jax.random.fold_in(streams_of[24], 71), 0),
        "weight_two": draw_weight_two(jax.random.fold_in(streams_of[24], 71), 0),
        "weight_three": draw_weight_three(jax.random.fold_in(streams_of[24], 71), 0),
        "biases": bell_draw(streams_of[15], (2 * HID + CLS,), 0.3, 1.5, (), jnp.float32),
        "mean_one": bell_draw(streams_of[16], (2 * F_IN, HID), (0.02 / 679), 0.0004272461, (), jnp.float32),
        "mean_two": bell_draw(streams_of[17], (2 * HID, HID), (0.02 / 679), 0.0004272461, (), jnp.float32),
        "mean_three": bell_draw(streams_of[18], (2 * HID, CLS), (0.02 / 679), 0.0004272461, (), jnp.float32),
        "mean_biases": bell_draw(streams_of[19], (2 * HID + CLS,), (0.08 / 679), 0.0017089844, (), jnp.float32),
        "square_one": jnp.clip(jnp.exp(jax.random.uniform(streams_of[20], (2 * F_IN, HID), jnp.float32, math.log(8.676018237174787e-10), math.log(3.470407294869915e-09))), 8.676018237174787e-10, 3.470407294869915e-09),
        "square_two": jnp.clip(jnp.exp(jax.random.uniform(streams_of[21], (2 * HID, HID), jnp.float32, math.log(8.676018237174787e-10), math.log(3.470407294869915e-09))), 8.676018237174787e-10, 3.470407294869915e-09),
        "square_three": jnp.clip(jnp.exp(jax.random.uniform(streams_of[22], (2 * HID, CLS), jnp.float32, math.log(8.676018237174787e-10), math.log(3.470407294869915e-09))), 8.676018237174787e-10, 3.470407294869915e-09),
        "square_biases": jnp.clip(jnp.exp(jax.random.uniform(streams_of[23], (2 * HID + CLS,), jnp.float32, math.log(1.388162917947966e-08), math.log(5.552651671791864e-08))), 1.388162917947966e-08, 5.552651671791864e-08),
    }


precise = lax.Precision.HIGHEST
keep_share = 0.95
smooth = 0.1
clip_level = 0.02
learn_rate = 0.03
weight_decay = 0.01
beta_first = 0.5
beta_second = 0.5
epsilon = 1e-08

@jax.custom_vjp
def low(v):
    return lax.optimization_barrier(v.astype(jnp.bfloat16)).astype(jnp.float32)

@jax.custom_vjp
def low_back(v):
    return v

def low_keep(v):
    return (low(v), None)

def low_pass(kept, grad):
    return (grad,)

def back_keep(v):
    return (v, None)

def back_low(kept, grad):
    return (low(grad),)
low.defvjp(low_keep, low_pass)
low_back.defvjp(back_keep, back_low)

def matmul_exact(left, right):
    return jnp.dot(left, right, precision=precise, preferred_element_type=jnp.float32)

def gelu_smooth(values):
    return jax.nn.gelu(values, approximate=True)

def global_index(indices, device):
    own_limit = NODE_DEV
    halo_limit = NODE_DEV + HALO
    owned = device * NODE_DEV + indices
    haloed = NODES + device * HALO + (indices - own_limit)
    hubbed = NODES + DEVICES * HALO + (indices - halo_limit)
    return jnp.where(indices < own_limit, owned, jnp.where(indices < halo_limit, haloed, hubbed)).astype(jnp.int32)

def masked_mean(table_rows, indices, selector, device):
    picked = table_rows[global_index(indices, device)]
    weights = selector.astype(jnp.float32)
    summed = lax.optimization_barrier(jnp.sum(picked * weights[:, :, None], axis=1))
    counted = jnp.maximum(lax.optimization_barrier(jnp.sum(weights, axis=1)), 1.0)
    return summed / counted[:, None]

def aggregate(table_rows, graph):
    low_lists, low_masks, high_lists, high_masks, hub_lists, hub_masks = graph

    def one_device(inputs):
        device, low_index, low_select, high_index, high_select, hub_index, hub_select = inputs
        mean_rows = jnp.concatenate([masked_mean(table_rows, low_index, low_select, device), masked_mean(table_rows, high_index, high_select, device)], axis=0)
        picked = table_rows[global_index(hub_index, device)]
        hub_part = lax.optimization_barrier(jnp.sum(picked * hub_select.astype(jnp.float32)[:, :, None], axis=1))
        return (mean_rows, hub_part)
    devices = jnp.arange(DEVICES, dtype=jnp.int32)
    mean_rows, hub_parts = lax.map(jax.checkpoint(one_device), (devices, low_lists.reshape(DEVICES, NLOW, K_LOW), low_masks.reshape(DEVICES, NLOW, K_LOW), high_lists.reshape(DEVICES, NHIGH, K_HIGH), high_masks.reshape(DEVICES, NHIGH, K_HIGH), hub_lists, hub_masks))
    return (mean_rows.reshape(NODES, table_rows.shape[1]), lax.optimization_barrier(jnp.sum(hub_parts, axis=0)))

def reference(features, hub_features, low_lists, low_masks, high_lists, high_masks, hub_lists, hub_masks, send_rows, labels, train_mask, stale_rows, weight_one, weight_two, weight_three, biases, mean_one, mean_two, mean_three, mean_biases, square_one, square_two, square_three, square_biases):
    graph = (low_lists, low_masks, high_lists, high_masks, hub_lists, hub_masks)
    offsets = (jnp.arange(DEVICES, dtype=jnp.int32) * NODE_DEV)[None, :, None]
    halo_index = (jnp.transpose(send_rows, (1, 0, 2)) + offsets).reshape(DEVICES * HALO).astype(jnp.int32)
    hub_count = lax.optimization_barrier(jnp.sum(hub_masks.astype(jnp.float32), axis=(0, 2)))
    train_weights = train_mask.astype(jnp.float32)

    def forward(params):
        layer_weights = params[:3]
        bias_all = params[3]
        bias_parts = (bias_all[:HID], bias_all[HID:2 * HID], bias_all[2 * HID:])
        owned = features
        hub_rows = hub_features
        renewed = []
        node_pre = None
        for layer_index in range(3):
            fresh_rows = owned[halo_index]
            if layer_index == 0:
                halo_rows = fresh_rows
            else:
                halo_rows = keep_share * stale_rows[layer_index - 1] + (1.0 - keep_share) * fresh_rows
                renewed.append(halo_rows)
            lookup = jnp.concatenate([owned, halo_rows, hub_rows], axis=0)
            mean_rows, hub_sum = aggregate(lookup, graph)
            node_pre = matmul_exact(jnp.concatenate([owned, mean_rows], axis=1), layer_weights[layer_index]) + bias_parts[layer_index]
            if layer_index < 2:
                hub_in = jnp.concatenate([hub_rows, hub_sum / hub_count[:, None]], axis=1)
                hub_pre = matmul_exact(hub_in, layer_weights[layer_index]) + bias_parts[layer_index]
                owned = gelu_smooth(node_pre)
                hub_rows = gelu_smooth(hub_pre)
        log_probs = jax.nn.log_softmax(node_pre, axis=1)
        onehot = (labels[:, None] == jnp.arange(CLS, dtype=jnp.int32)[None, :]).astype(jnp.float32)
        target = (1.0 - smooth) * onehot + smooth / CLS
        summed_loss = jnp.sum(-lax.optimization_barrier(jnp.sum(target * log_probs, axis=1)) * train_weights)
        counted = jnp.sum(train_weights)
        return (summed_loss / counted, (summed_loss, counted, jnp.stack(renewed)))
    params = (weight_one, weight_two, weight_three, biases)
    loss_value, pull, extras = jax.vjp(forward, params, has_aux=True)
    gradients = pull(jnp.ones_like(loss_value))[0]
    summed_loss, counted, renewed = extras
    grad_norm = jnp.sqrt(sum((jnp.sum(grad * grad) for grad in gradients)))
    factor = jnp.minimum(1.0, clip_level / (grad_norm + 1e-06))
    firsts = (mean_one, mean_two, mean_three, mean_biases)
    seconds = (square_one, square_two, square_three, square_biases)
    new_params, new_firsts, new_seconds = ([], [], [])
    for weight, grad, first, second in zip(params, gradients, firsts, seconds):
        clipped = grad * factor
        moment = beta_first * first + (1.0 - beta_first) * clipped
        squared = beta_second * second + (1.0 - beta_second) * clipped * clipped
        unbiased = moment / (1.0 - beta_first ** STEP)
        scaled = squared / (1.0 - beta_second ** STEP)
        new_params.append(weight - learn_rate * (unbiased / (jnp.sqrt(scaled) + epsilon) + weight_decay * weight))
        new_firsts.append(moment)
        new_seconds.append(squared)
    return (grad_norm, summed_loss, counted, new_params[0], new_params[1], new_params[2], new_params[3], new_firsts[0], new_firsts[1], new_firsts[2], new_firsts[3], new_seconds[0], new_seconds[1], new_seconds[2], new_seconds[3], new_params[0].astype(jnp.bfloat16), new_params[1].astype(jnp.bfloat16), new_params[2].astype(jnp.bfloat16), new_params[3].astype(jnp.bfloat16), renewed)
```

```python
import functools

import jax
import jax.numpy as jnp
from jax import lax
from jax.experimental import pallas as pl
from jax.experimental.pallas import tpu as pltpu
from jax.sharding import PartitionSpec as P

MESH = pl.DeviceIdType.MESH
F32 = jnp.float32
BF16 = jnp.bfloat16

STEP = 5
KEEP = 0.95
SMOOTH = 0.1
CLIP = 0.02
RATE = 0.03
DECAY = 0.01
EPSILON = 1e-08
CORRECT = 1.0 - 0.5**STEP
GELU_A = 0.7978845608
GELU_B = 0.044715
LANES = 128


def up(value, unit):
    return -(-value // unit) * unit


def split(values):
    high = values.astype(BF16)
    return high, (values - high.astype(F32)).astype(BF16)


def dot(left, right):
    return jnp.dot(left, right, preferred_element_type=F32)


def dot_nt(left, right):
    return lax.dot_general(left, right, (((1,), (1,)), ((), ())), preferred_element_type=F32)


def dot_tn(left, right):
    return lax.dot_general(left, right, (((0,), (0,)), ((), ())), preferred_element_type=F32)


def three(product, left, right):
    return (
        product(left[0], right[1]) + product(left[1], right[0])
    ) + product(left[0], right[0])


def gelu(v):
    return 0.5 * v * (1.0 + jnp.tanh(GELU_A * (v + GELU_B * (v * v * v))))


def gelu_slope(v):
    t = jnp.tanh(GELU_A * (v + GELU_B * (v * v * v)))
    return 0.5 * (1.0 + t) + (0.5 * GELU_A) * v * (1.0 - t * t) * (1.0 + (3.0 * GELU_B) * (v * v))


def tiles(total, step, body):
    @pl.loop(0, total // step)
    def _(index):
        body(pl.multiple_of(index * step, step))


class Sizes:
    def __init__(self, mesh, features, low_lists, high_lists, hub_lists, send_rows, weight_one, weight_three):
        self.dom, self.sub = mesh.shape["dom"], mesh.shape["sub"]
        self.devices = self.dom * self.sub
        self.nodes, self.fin = features.shape
        self.low = low_lists.shape[0]
        self.high = high_lists.shape[0]
        self.hubs = hub_lists.shape[1]
        self.blk = send_rows.shape[2]
        self.halo = self.devices * self.blk
        self.hid = weight_one.shape[1]
        self.cls = weight_three.shape[1]
        self.rows = self.nodes + self.hubs
        self.table = self.nodes + self.halo + self.hubs
        self.fpad = up(self.fin, LANES)
        self.frows = up(self.fin, 8)
        self.shift = self.fin % 8
        self.brows = up(self.fin + self.shift, 8)
        self.part = self.hubs // self.dom
        self.packed = self.blk % 16 == 0
        self.cblk = self.blk // 2 if self.packed else self.blk
        unit = 8 * self.devices
        self.off_two = 2 * self.frows
        self.off_three = self.off_two + 2 * (2 * self.hid)
        self.off_bias = self.off_three + self.hid
        self.rows_early = up(self.off_bias + 8, unit)
        self.rows_late = up(2 * self.brows, unit)


def train_kernel(
    z,
    feat, hubf, lowl, lowm, highl, highm, hubl, hubm, send, lab, tmask, stale_hbm, w1, w2, w3, bias,
    early_hbm, late_hbm, fresh_hbm, misc,
    ab, abt, sel, selt, colb, keys, xh, xl, xth, xtl, w1h, w1l, w2h, w2l, w3h, w3l,
    tb, tc, inv, q, h1h, h1l, m1h, m1l, h2h, h2l, dg0, dg1, dph, dpl, dmh, dml, eb, gown, ghub, stale, newst,
    zst, pself, labc, trainw, bulkh,
    send_a, recv_a, send_b, recv_b, send_c, recv_c, send_d, recv_d, send_e, recv_e, send_f, recv_f, send_g, recv_g,
    hs0, ha0, hb0, hg0, hs1, ha1, hb1, hg1, hs2, ha2, hb2, hg2, hs3, ha3, hb3, hg3, hs4, ha4, hb4, hg4,
    es, ea, ep, ebuf, er, ls, la, lp, lbuf, lr,
    xs, xr, hsem_s, hsem_r, gsem_s, gsem_r, lsem,
):
    d = lax.axis_index("dom")
    s = lax.axis_index("sub")
    me = d * z.sub + s
    nd, halo, hubs, hid = z.nodes, z.halo, z.hubs, z.hid
    halo0, hub0 = nd, nd + halo
    i32 = jnp.int32

    barrier = pltpu.get_barrier_semaphore()

    @pl.loop(1, z.devices)
    def _(k):
        pl.semaphore_signal(
            barrier,
            inc=1,
            device_id=(lax.rem(d + k // z.sub, z.dom), lax.rem(s + k % z.sub, z.sub)),
            device_id_type=MESH,
        )

    stale_copy = pltpu.make_async_copy(stale_hbm, stale, lsem.at[0])
    stale_copy.start()

    def remote(src, dst, ssem, rsem, pd, ps):
        return pltpu.make_async_remote_copy(
            src_ref=src, dst_ref=dst, send_sem=ssem, recv_sem=rsem, device_id=(pd, ps), device_id_type=MESH
        )

    def exchange_start(src, dst, i):
        @pl.loop(1, z.devices)
        def _(k):
            pd = lax.rem(d + k // z.sub, z.dom)
            ps = lax.rem(s + k % z.sub, z.sub)
            remote(src.at[pd * z.sub + ps], dst.at[me], xs.at[i], xr.at[i], pd, ps).start()

        dst[me] = src[me]

    def exchange_wait(src, dst, i):
        some = pl.ds(0, z.devices - 1)
        copy = remote(src.at[some], dst.at[some], xs.at[i], xr.at[i], lax.rem(d + 1, z.dom), s)
        copy.wait_recv()
        copy.wait_send()

    def hub_scatter(src, ra, i):
        @pl.loop(1, z.dom)
        def _(k):
            pd = lax.rem(d + k, z.dom)
            remote(src.at[pd], ra.at[d], hsem_s.at[i, 0], hsem_r.at[i, 0], pd, s).start()

        ra[d] = src[d]

    def hub_swap(src, ra, rb, i):
        some = pl.ds(0, z.dom - 1)
        copy = remote(src.at[some], ra.at[some], hsem_s.at[i, 0], hsem_r.at[i, 0], lax.rem(d + 1, z.dom), s)
        copy.wait_recv()
        total = ra[0]
        for k in range(1, z.dom):
            total = total + ra[k]
        rb[s] = total

        @pl.loop(1, z.sub)
        def _(k):
            ps = lax.rem(s + k, z.sub)
            remote(rb.at[s], rb.at[s], hsem_s.at[i, 1], hsem_r.at[i, 1], d, ps).start()

        copy.wait_send()

    def hub_gather(rb, rg, i):
        some = pl.ds(0, z.sub - 1)
        copy = remote(rb.at[some], rb.at[some], hsem_s.at[i, 1], hsem_r.at[i, 1], d, lax.rem(s + 1, z.sub))
        copy.wait_recv()
        total = rb[0]
        for k in range(1, z.sub):
            total = total + rb[k]
        rg[d] = total

        @pl.loop(1, z.dom)
        def _(k):
            pd = lax.rem(d + k, z.dom)
            remote(rg.at[d], rg.at[d], hsem_s.at[i, 2], hsem_r.at[i, 2], pd, s).start()

        copy.wait_send()

    def hub_end(rg, i):
        some = pl.ds(0, z.dom - 1)
        copy = remote(rg.at[some], rg.at[some], hsem_s.at[i, 2], hsem_r.at[i, 2], lax.rem(d + 1, z.dom), s)
        copy.wait_recv()
        copy.wait_send()

    def hub_value(rg):
        return rg[...].reshape(hubs, rg.shape[-1])

    def grad_scatter(src, ra, i):
        big = src.shape[0] // z.dom

        @pl.loop(1, z.dom)
        def _(k):
            pd = lax.rem(d + k, z.dom)
            remote(
                src.at[pl.ds(pl.multiple_of(pd * big, 8), big)], ra.at[d], gsem_s.at[i, 0], gsem_r.at[i, 0], pd, s
            ).start()

    def grad_swap(src, ra, rp, rb, i):
        big = src.shape[0] // z.dom
        small = big // z.sub
        some = pl.ds(0, z.dom - 1)
        ra[d] = src[pl.ds(pl.multiple_of(d * big, 8), big), :]
        copy = remote(ra.at[some], ra.at[some], gsem_s.at[i, 0], gsem_r.at[i, 0], lax.rem(d + 1, z.dom), s)
        copy.wait_recv()
        total = ra[0]
        for k in range(1, z.dom):
            total = total + ra[k]
        rp[...] = total

        @pl.loop(1, z.sub)
        def _(k):
            ps = lax.rem(s + k, z.sub)
            remote(
                rp.at[pl.ds(pl.multiple_of(ps * small, 8), small)], rb.at[s], gsem_s.at[i, 1], gsem_r.at[i, 1], d, ps
            ).start()

        copy.wait_send()

    def grad_sub_gather(src, rp, rb, res, i):
        big = src.shape[0] // z.dom
        small = big // z.sub
        some = pl.ds(0, z.sub - 1)
        rb[s] = rp[pl.ds(pl.multiple_of(s * small, 8), small), :]
        copy = remote(rb.at[some], rb.at[some], gsem_s.at[i, 1], gsem_r.at[i, 1], d, lax.rem(s + 1, z.sub))
        copy.wait_recv()
        total = rb[0]
        for k in range(1, z.sub):
            total = total + rb[k]
        mine = pl.ds(pl.multiple_of(me * small, 8), small)
        res[mine, :] = total

        @pl.loop(1, z.sub)
        def _(k):
            ps = lax.rem(s + k, z.sub)
            remote(res.at[mine], res.at[mine], gsem_s.at[i, 2], gsem_r.at[i, 2], d, ps).start()

        copy.wait_send()

    def grad_dom_gather(res, i):
        big = res.shape[0] // z.dom
        small = big // z.sub
        some = pl.ds(0, big - small)
        copy = remote(res.at[some], res.at[some], gsem_s.at[i, 2], gsem_r.at[i, 2], d, lax.rem(s + 1, z.sub))
        copy.wait_recv()
        group = pl.ds(pl.multiple_of(d * big, 8), big)

        @pl.loop(1, z.dom)
        def _(k):
            pd = lax.rem(d + k, z.dom)
            remote(res.at[group], res.at[group], gsem_s.at[i, 3], gsem_r.at[i, 3], pd, s).start()

        copy.wait_send()

    def grad_end(res, i):
        big = res.shape[0] // z.dom
        some = pl.ds(0, res.shape[0] - big)
        copy = remote(res.at[some], res.at[some], gsem_s.at[i, 3], gsem_r.at[i, 3], lax.rem(d + 1, z.dom), s)
        copy.wait_recv()
        copy.wait_send()

    def put_split(ref, rows, values):
        width = values.shape[1]
        high, rest = split(values)
        ref[rows, 0:width] = high
        ref[rows, width : 2 * width] = rest

    def both(left, right):
        width = right.shape[1] // 2
        return dot(left, right[:, width:]) + dot(left, right[:, :width])

    per_tile = 256 // z.blk

    xh[:, 512 : z.fpad] = jnp.zeros((z.rows, z.fpad - 512), BF16)
    xl[:, 512 : z.fpad] = jnp.zeros((z.rows, z.fpad - 512), BF16)
    w1h[512 : z.fpad, :] = jnp.zeros((z.fpad - 512, 2 * hid), BF16)
    w1l[512 : z.fpad, :] = jnp.zeros((z.fpad - 512, 2 * hid), BF16)
    high, rest = split(feat[...])
    xh[0:nd, 0 : z.fin] = high
    xl[0:nd, 0 : z.fin] = rest
    high, rest = split(w1[z.fin : 2 * z.fin, :])
    w1h[0 : z.fin, hid : 2 * hid] = high
    w1l[0 : z.fin, hid : 2 * hid] = rest

    def project(rows, columns):
        return three(dot, (xh[rows, :], xl[rows, :]), (w1h[:, columns], w1l[:, columns]))

    tiles(nd, 256, lambda r: put_split(tb, pl.ds(r, 256), project(pl.ds(r, 256), slice(hid, 2 * hid))))

    eye = lax.broadcasted_iota(i32, (z.blk, z.blk), 0) == lax.broadcasted_iota(i32, (z.blk, z.blk), 1)

    @pl.loop(0, z.devices)
    def _(p):
        line = jnp.broadcast_to(send[pl.ds(p, 1), :], (z.blk, z.blk))
        colb[pl.ds(pl.multiple_of(p * z.blk, z.blk), z.blk), :] = jnp.sum(
            jnp.where(eye, line, 0), axis=1, keepdims=True
        )

    def pick_tile(r):
        rows = pl.ds(r, 256)
        chosen = jnp.where(colb[rows, :] == lax.broadcasted_iota(i32, (256, nd), 1), 1.0, 0.0).astype(BF16)
        sel[rows, :] = chosen
        values = both(chosen, tb[0:nd, :])
        send_a[pl.ds(r // z.blk, per_tile)] = values.reshape(per_tile, z.blk, hid)

    tiles(halo, 256, pick_tile)
    pl.semaphore_wait(barrier, z.devices - 1)
    exchange_start(send_a, recv_a, 0)

    weights = lowm[...].astype(F32)
    inv[0 : z.low, :] = 1.0 / jnp.maximum(jnp.sum(weights, axis=1, keepdims=True), 1.0)
    weights = highm[...].astype(F32)
    inv[z.low : nd, :] = 1.0 / jnp.maximum(jnp.sum(weights, axis=1, keepdims=True), 1.0)
    diag = lax.broadcasted_iota(i32, (LANES, LANES), 0) == lax.broadcasted_iota(i32, (LANES, LANES), 1)
    for block in range(nd // LANES):
        rows = slice(block * LANES, (block + 1) * LANES)
        line = jnp.broadcast_to(lab[block : block + 1, :], (LANES, LANES))
        labc[rows, :] = jnp.sum(jnp.where(diag, line, 0), axis=1, keepdims=True)
        line = jnp.broadcast_to(tmask[block : block + 1, :].astype(F32), (LANES, LANES))
        trainw[rows, :] = jnp.sum(jnp.where(diag, line, 0.0), axis=1, keepdims=True)
    train_local = jnp.sum(jnp.sum(tmask[...].astype(F32), axis=1, keepdims=True), axis=0, keepdims=True)
    hub_local = jnp.sum(hubm[...].astype(F32), axis=1, keepdims=True)
    lane = lax.broadcasted_iota(i32, (hubs, LANES), 1)
    hs0[...] = jnp.where(lane == 0, hub_local, jnp.where(lane == 1, train_local, 0.0)).reshape(hs0.shape)
    hub_scatter(hs0, ha0, 0)

    keys[0 : z.low, 0 : lowl.shape[1]] = jnp.where(lowm[...] > 0, lowl[...], -1)
    keys[z.low : nd, 0 : highl.shape[1]] = jnp.where(highm[...] > 0, highl[...], -1)
    keys[nd : z.rows, 0 : hubl.shape[1]] = jnp.where(hubm[...] > 0, hubl[...], -1)

    def build(first, count, slots):
        width = z.table // 2

        def group(r):
            rows = pl.ds(first + r, 16)
            key = keys[rows, 0:LANES]
            for half in range(2):
                place = lax.broadcasted_iota(i32, (16, width), 1) + half * width
                total = jnp.zeros((16, width), F32)
                for k in range(slots):
                    total = total + jnp.where(key[:, k : k + 1] == place, 1.0, 0.0)
                ab[rows, half * width : (half + 1) * width] = total.astype(BF16)

        tiles(count, 16, group)

    build(0, z.low, lowl.shape[1])
    hub_swap(hs0, ha0, hb0, 0)
    build(nd, hubs, hubl.shape[1])
    hub_gather(hb0, hg0, 0)
    build(z.low, z.high, highl.shape[1])

    high, rest = split(hubf[...])
    xh[nd : z.rows, 0 : z.fin] = high
    xl[nd : z.rows, 0 : z.fin] = rest
    high, rest = split(w1[0 : z.fin, :])
    w1h[0 : z.fin, 0:hid] = high
    w1l[0 : z.fin, 0:hid] = rest
    put_split(tb, slice(hub0, z.table), project(slice(nd, z.rows), slice(hid, 2 * hid)))

    def own_tile(r):
        rows = pl.ds(r, 256)
        q[rows, :] = project(rows, slice(0, hid)) + bias[0:1, :]

    tiles(z.rows, 256, own_tile)
    high, rest = split(w2[...])
    w2h[...] = high
    w2l[...] = rest
    w3h[:, :] = jnp.zeros(w3h.shape, BF16)
    w3l[:, :] = jnp.zeros(w3l.shape, BF16)
    high, rest = split(w3[...])
    w3h[:, 0 : z.cls] = high
    w3l[:, 0 : z.cls] = rest
    hub_end(hg0, 0)
    sums = hub_value(hg0)
    inv[nd : z.rows, :] = 1.0 / sums[:, 0:1]
    misc[...] = sums[0:8, :]
    train_total = sums[0:1, 1:2]

    exchange_wait(send_a, recv_a, 0)
    put_split(tb, slice(halo0, hub0), recv_a[...].reshape(halo, hid))
    hs1[...] = both(ab[nd : z.rows, :], tb[...]).reshape(hs1.shape)
    hub_scatter(hs1, ha1, 1)

    def layer_one(r):
        rows = pl.ds(r, 256)
        pre = q[rows, :] + both(ab[rows, :], tb[...]) * inv[rows, :]
        q[rows, :] = pre
        high, rest = split(gelu(pre))
        h1h[rows, :] = high
        h1l[rows, :] = rest

    tiles(nd, 256, layer_one)
    tb[0:nd, 0:hid] = h1h[0:nd, :]
    tb[0:nd, hid : 2 * hid] = h1l[0:nd, :]

    def pick(target):
        def body(r):
            values = both(sel[pl.ds(r, 256), :], tb[0:nd, :])
            target[pl.ds(r // z.blk, per_tile)] = values.reshape(per_tile, z.blk, hid)

        tiles(halo, 256, body)

    pick(send_b)
    exchange_start(send_b, recv_b, 1)

    def turn(source, target, r_count, c_count, step=128):
        def body(r):
            for c in range(0, c_count, step):
                target[c : c + step, pl.ds(r, step)] = source[pl.ds(r, step), c : c + step].T

        tiles(r_count, step, body)

    hub_swap(hs1, ha1, hb1, 1)
    turn(ab, abt, z.rows, z.table)
    hub_gather(hb1, hg1, 1)
    turn(sel, selt, halo, nd)
    turn(xh, xth, z.rows, z.fpad)
    turn(xl, xtl, z.rows, z.fpad)
    stale_copy.wait()
    zst[...] = three(dot, split(KEEP * stale[1]), (w3h[hid : 2 * hid, :], w3l[hid : 2 * hid, :]))
    dg0[0:nd, :] = gelu_slope(q[0:nd, :])
    hub_end(hg1, 1)
    pre = q[nd : z.rows, :] + hub_value(hg1) * inv[nd : z.rows, :]
    dg0[nd : z.rows, :] = gelu_slope(pre)
    high, rest = split(gelu(pre))
    h1h[nd : z.rows, :] = high
    h1l[nd : z.rows, :] = rest
    tb[hub0 : z.table, 0:hid] = high
    tb[hub0 : z.table, hid : 2 * hid] = rest

    def own_two(r):
        rows = pl.ds(r, 256)
        q[rows, :] = three(dot, (h1h[rows, :], h1l[rows, :]), (w2h[0:hid, :], w2l[0:hid, :])) + bias[1:2, :]

    tiles(z.rows, 256, own_two)

    exchange_wait(send_b, recv_b, 1)

    def renew(slot, recv):
        newst[slot] = KEEP * stale[slot] + (1.0 - KEEP) * recv[...].reshape(halo, hid)

    renew(0, recv_b)
    put_split(tb, slice(halo0, hub0), newst[0])
    hs2[...] = both(ab[nd : z.rows, :], tb[...]).reshape(hs2.shape)
    hub_scatter(hs2, ha2, 2)

    def layer_two(r):
        rows = pl.ds(r, 256)
        mean = split(both(ab[rows, :], tb[...]) * inv[rows, :])
        m1h[rows, :] = mean[0]
        m1l[rows, :] = mean[1]
        pre = q[rows, :] + three(dot, mean, (w2h[hid : 2 * hid, :], w2l[hid : 2 * hid, :]))
        q[rows, :] = pre
        high, rest = split(gelu(pre))
        h2h[rows, :] = high
        h2l[rows, :] = rest
        put_split(tc, rows, three(dot, (high, rest), (w3h[hid : 2 * hid, :], w3l[hid : 2 * hid, :])))

    tiles(nd, 256, layer_two)
    class_lane = lax.broadcasted_iota(i32, (1, 1, LANES), 2) < LANES // 2

    def pack(values):
        groups = values.shape[0] // z.blk
        blocks = values.reshape(groups, z.blk, LANES)
        if z.packed:
            return blocks[:, : z.cblk] + pltpu.roll(blocks[:, z.cblk :], LANES // 2, 2)
        return blocks

    def unpack(blocks):
        if z.packed:
            first = jnp.where(class_lane, blocks, 0.0)
            second = jnp.where(class_lane, pltpu.roll(blocks, LANES // 2, 2), 0.0)
            blocks = jnp.concatenate([first, second], axis=1)
        return blocks.reshape(halo, LANES)

    def pick_class(r):
        values = both(sel[pl.ds(r, 256), :], tc[0:nd, :])
        send_c[pl.ds(r // z.blk, per_tile)] = pack(values)

    tiles(halo, 256, pick_class)
    exchange_start(send_c, recv_c, 2)
    hub_swap(hs2, ha2, hb2, 2)

    def own_three(r):
        rows = pl.ds(r, 256)
        pself[rows, :] = three(dot, (h2h[rows, :], h2l[rows, :]), (w3h[0:hid, :], w3l[0:hid, :])) + bias[2:3, 0:LANES]

    tiles(nd, 256, own_three)
    hub_gather(hb2, hg2, 2)
    dg1[0:nd, :] = gelu_slope(q[0:nd, :])
    hub_end(hg2, 2)
    mean = split(hub_value(hg2) * inv[nd : z.rows, :])
    m1h[nd : z.rows, :] = mean[0]
    m1l[nd : z.rows, :] = mean[1]
    pre = q[nd : z.rows, :] + three(dot, mean, (w2h[hid : 2 * hid, :], w2l[hid : 2 * hid, :]))
    high, rest = split(gelu(pre))
    h2h[nd : z.rows, :] = high
    h2l[nd : z.rows, :] = rest
    put_split(tc, slice(hub0, z.table), three(dot, (high, rest), (w3h[hid : 2 * hid, :], w3l[hid : 2 * hid, :])))
    q[nd : z.rows, :] = pre

    exchange_wait(send_c, recv_c, 2)
    put_split(tc, slice(halo0, hub0), zst[...] + (1.0 - KEEP) * unpack(recv_c[...]))
    used = lax.broadcasted_iota(i32, (256, LANES), 1)
    es[...] = jnp.zeros(es.shape, F32)
    ls[...] = jnp.zeros(ls.shape, F32)

    def head(r):
        rows = pl.ds(r, 256)
        logits = pself[rows, :] + both(ab[rows, :], tc[...]) * inv[rows, :]
        valid = used < z.cls
        top = jnp.max(jnp.where(valid, logits, -1e30), axis=1, keepdims=True)
        shifted = logits - top
        powers = jnp.where(valid, jnp.exp(jnp.where(valid, shifted, 0.0)), 0.0)
        total = jnp.sum(powers, axis=1, keepdims=True)
        log_probs = jnp.where(valid, shifted - jnp.log(total), 0.0)
        target = jnp.where(used == labc[rows, :], 1.0 - SMOOTH, 0.0) + SMOOTH / z.cls
        weight = trainw[rows, :]
        losses = jnp.sum(jnp.where(valid, -target * log_probs, 0.0), axis=1, keepdims=True) * weight
        grad = jnp.where(valid, powers / total - target, 0.0) * weight / train_total
        es[z.off_bias + 4 : z.off_bias + 5, :] = es[z.off_bias + 4 : z.off_bias + 5, :] + jnp.sum(
            grad, axis=0, keepdims=True
        )
        es[z.off_bias + 5 : z.off_bias + 6, :] = es[z.off_bias + 5 : z.off_bias + 6, :] + jnp.sum(
            losses, axis=0, keepdims=True
        )
        high, rest = split(grad)
        dph[rows, 0:LANES] = high
        dpl[rows, 0:LANES] = rest
        high, rest = split(grad * inv[rows, :])
        eb[rows, 0:LANES] = high
        eb[rows, LANES : 2 * LANES] = rest

    tiles(nd, 256, head)

    hub_class = both(abt[hub0 : z.table, 0:nd], eb[0:nd, 0 : 2 * LANES])
    hs3[...] = hub_class.reshape(hs3.shape)
    hub_scatter(hs3, ha3, 3)

    def back_class(r):
        values = both(abt[pl.ds(halo0 + r, 256), 0:nd], eb[0:nd, 0 : 2 * LANES])
        put_split(tc, pl.ds(halo0 + r, 256), values)
        send_d[pl.ds(r // z.blk, per_tile)] = pack((1.0 - KEEP) * values)

    tiles(halo, 256, back_class)
    exchange_start(send_d, recv_d, 3)
    hub_swap(hs3, ha3, hb3, 3)
    gown[0:nd, 0:LANES] = both(abt[0:nd, 0:nd], eb[0:nd, 0 : 2 * LANES])
    hub_gather(hb3, hg3, 3)

    lower = three(dot_tn, split(KEEP * stale[1]), (tc[halo0:hub0, 0:LANES], tc[halo0:hub0, LANES : 2 * LANES]))
    lower = lower + three(dot_tn, (h2h[nd : z.rows, :], h2l[nd : z.rows, :]), split(hub_class))
    ghub[:, 0:LANES] = lower
    ghub[:, LANES : 2 * LANES] = three(dot_tn, (h2h[0:nd, :], h2l[0:nd, :]), (dph[0:nd, 0:LANES], dpl[0:nd, 0:LANES]))
    dg1[nd : z.rows, :] = gelu_slope(q[nd : z.rows, :])

    hub_end(hg3, 3)
    node = three(dot_nt, split(hub_value(hg3)), (w3h[hid : 2 * hid, :], w3l[hid : 2 * hid, :])) * dg1[nd : z.rows, :]
    high, rest = split(node)
    dph[nd : z.rows, :] = high
    dpl[nd : z.rows, :] = rest

    def owned(values):
        row = lax.broadcasted_iota(i32, (hubs, 1), 0)
        share = hubs // z.devices
        mine = jnp.where(row >= me * share, 1.0, 0.0) * jnp.where(row < (me + 1) * share, 1.0, 0.0)
        return values * mine

    def hub_own(values):
        high, rest = split(owned(values))
        dmh[nd : z.rows, :] = high
        dml[nd : z.rows, :] = rest

    def column_sums(lanes):
        return jnp.sum(dmh[:, lanes].astype(F32) + dml[:, lanes].astype(F32), axis=0, keepdims=True)

    hub_own(node)
    exchange_wait(send_d, recv_d, 3)
    put_split(tc, slice(halo0, hub0), unpack(recv_d[...]))
    own_class = gown[0:nd, 0:LANES] + both(selt[...], tc[halo0:hub0, :])
    gown[0:nd, 0:LANES] = own_class
    own_class = split(own_class)
    node = (
        three(dot_nt, own_class, (w3h[hid : 2 * hid, :], w3l[hid : 2 * hid, :]))
        + three(dot_nt, (dph[0:nd, 0:LANES], dpl[0:nd, 0:LANES]), (w3h[0:hid, :], w3l[0:hid, :]))
    ) * dg1[0:nd, :]
    high, rest = split(node)
    dph[0:nd, :] = high
    dpl[0:nd, :] = rest
    dmh[0:nd, :] = high
    dml[0:nd, :] = rest

    def spread(r):
        rows = pl.ds(r, 256)
        values = three(dot_nt, (dph[rows, :], dpl[rows, :]), (w2h[hid : 2 * hid, :], w2l[hid : 2 * hid, :]))
        put_split(eb, rows, values * inv[rows, :])

    tiles(z.rows, 256, spread)
    hs4[...] = both(abt[hub0 : z.table, :], eb[...]).reshape(hs4.shape)
    hub_scatter(hs4, ha4, 4)

    def send_halo(target, factor):
        def body(r):
            values = both(abt[pl.ds(halo0 + r, 256), :], eb[...]) * factor
            target[pl.ds(r // z.blk, per_tile)] = values.reshape(per_tile, z.blk, hid)

        tiles(halo, 256, body)

    send_halo(send_e, 1.0 - KEEP)
    exchange_start(send_e, recv_e, 4)
    hub_swap(hs4, ha4, hb4, 4)

    lower = ghub[:, 0:LANES] + three(dot_tn, (h2h[0:nd, :], h2l[0:nd, :]), split(gown[0:nd, 0:LANES]))
    es[z.off_three : z.off_three + hid, :] = ghub[:, LANES : 2 * LANES] + pltpu.roll(lower, LANES // 2, 1)

    def own_back(r):
        rows = pl.ds(r, 256)
        q[rows, :] = three(dot_nt, (dph[rows, :], dpl[rows, :]), (w2h[0:hid, :], w2l[0:hid, :]))

    tiles(z.rows, 256, own_back)

    def own_table(r):
        rows = pl.ds(r, 256)
        q[rows, :] = q[rows, :] + both(abt[rows, :], eb[...])

    tiles(nd, 256, own_table)
    hub_gather(hb4, hg4, 4)
    for half in range(2):
        lanes = slice(half * LANES, (half + 1) * LANES)
        start = z.off_two + half * 2 * hid
        es[start : start + hid, :] = three(dot_tn, (h1h[...], h1l[...]), (dmh[:, lanes], dml[:, lanes]))
        es[start + hid : start + 2 * hid, :] = three(dot_tn, (m1h[...], m1l[...]), (dmh[:, lanes], dml[:, lanes]))
        es[z.off_bias + 2 + half : z.off_bias + 3 + half, :] = column_sums(lanes)

    tb[0:nd, 0:hid] = h2h[0:nd, :]
    tb[0:nd, hid : 2 * hid] = h2l[0:nd, :]
    pick(send_g)
    hub_end(hg4, 4)
    node = (hub_value(hg4) + q[nd : z.rows, :]) * dg0[nd : z.rows, :]
    high, rest = split(node)
    dph[nd : z.rows, :] = high
    dpl[nd : z.rows, :] = rest
    hub_own(node)
    put_split(eb, slice(nd, z.rows), node * inv[nd : z.rows, :])

    exchange_wait(send_e, recv_e, 4)
    put_split(tb, slice(halo0, hub0), recv_e[...].reshape(halo, hid))
    node = (q[0:nd, :] + both(selt[...], tb[halo0:hub0, :])) * dg0[0:nd, :]
    high, rest = split(node)
    dmh[0:nd, :] = high
    dml[0:nd, :] = rest
    put_split(eb, slice(0, nd), node * inv[0:nd, :])

    send_halo(send_f, 1.0)
    exchange_start(send_f, recv_f, 5)
    one_upper = three(dot, (xth[...], xtl[...]), (dmh[...], dml[...]))
    for half in range(2):
        lanes = slice(half * LANES, (half + 1) * LANES)
        es[half * z.frows : (half + 1) * z.frows, :] = one_upper[0 : z.frows, lanes]
        es[z.off_bias + half : z.off_bias + 1 + half, :] = column_sums(lanes)
    grad_scatter(es, ea, 0)

    def own_last(r):
        gown[pl.ds(r, 256), :] = both(abt[pl.ds(r, 256), :], eb[...])

    tiles(nd, 256, own_last)
    high, rest = split(both(abt[hub0 : z.table, :], eb[...]))
    dmh[nd : z.rows, :] = high
    dml[nd : z.rows, :] = rest
    grad_swap(es, ea, ep, ebuf, 0)
    grad_sub_gather(es, ep, ebuf, er, 0)
    grad_dom_gather(er, 0)

    exchange_wait(send_f, recv_f, 5)
    exchange_start(send_g, recv_g, 6)
    put_split(tb, slice(halo0, hub0), recv_f[...].reshape(halo, hid))
    high, rest = split(gown[...] + both(selt[...], tb[halo0:hub0, :]))
    dmh[0:nd, :] = high
    dml[0:nd, :] = rest
    one_lower = three(dot, (xth[...], xtl[...]), (dmh[...], dml[...]))
    for half in range(2):
        lanes = slice(half * LANES, (half + 1) * LANES)
        start = half * z.brows + z.shift
        ls[start : start + z.fin, :] = one_lower[0 : z.fin, lanes]
    grad_scatter(ls, la, 1)
    grad_end(er, 0)
    early_copy = pltpu.make_async_copy(er, early_hbm, lsem.at[1])
    early_copy.start()
    grad_swap(ls, la, lp, lbuf, 1)
    grad_sub_gather(ls, lp, lbuf, lr, 1)
    grad_dom_gather(lr, 1)
    exchange_wait(send_g, recv_g, 6)
    renew(1, recv_g)
    fresh_copy = pltpu.make_async_copy(newst, fresh_hbm, lsem.at[2])
    fresh_copy.start()
    grad_end(lr, 1)
    late_copy = pltpu.make_async_copy(lr, late_hbm, lsem.at[3])
    late_copy.start()
    early_copy.wait()
    fresh_copy.wait()
    late_copy.wait()


def train(z, *args):
    b, f, i = BF16, F32, jnp.int32
    vmem = pltpu.VMEM
    n, rows, tab, hid, halo = z.nodes, z.rows, z.table, z.hid, z.halo
    wide = (z.devices, z.blk, hid)
    thin = (z.devices, z.cblk, LANES)

    def hub_buffers(width):
        return [
            vmem((z.dom, z.part, width), f),
            vmem((z.dom, z.part, width), f),
            vmem((z.sub, z.part, width), f),
            vmem((z.dom, z.part, width), f),
        ]

    def grad_buffers(total):
        big = total // z.dom
        return [
            vmem((total, LANES), f),
            vmem((z.dom, big, LANES), f),
            vmem((big, LANES), f),
            vmem((z.sub, big // z.sub, LANES), f),
            vmem((total, LANES), f),
        ]

    scratch = [
        vmem((rows, tab), b), vmem((tab, rows), b), vmem((halo, n), b), vmem((n, halo), b), vmem((halo, 1), i),
        vmem((rows, LANES), i),
        vmem((rows, z.fpad), b), vmem((rows, z.fpad), b), vmem((z.fpad, rows), b), vmem((z.fpad, rows), b),
        vmem((z.fpad, 2 * hid), b), vmem((z.fpad, 2 * hid), b),
        vmem((2 * hid, hid), b), vmem((2 * hid, hid), b), vmem((2 * hid, LANES), b), vmem((2 * hid, LANES), b),
        vmem((tab, 2 * hid), b), vmem((tab, 2 * LANES), b), vmem((rows, 1), f), vmem((rows, hid), f),
        *[vmem((rows, hid), b) for _ in range(6)],
        vmem((rows, hid), f), vmem((rows, hid), f),
        *[vmem((rows, hid), b) for _ in range(4)],
        vmem((rows, 2 * hid), b), vmem((n, hid), f), vmem((z.hubs, hid), f),
        vmem((2, halo, hid), f), vmem((2, halo, hid), f),
        vmem((halo, LANES), f), vmem((n, LANES), f), vmem((n, 1), i), vmem((n, 1), f), vmem((8, LANES), f),
        vmem(wide, f), vmem(wide, f), vmem(wide, f), vmem(wide, f),
        vmem(thin, f), vmem(thin, f), vmem(thin, f), vmem(thin, f),
        vmem(wide, f), vmem(wide, f), vmem(wide, f), vmem(wide, f), vmem(wide, f), vmem(wide, f),
        *hub_buffers(LANES), *hub_buffers(hid), *hub_buffers(hid), *hub_buffers(LANES), *hub_buffers(hid),
        *grad_buffers(z.rows_early), *grad_buffers(z.rows_late),
        pltpu.SemaphoreType.DMA((7,)), pltpu.SemaphoreType.DMA((7,)),
        pltpu.SemaphoreType.DMA((5, 3)), pltpu.SemaphoreType.DMA((5, 3)),
        pltpu.SemaphoreType.DMA((2, 4)), pltpu.SemaphoreType.DMA((2, 4)),
        pltpu.SemaphoreType.DMA((4,)),
    ]
    inside = pl.BlockSpec(memory_space=pltpu.VMEM)
    outside = pl.BlockSpec(memory_space=pl.ANY)
    return pl.pallas_call(
        functools.partial(train_kernel, z),
        out_shape=(
            jax.ShapeDtypeStruct((z.rows_early, LANES), f),
            jax.ShapeDtypeStruct((z.rows_late, LANES), f),
            jax.ShapeDtypeStruct((2, halo, hid), f),
            jax.ShapeDtypeStruct((8, LANES), f),
        ),
        in_specs=[inside] * 11 + [outside] + [inside] * 4,
        out_specs=(outside, outside, outside, inside),
        scratch_shapes=scratch,
        compiler_params=pltpu.CompilerParams(
            collective_id=0, has_side_effects=True, vmem_limit_bytes=62 * 1024 * 1024
        ),
        name="train",
    )(*args)


def update_kernel(z, early, late, w1, w2, w3, bs, m1, m2, m3, mb, v1, v2, v3, vb,
                  o_norm, o1, o2, o3, ob, n1, n2, n3, nb, s1, s2, s3, sb, c1, c2, c3, cb):
    def squares(values):
        return jnp.sum(jnp.sum(values * values, axis=0, keepdims=True), axis=1, keepdims=True)

    whole = early[0 : z.off_bias, :]
    row = early[z.off_bias : z.off_bias + 5, :]
    norm = jnp.sqrt(squares(whole) + squares(row) + squares(late[0 : 2 * z.brows, :]))
    o_norm[...] = norm
    factor = jnp.minimum(1.0, CLIP / (norm + 1e-06))

    def renew(rows, lanes, grad, w, m, v, ow, om, ov):
        clipped = grad * factor
        moment = 0.5 * m[rows, lanes] + 0.5 * clipped
        second = 0.5 * v[rows, lanes] + 0.5 * clipped * clipped
        old = w[rows, lanes]
        om[rows, lanes] = moment
        ov[rows, lanes] = second
        ow[rows, lanes] = old - RATE * (
            (moment / CORRECT) / (jnp.sqrt(second / CORRECT) + EPSILON) + DECAY * old
        )

    low = z.fin - z.shift
    for half in range(2):
        lanes = slice(half * LANES, (half + 1) * LANES)
        e0, l0 = half * z.frows, half * z.brows
        one = (w1, m1, v1, o1, n1, s1)
        renew(slice(0, low), lanes, early[e0 : e0 + low, :], *one)
        if z.shift:
            renew(
                slice(low, low + 8), lanes, early[e0 + low : e0 + low + 8, :] + late[l0 : l0 + 8, :], *one
            )
            renew(slice(low + 8, 2 * z.fin), lanes, late[l0 + 8 : l0 + z.fin + z.shift, :], *one)
        else:
            renew(slice(low, 2 * z.fin), lanes, late[l0 : l0 + z.fin, :], *one)
        start = z.off_two + half * 2 * z.hid
        renew(slice(0, 2 * z.hid), lanes, early[start : start + 2 * z.hid, :], w2, m2, v2, o2, n2, s2)
        both = early[z.off_three : z.off_three + z.hid, :]
        if half:
            both = pltpu.roll(both, LANES // 2, 1)
        renew(
            slice(half * z.hid, (half + 1) * z.hid), slice(0, z.cls), both[:, 0 : z.cls], w3, m3, v3, o3, n3, s3
        )
    flat = jnp.concatenate([early[z.off_bias + k : z.off_bias + k + 1, :] for k in range(5)], axis=1)
    wide = slice(0, bs.shape[1])
    renew(slice(0, 1), wide, flat[:, wide], bs, mb, vb, ob, nb, sb)
    c1[...] = o1[...].astype(BF16)
    c2[...] = o2[...].astype(BF16)
    c3[...] = o3[...].astype(BF16)
    cb[...] = ob[...].astype(BF16)


def update(z, *args):
    weights = args[2:6]
    same = [jax.ShapeDtypeStruct(w.shape, F32) for w in weights]
    copies = [jax.ShapeDtypeStruct(w.shape, BF16) for w in weights]
    inside = pl.BlockSpec(memory_space=pltpu.VMEM)
    shapes = [jax.ShapeDtypeStruct((1, 1), F32), *same, *same, *same, *copies]
    return pl.pallas_call(
        functools.partial(update_kernel, z),
        out_shape=tuple(shapes),
        in_specs=[inside] * len(args),
        out_specs=tuple([inside] * len(shapes)),
        compiler_params=pltpu.CompilerParams(vmem_limit_bytes=62 * 1024 * 1024),
        name="update",
    )(*args)


def solution(mesh):
    def local(
        features, hub_features, low_lists, low_masks, high_lists, high_masks, hub_lists, hub_masks, send_rows,
        labels, train_mask, stale_rows, weight_one, weight_two, weight_three, biases,
        mean_one, mean_two, mean_three, mean_biases, square_one, square_two, square_three, square_biases,
    ):
        z = Sizes(mesh, features, low_lists, high_lists, hub_lists, send_rows, weight_one, weight_three)
        hid, cls = z.hid, z.cls
        rows = jnp.pad(biases, (0, 3 * hid - biases.shape[0])).reshape(3, hid)
        early, late, renewed, misc = train(
            z, features, hub_features, low_lists, low_masks, high_lists, high_masks, hub_lists[0], hub_masks[0],
            send_rows[0], labels.reshape(-1, LANES), train_mask.reshape(-1, LANES), stale_rows,
            weight_one, weight_two, weight_three, rows,
        )
        line = lambda v: v.reshape(1, -1)
        norm, o1, o2, o3, ob, n1, n2, n3, nb, s1, s2, s3, sb, c1, c2, c3, cb = update(
            z, early, late, weight_one, weight_two, weight_three, line(biases),
            mean_one, mean_two, mean_three, line(mean_biases),
            square_one, square_two, square_three, line(square_biases),
        )
        flat = lambda v: v.reshape(-1)
        return (
            norm[0, 0], early[z.off_bias + 5, 0], misc[0, 1],
            o1, o2, o3, flat(ob), n1, n2, n3, flat(nb), s1, s2, s3, flat(sb), c1, c2, c3, flat(cb), renewed,
        )

    spread = ("dom", "sub")
    rows, all_same, cube = P(spread, None), P(), P(spread, None, None)
    stale = P(None, spread, None)
    in_specs = (
        rows, all_same, rows, rows, rows, rows, cube, cube, cube, P(spread), P(spread), stale, *[all_same] * 12
    )
    out_specs = (*[all_same] * 19, stale)
    return jax.shard_map(local, mesh=mesh, in_specs=in_specs, out_specs=out_specs, check_vma=False)
```

```python
import functools

import jax
import jax.numpy as jnp
from jax import lax
from jax.experimental import pallas as pl
from jax.experimental.pallas import tpu as pltpu
from jax.sharding import PartitionSpec as P

MESH = pl.DeviceIdType.MESH
F32 = jnp.float32
BF16 = jnp.bfloat16

STEP = 5
KEEP = 0.95
SMOOTH = 0.1
CLIP = 0.02
RATE = 0.03
DECAY = 0.01
EPSILON = 1e-08
CORRECT = 1.0 - 0.5**STEP
GELU_A = 0.7978845608
GELU_B = 0.044715
LANES = 128


def up(value, unit):
    return -(-value // unit) * unit


def split(values):
    high = values.astype(BF16)
    return high, (values - high.astype(F32)).astype(BF16)


def dot(left, right):
    return jnp.dot(left, right, preferred_element_type=F32)


def dot_nt(left, right):
    return lax.dot_general(left, right, (((1,), (1,)), ((), ())), preferred_element_type=F32)


def dot_tn(left, right):
    return lax.dot_general(left, right, (((0,), (0,)), ((), ())), preferred_element_type=F32)


def three(product, left, right):
    return (
        product(left[0], right[1]) + product(left[1], right[0])
    ) + product(left[0], right[0])


def gelu(v):
    return 0.5 * v * (1.0 + jnp.tanh(GELU_A * (v + GELU_B * (v * v * v))))


def gelu_slope(v):
    t = jnp.tanh(GELU_A * (v + GELU_B * (v * v * v)))
    return 0.5 * (1.0 + t) + (0.5 * GELU_A) * v * (1.0 - t * t) * (1.0 + (3.0 * GELU_B) * (v * v))


def tiles(total, step, body):
    @pl.loop(0, total // step)
    def _(index):
        body(pl.multiple_of(index * step, step))


class Sizes:
    def __init__(self, mesh, features, low_lists, high_lists, hub_lists, send_rows, weight_one, weight_three):
        self.dom, self.sub = mesh.shape["dom"], mesh.shape["sub"]
        self.devices = self.dom * self.sub
        self.nodes, self.fin = features.shape
        self.low, self.k_low = low_lists.shape
        self.high, self.k_high = high_lists.shape
        self.hubs, self.k_hub = hub_lists.shape[1:]
        self.blk = send_rows.shape[2]
        self.halo = self.devices * self.blk
        self.hid = weight_one.shape[1]
        self.halves = self.hid // LANES
        self.cls = weight_three.shape[1]
        self.rows = self.nodes + self.hubs
        self.table = self.nodes + self.halo + self.hubs
        self.fpad = up(self.fin, LANES)
        self.frows = up(self.fin, 8)
        self.shift = self.fin % 8
        self.brows = up(self.fin + self.shift, 8)
        self.part = self.hubs // self.dom
        self.packed = self.blk % 16 == 0
        self.cblk = self.blk // 2 if self.packed else self.blk
        unit = 8 * self.devices
        self.at_three = self.halves * 2 * self.hid
        self.at_bias = self.halves * self.frows
        self.flat = (
            up(self.at_three + self.hid, unit),
            up(self.at_bias + 8, unit),
            up(self.halves * self.brows, unit),
        )
        self.levels = (2, self.dom // 2, self.sub)


class HubSum:
    def __init__(self, z, place, remote, buffers, sems, index):
        self.z, self.place, self.remote = z, place, remote
        self.source, self.ra, self.rb, self.out = buffers
        self.sent, self.got = sems
        self.index = index

    def put(self, values):
        self.source[...] = values.reshape(self.source.shape)

    def sems(self, phase):
        return self.sent.at[self.index, phase], self.got.at[self.index, phase]

    def over_dom(self, start, phase):
        d, s = self.place

        @pl.loop(1, self.z.dom)
        def _(k):
            pd = lax.rem(d + k, self.z.dom)
            src, dst = start(pd)
            self.remote(src, dst, *self.sems(phase), pd, s).start()

    def dom_done(self, ref, phase):
        d, s = self.place
        some = ref.at[pl.ds(0, self.z.dom - 1)]
        copy = self.remote(some, some, *self.sems(phase), lax.rem(d + 1, self.z.dom), s)
        copy.wait_recv()
        copy.wait_send()

    def scatter(self):
        d, s = self.place
        self.over_dom(lambda pd: (self.source.at[pd], self.ra.at[d]), 0)

    def swap(self):
        d, s = self.place
        self.dom_done(self.ra, 0)
        total = self.source[d]
        for k in range(1, self.z.dom):
            total = total + self.ra[lax.rem(d + k, self.z.dom)]
        self.rb[s] = total

        @pl.loop(1, self.z.sub)
        def _(k):
            ps = lax.rem(s + k, self.z.sub)
            self.remote(self.rb.at[s], self.rb.at[s], *self.sems(1), d, ps).start()

    def gather(self):
        d, s = self.place
        some = self.rb.at[pl.ds(0, self.z.sub - 1)]
        copy = self.remote(some, some, *self.sems(1), d, lax.rem(s + 1, self.z.sub))
        copy.wait_recv()
        copy.wait_send()
        total = self.rb[0]
        for k in range(1, self.z.sub):
            total = total + self.rb[k]
        self.out[d] = total
        self.over_dom(lambda pd: (self.out.at[d], self.out.at[d]), 2)

    def end(self):
        self.dom_done(self.out, 2)
        return self.out[...].reshape(self.z.hubs, self.out.shape[-1])


class FlatSum:
    def __init__(self, z, place, remote, buffers, sems, index):
        d, s = place
        self.remote, self.index = remote, index
        self.source, self.out = buffers[0], buffers[1]
        self.landed, self.parts = buffers[2:5], (buffers[0], *buffers[5:7])
        self.sent, self.got = sems
        pair = lax.rem(d, 2)
        chip = d // 2
        self.levels = (
            (2, pair, lambda j: (chip * 2 + j, s)),
            (z.dom // 2, chip, lambda j: (j * 2 + pair, s)),
            (z.sub, s, lambda j: (d, j)),
        )
        self.first, offset, rows = [], 0, self.source.shape[0]
        for size, mine, _ in self.levels:
            rows = rows // size
            self.first.append((offset, rows))
            offset = offset + mine * rows

    def sems(self, phase):
        return self.sent.at[self.index, phase], self.got.at[self.index, phase]

    def rows(self, start, count):
        return pl.ds(pl.multiple_of(start, 8), count)

    def send(self, level):
        size, mine, peer = self.levels[level]
        count = self.first[level][1]

        @pl.loop(1, size)
        def _(k):
            j = lax.rem(mine + k, size)
            self.remote(
                self.parts[level].at[self.rows(j * count, count)],
                self.landed[level].at[mine],
                *self.sems(level),
                *peer(j),
            ).start()

    def receive(self, level):
        size, mine, peer = self.levels[level]
        offset, count = self.first[level]
        ref = self.landed[level]
        some = ref.at[pl.ds(0, size - 1)]
        copy = self.remote(some, some, *self.sems(level), *peer(lax.rem(mine + 1, size)))
        copy.wait_recv()
        copy.wait_send()
        total = self.parts[level][self.rows(mine * count, count), :]
        for k in range(1, size):
            total = total + ref[lax.rem(mine + k, size)]
        if level + 1 < len(self.levels):
            self.parts[level + 1][...] = total
        else:
            self.out[self.rows(offset + mine * count, count), :] = total

    def spread(self, level):
        size, mine, peer = self.levels[level]
        offset, count = self.first[level]
        held = self.out.at[self.rows(offset + mine * count, count)]

        @pl.loop(1, size)
        def _(k):
            j = lax.rem(mine + k, size)
            self.remote(held, held, *self.sems(3 + level), *peer(j)).start()

    def collect(self, level):
        size, mine, peer = self.levels[level]
        some = self.out.at[pl.ds(0, (size - 1) * self.first[level][1])]
        copy = self.remote(some, some, *self.sems(3 + level), *peer(lax.rem(mine + 1, size)))
        copy.wait_recv()
        copy.wait_send()


HUB_SUMS = (1, 1, 1, 1, 1, 1, 2)


def train_kernel(
    z,
    feat, hubf, lowl, lowm, highl, highm, hubl, hubm, send, lab, tmask, stale_hbm, w1, w2, w3, bias,
    two_hbm, upper_hbm, lower_hbm, fresh_hbm, misc,
    ab, abt, sel, selt, colb, keyt, keys, xh, xl, xth, xtl, w1h, w1l, w2h, w2l, w3t, w3h, w3l,
    tb, tc, inv, q, magg, h1h, h1l, m1h, m1l, h2h, h2l, dg0, dg1, dph, dpl, dmh, dml, eb, gown, gthree, stale,
    zst, pself, labc, trainw, brow,
    send_a, recv_a, send_b, recv_b, send_c, recv_c, send_d, recv_d, recv_e, recv_f, send_g, recv_g,
    *rest_refs,
):
    hub_refs, flat_refs = rest_refs[: 4 * len(HUB_SUMS)], rest_refs[4 * len(HUB_SUMS) : -7]
    xs, xr, hsem_s, hsem_r, gsem_s, gsem_r, lsem = rest_refs[-7:]
    send_e, send_f = send_a, send_b
    d = lax.axis_index("dom")
    s = lax.axis_index("sub")
    me = d * z.sub + s
    nd, halo, hubs, hid, fin = z.nodes, z.halo, z.hubs, z.hid, z.fin
    halo0, hub0 = nd, nd + halo
    own, halos, hubr = slice(0, nd), slice(halo0, hub0), slice(hub0, z.table)
    hubq = slice(nd, z.rows)
    up_rows, low_rows = slice(0, hid), slice(hid, 2 * hid)
    i32 = jnp.int32
    both = range(z.halves)

    def lanes(h):
        return slice(h * LANES, (h + 1) * LANES)

    barrier = pltpu.get_barrier_semaphore()

    @pl.loop(1, z.devices)
    def _(k):
        pl.semaphore_signal(
            barrier,
            inc=1,
            device_id=(lax.rem(d + k // z.sub, z.dom), lax.rem(s + k % z.sub, z.sub)),
            device_id_type=MESH,
        )

    stale_copy = pltpu.make_async_copy(stale_hbm, stale, lsem.at[0])
    stale_copy.start()

    def remote(src, dst, ssem, rsem, pd, ps):
        return pltpu.make_async_remote_copy(
            src_ref=src, dst_ref=dst, send_sem=ssem, recv_sem=rsem, device_id=(pd, ps), device_id_type=MESH
        )

    place = (d, s)
    sums = [
        HubSum(z, place, remote, hub_refs[4 * i : 4 * i + 4], (hsem_s, hsem_r), i) for i in range(len(HUB_SUMS))
    ]
    grads = [FlatSum(z, place, remote, flat_refs[7 * i : 7 * i + 7], (gsem_s, gsem_r), i) for i in range(3)]
    two, upper, lower = grads

    def part_of(portion):
        return 1 + (z.devices - 1) * portion // 8

    def exchange_start(src, dst, i, first=0, last=8):
        @pl.loop(part_of(first), part_of(last))
        def _(k):
            pd = lax.rem(d + k // z.sub, z.dom)
            ps = lax.rem(s + k % z.sub, z.sub)
            remote(src.at[pd * z.sub + ps], dst.at[me], xs.at[i], xr.at[i], pd, ps).start()

        if first == 0:
            dst[me] = src[me]

    def exchange_wait(src, dst, i):
        some = pl.ds(0, z.devices - 1)
        copy = remote(src.at[some], dst.at[some], xs.at[i], xr.at[i], lax.rem(d + 1, z.dom), s)
        copy.wait_recv()
        copy.wait_send()

    def put_split(ref, rows, values):
        width = values.shape[1]
        high, rest = split(values)
        ref[rows, 0:width] = high
        ref[rows, width : 2 * width] = rest

    def put_pair(high_ref, rest_ref, rows, columns, values):
        high, rest = split(values)
        high_ref[rows, columns] = high
        rest_ref[rows, columns] = rest
        return high, rest

    def added(product):
        return product[:, :LANES] + product[:, LANES:]

    per_tile = 256 // z.blk

    keyt[...] = jnp.full(keyt.shape, -1, i32)
    keyt[0 : z.k_low, 0 : z.low] = jnp.where(lowm[...] > 0, lowl[...], -1)
    keyt[0 : z.k_high, z.low : nd] = jnp.where(highm[...] > 0, highl[...], -1)
    keyt[0 : z.k_hub, hubq] = jnp.where(hubm[...] > 0, hubl[...], -1)
    for block in range(z.rows // LANES):
        keys[lanes(block), :] = keyt[:, lanes(block)].T
    counts = jnp.sum(jnp.where(keys[...] >= 0, 1.0, 0.0), axis=1, keepdims=True)
    inv[own, :] = 1.0 / jnp.maximum(counts[own, :], 1.0)
    train_local = jnp.sum(jnp.sum(tmask[...].astype(F32), axis=1, keepdims=True), axis=0, keepdims=True)
    lane = lax.broadcasted_iota(i32, (hubs, LANES), 1)
    sums[0].put(jnp.where(lane == 0, counts[hubq, :], jnp.where(lane == 1, train_local, 0.0)))

    def turn(source, target, r_count, c_count, c_start=0, step=128):
        def body(r):
            for c in range(c_start, c_count, step):
                target[c : c + step, pl.ds(r, step)] = source[pl.ds(r, step), c : c + step].T

        tiles(r_count, step, body)

    pad0 = fin // 16 * 16
    xth[pad0 : z.fpad, :] = jnp.zeros((z.fpad - pad0, z.rows), BF16)
    xtl[pad0 : z.fpad, :] = jnp.zeros((z.fpad - pad0, z.rows), BF16)
    w1h[pad0 : z.fpad, :] = jnp.zeros((z.fpad - pad0, 2 * hid), BF16)
    w1l[pad0 : z.fpad, :] = jnp.zeros((z.fpad - pad0, 2 * hid), BF16)
    put_pair(xth, xtl, slice(0, fin), own, feat[...])
    turn(xth, xh, z.fpad, nd)
    turn(xtl, xl, z.fpad, nd)
    pl.semaphore_wait(barrier, z.devices - 1)
    sums[0].scatter()
    put_pair(w1h, w1l, slice(0, fin), low_rows, w1[fin : 2 * fin, :])

    def project(rows, columns):
        return three(dot, (xh[rows, :], xl[rows, :]), (w1h[:, columns], w1l[:, columns]))

    def put_halves(rows, values):
        for h in both:
            put_split(tb.at[h], rows, values[:, lanes(h)])

    tiles(nd, 256, lambda r: put_halves(pl.ds(r, 256), project(pl.ds(r, 256), low_rows)))
    sums[0].swap()

    eye = lax.broadcasted_iota(i32, (z.blk, z.blk), 0) == lax.broadcasted_iota(i32, (z.blk, z.blk), 1)

    @pl.loop(0, z.devices)
    def _(p):
        line = jnp.broadcast_to(send[pl.ds(p, 1), :], (z.blk, z.blk))
        colb[pl.ds(pl.multiple_of(p * z.blk, z.blk), z.blk), :] = jnp.sum(
            jnp.where(eye, line, 0), axis=1, keepdims=True
        )

    def sel_tile(r):
        rows = pl.ds(r, 256)
        sel[rows, :] = jnp.where(colb[rows, :] == lax.broadcasted_iota(i32, (256, nd), 1), 1.0, 0.0).astype(BF16)

    tiles(halo, 256, sel_tile)

    def pick(source, target):
        def body(r):
            values = added(dot(sel[pl.ds(r, 256), :], source[own, :]))
            target[pl.ds(r // z.blk, per_tile)] = values.reshape(per_tile, z.blk, LANES)

        tiles(halo, 256, body)

    pick(tb.at[0], send_a.at[0])
    sums[0].gather()
    for h in both:
        if h:
            pick(tb.at[h], send_a.at[h])
        exchange_start(send_a.at[h], recv_a.at[h], h)

    def build(first, count, slots):
        width = z.table // 2

        def group(r):
            rows = pl.ds(first + r, 16)
            key = keys[rows, :]
            for half in range(2):
                spot = lax.broadcasted_iota(i32, (16, width), 1) + half * width
                total = jnp.zeros((16, width), F32)
                for k in range(slots):
                    total = total + jnp.where(key[:, k : k + 1] == spot, 1.0, 0.0)
                ab[rows, half * width : (half + 1) * width] = total.astype(BF16)

        tiles(count, 16, group)

    build(0, z.low, z.k_low)
    build(nd, hubs, z.k_hub)
    hub_totals = sums[0].end()
    inv[hubq, :] = 1.0 / hub_totals[:, 0:1]
    misc[...] = hub_totals[0:8, :]
    build(z.low, z.high, z.k_high)

    put_pair(xth, xtl, slice(0, fin), hubq, hubf[...])
    turn(xth, xh, z.fpad, z.rows, nd)
    turn(xtl, xl, z.fpad, z.rows, nd)
    put_pair(w1h, w1l, slice(0, fin), up_rows, w1[0:fin, :])
    brow[...] = jnp.zeros(brow.shape, F32)
    line = bias[...].reshape(1, 2 * hid + z.cls)
    brow[0:1, :] = line[:, 0:hid]
    brow[1:2, :] = line[:, hid : 2 * hid]
    brow[2:3, 0 : z.cls] = line[:, 2 * hid : 2 * hid + z.cls]
    put_halves(hubr, project(hubq, low_rows))

    def own_tile(r):
        rows = pl.ds(r, 256)
        q[rows, :] = project(rows, up_rows) + brow[0:1, :]

    tiles(z.rows, 256, own_tile)

    def gather_local(h):
        def body(r):
            rows = pl.ds(r, 256)
            magg[rows, lanes(h)] = added(dot(ab[rows, own], tb[h, own, :]) + dot(ab[rows, hubr], tb[h, hubr, :]))

        tiles(z.rows, 256, body)

    for h in both:
        gather_local(h)
    put_pair(w2h, w2l, slice(0, 2 * hid), slice(0, hid), w2[...])
    w3t[...] = jnp.zeros(w3t.shape, F32)
    w3t[0 : z.cls, :] = w3[...]
    put_pair(w3h, w3l, slice(0, 2 * hid), slice(0, LANES), w3t[...].T)

    def with_halo(rows, h):
        return magg[rows, lanes(h)] + added(dot(ab[rows, halos], tb[h, halos, :]))

    def layer_one(h):
        def body(r):
            rows = pl.ds(r, 256)
            pre = q[rows, lanes(h)] + with_halo(rows, h) * inv[rows, :]
            q[rows, lanes(h)] = pre
            high, rest = put_pair(h1h, h1l, rows, lanes(h), gelu(pre))
            tb[h, rows, 0:LANES] = high
            tb[h, rows, LANES : 2 * LANES] = rest

        tiles(nd, 256, body)

    def first_half():
        exchange_wait(send_a.at[0], recv_a.at[0], 0)
        put_split(tb.at[0], halos, recv_a[0].reshape(halo, LANES))
        sums[1].put(with_halo(hubq, 0))
        sums[1].scatter()
        layer_one(0)
        pick(tb.at[0], send_b.at[0])
        exchange_start(send_b.at[0], recv_b.at[0], 2, 0, 4)

    first_half()
    exchange_wait(send_a.at[1], recv_a.at[1], 1)
    sums[1].swap()
    put_split(tb.at[1], halos, recv_a[1].reshape(halo, LANES))
    sums[2].put(with_halo(hubq, 1))
    sums[2].scatter()
    exchange_start(send_b.at[0], recv_b.at[0], 2, 4, 8)
    layer_one(1)
    pick(tb.at[1], send_b.at[1])
    sums[1].gather()
    sums[2].swap()
    exchange_start(send_b.at[1], recv_b.at[1], 3, 0, 4)
    turn(ab, abt, z.rows, z.table)
    sums[2].gather()
    exchange_start(send_b.at[1], recv_b.at[1], 3, 4, 8)

    turn(sel, selt, halo, nd)
    stale_copy.wait()
    zst[...] = three(dot, split(KEEP * stale[1]), (w3h[low_rows, :], w3l[low_rows, :]))
    dg0[own, :] = gelu_slope(q[own, :])
    for block in range(nd // LANES):
        diag = lax.broadcasted_iota(i32, (LANES, LANES), 0) == lax.broadcasted_iota(i32, (LANES, LANES), 1)
        line = jnp.broadcast_to(lab[block : block + 1, :], (LANES, LANES))
        labc[lanes(block), :] = jnp.sum(jnp.where(diag, line, 0), axis=1, keepdims=True)
        line = jnp.broadcast_to(tmask[block : block + 1, :].astype(F32), (LANES, LANES))
        trainw[lanes(block), :] = jnp.sum(jnp.where(diag, line, 0.0), axis=1, keepdims=True)
    for h in both:
        pre = q[hubq, lanes(h)] + sums[1 + h].end() * inv[hubq, :]
        dg0[hubq, lanes(h)] = gelu_slope(pre)
        high, rest = put_pair(h1h, h1l, hubq, lanes(h), gelu(pre))
        tb[h, hubr, 0:LANES] = high
        tb[h, hubr, LANES : 2 * LANES] = rest

    for h in both:
        gather_local(h)

    def own_two(r):
        rows = pl.ds(r, 256)
        q[rows, :] = three(dot, (h1h[rows, :], h1l[rows, :]), (w2h[up_rows, :], w2l[up_rows, :])) + brow[1:2, :]

    tiles(z.rows, 256, own_two)

    def second(h):
        exchange_wait(send_b.at[h], recv_b.at[h], 2 + h)
        renewed = KEEP * stale[0, :, lanes(h)] + (1.0 - KEEP) * recv_b[h].reshape(halo, LANES)
        stale[0, :, lanes(h)] = renewed
        put_split(tb.at[h], halos, renewed)
        sums[3 + h].put(with_halo(hubq, h))
        sums[3 + h].scatter()

        def body(r):
            rows = pl.ds(r, 256)
            put_pair(m1h, m1l, rows, lanes(h), with_halo(rows, h) * inv[rows, :])

        tiles(nd, 256, body)

    second(0)
    sums[3].swap()
    second(1)
    sums[3].gather()

    def layer_two(r):
        rows = pl.ds(r, 256)
        pre = q[rows, :] + three(dot, (m1h[rows, :], m1l[rows, :]), (w2h[low_rows, :], w2l[low_rows, :]))
        q[rows, :] = pre
        high, rest = put_pair(h2h, h2l, rows, slice(0, hid), gelu(pre))
        put_split(tc, rows, three(dot, (high, rest), (w3h[low_rows, :], w3l[low_rows, :])))

    tiles(nd, 256, layer_two)
    class_lane = lax.broadcasted_iota(i32, (1, 1, LANES), 2) < LANES // 2

    def pack(values):
        blocks = values.reshape(values.shape[0] // z.blk, z.blk, LANES)
        if z.packed:
            return blocks[:, : z.cblk] + pltpu.roll(blocks[:, z.cblk :], LANES // 2, 2)
        return blocks

    def unpack(blocks):
        if z.packed:
            first = jnp.where(class_lane, blocks, 0.0)
            second = jnp.where(class_lane, pltpu.roll(blocks, LANES // 2, 2), 0.0)
            blocks = jnp.concatenate([first, second], axis=1)
        return blocks.reshape(halo, LANES)

    def pick_class(r):
        send_c[pl.ds(r // z.blk, per_tile)] = pack(added(dot(sel[pl.ds(r, 256), :], tc[own, :])))

    tiles(halo, 256, pick_class)
    sums[4].swap()
    exchange_start(send_c, recv_c, 4)

    def pick_wide(r):
        chosen = sel[pl.ds(r, 256), :]
        values = dot(chosen, h2l[own, :]) + dot(chosen, h2h[own, :])
        send_g[pl.ds(r // z.blk, per_tile)] = values.reshape(per_tile, z.blk, hid)

    tiles(halo, 256, pick_wide)
    sums[4].gather()
    exchange_start(send_g, recv_g, 5, 0, 3)

    def own_three(r):
        rows = pl.ds(r, 256)
        pself[rows, :] = three(dot, (h2h[rows, :], h2l[rows, :]), (w3h[up_rows, :], w3l[up_rows, :])) + brow[2:3, 0:LANES]

    tiles(nd, 256, own_three)
    dg1[own, :] = gelu_slope(q[own, :])
    for h in both:
        put_pair(m1h, m1l, hubq, lanes(h), sums[3 + h].end() * inv[hubq, :])
    pre = q[hubq, :] + three(dot, (m1h[hubq, :], m1l[hubq, :]), (w2h[low_rows, :], w2l[low_rows, :]))
    high, rest = put_pair(h2h, h2l, hubq, slice(0, hid), gelu(pre))
    put_split(tc, hubr, three(dot, (high, rest), (w3h[low_rows, :], w3l[low_rows, :])))
    q[hubq, :] = pre

    def class_local(r):
        rows = pl.ds(r, 256)
        magg[rows, 0:LANES] = added(dot(ab[rows, own], tc[own, :]) + dot(ab[rows, hubr], tc[hubr, :]))

    tiles(nd, 256, class_local)

    two.source[...] = jnp.zeros(two.source.shape, F32)
    upper.source[...] = jnp.zeros(upper.source.shape, F32)
    lower.source[...] = jnp.zeros(lower.source.shape, F32)
    exchange_wait(send_c, recv_c, 4)
    put_split(tc, halos, zst[...] + (1.0 - KEEP) * unpack(recv_c[...]))
    used = lax.broadcasted_iota(i32, (256, LANES), 1)
    train_total = misc[0:1, 1:2]
    at_bias = z.at_bias

    def head(r):
        rows = pl.ds(r, 256)
        logits = pself[rows, :] + (magg[rows, 0:LANES] + added(dot(ab[rows, halos], tc[halos, :]))) * inv[rows, :]
        valid = used < z.cls
        top = jnp.max(jnp.where(valid, logits, -1e30), axis=1, keepdims=True)
        shifted = logits - top
        powers = jnp.where(valid, jnp.exp(jnp.where(valid, shifted, 0.0)), 0.0)
        total = jnp.sum(powers, axis=1, keepdims=True)
        log_probs = jnp.where(valid, shifted - jnp.log(total), 0.0)
        target = jnp.where(used == labc[rows, :], 1.0 - SMOOTH, 0.0) + SMOOTH / z.cls
        weight = trainw[rows, :]
        losses = jnp.sum(jnp.where(valid, -target * log_probs, 0.0), axis=1, keepdims=True) * weight
        grad = jnp.where(valid, powers / total - target, 0.0) * weight / train_total
        at = at_bias + 2 * z.halves
        upper.source[at : at + 1, :] = upper.source[at : at + 1, :] + jnp.sum(grad, axis=0, keepdims=True)
        at = at + 1
        upper.source[at : at + 1, :] = upper.source[at : at + 1, :] + jnp.sum(losses, axis=0, keepdims=True)
        put_pair(dph, dpl, rows, slice(0, LANES), grad)
        put_split(eb.at[0], rows, grad * inv[rows, :])

    tiles(nd, 256, head)

    sums[5].put(added(dot(abt[hubr, own], eb[0, own, :])))
    sums[5].scatter()

    def back_class(r):
        values = added(dot(abt[pl.ds(halo0 + r, 256), own], eb[0, own, :]))
        put_split(tc, pl.ds(halo0 + r, 256), values)
        send_d[pl.ds(r // z.blk, per_tile)] = pack((1.0 - KEEP) * values)

    tiles(halo, 256, back_class)
    sums[5].swap()
    exchange_start(send_d, recv_d, 6)
    gown[own, 0:LANES] = added(dot(abt[own, own], eb[0, own, :]))

    gthree[:, 0:LANES] = three(dot_tn, split(KEEP * stale[1]), (tc[halos, 0:LANES], tc[halos, LANES : 2 * LANES]))
    sums[5].gather()
    exchange_start(send_g, recv_g, 5, 3, 6)
    hub_class = split(sums[5].source[...].reshape(hubs, LANES))
    gthree[:, 0:LANES] = gthree[:, 0:LANES] + three(dot_tn, (h2h[hubq, :], h2l[hubq, :]), hub_class)
    gthree[:, LANES : 2 * LANES] = three(dot_tn, (h2h[own, :], h2l[own, :]), (dph[own, 0:LANES], dpl[own, 0:LANES]))
    dg1[hubq, :] = gelu_slope(q[hubq, :])

    def self_two(r):
        rows = pl.ds(r, 256)
        magg[rows, :] = three(
            dot_nt, (dph[rows, 0:LANES], dpl[rows, 0:LANES]), (w3h[up_rows, :], w3l[up_rows, :])
        )

    tiles(nd, 256, self_two)

    def owned(values):
        row = lax.broadcasted_iota(i32, (hubs, 1), 0)
        share = hubs // z.devices
        mine = jnp.where(row >= me * share, 1.0, 0.0) * jnp.where(row < (me + 1) * share, 1.0, 0.0)
        return values * mine

    def column_sums(columns):
        return jnp.sum(dmh[:, columns].astype(F32) + dml[:, columns].astype(F32), axis=0, keepdims=True)

    node = three(dot_nt, split(sums[5].end()), (w3h[low_rows, :], w3l[low_rows, :])) * dg1[hubq, :]
    put_pair(dph, dpl, hubq, slice(0, hid), node)
    put_pair(dmh, dml, hubq, slice(0, hid), owned(node))

    def spread(rows):
        values = three(dot_nt, (dph[rows, :], dpl[rows, :]), (w2h[low_rows, :], w2l[low_rows, :])) * inv[rows, :]
        for h in both:
            put_split(eb.at[h], rows, values[:, lanes(h)])

    spread(hubq)
    exchange_wait(send_d, recv_d, 6)
    put_split(tc, halos, unpack(recv_d[...]))

    def back_two(r):
        rows = pl.ds(r, 256)
        own_class = gown[rows, 0:LANES] + added(dot(selt[rows, :], tc[halos, :]))
        gown[rows, 0:LANES] = own_class
        node = (
            three(dot_nt, split(own_class), (w3h[low_rows, :], w3l[low_rows, :])) + magg[rows, :]
        ) * dg1[rows, :]
        high, rest = put_pair(dph, dpl, rows, slice(0, hid), node)
        dmh[rows, :] = high
        dml[rows, :] = rest
        spread(rows)

    tiles(nd, 256, back_two)

    for h in both:
        sums[6].source[:, :, lanes(h)] = added(dot(abt[hubr, :], eb[h])).reshape(z.dom, z.part, LANES)
    sums[6].scatter()

    def send_halo(target, factor, h):
        def body(r):
            values = added(dot(abt[pl.ds(halo0 + r, 256), :], eb[h])) * factor
            target[pl.ds(r // z.blk, per_tile)] = values.reshape(per_tile, z.blk, LANES)

        tiles(halo, 256, body)

    send_halo(send_e.at[0], 1.0 - KEEP, 0)
    exchange_start(send_e.at[0], recv_e.at[0], 7, 0, 4)
    sums[6].swap()
    exchange_start(send_e.at[0], recv_e.at[0], 7, 4, 8)
    send_halo(send_e.at[1], 1.0 - KEEP, 1)
    sums[6].gather()
    exchange_start(send_e.at[1], recv_e.at[1], 8, 0, 4)

    def own_back(r):
        rows = pl.ds(r, 256)
        q[rows, :] = three(dot_nt, (dph[rows, :], dpl[rows, :]), (w2h[up_rows, :], w2l[up_rows, :]))

    tiles(z.rows, 256, own_back)

    def own_table(r):
        rows = pl.ds(r, 256)
        for h in both:
            q[rows, lanes(h)] = q[rows, lanes(h)] + added(dot(abt[rows, :], eb[h]))

    tiles(nd, 256, own_table)
    gthree[:, 0:LANES] = gthree[:, 0:LANES] + three(dot_tn, (h2h[own, :], h2l[own, :]), split(gown[own, 0:LANES]))
    two.source[z.at_three : z.at_three + hid, :] = gthree[:, LANES : 2 * LANES] + pltpu.roll(
        gthree[:, 0:LANES], LANES // 2, 1
    )
    for h in both:
        start = h * 2 * hid
        pair = (dmh[:, lanes(h)], dml[:, lanes(h)])
        two.source[start : start + hid, :] = three(dot_tn, (h1h[...], h1l[...]), pair)
        two.source[start + hid : start + 2 * hid, :] = three(dot_tn, (m1h[...], m1l[...]), pair)
        at = at_bias + z.halves + h
        upper.source[at : at + 1, :] = column_sums(lanes(h))
    two.send(0)
    exchange_start(send_e.at[1], recv_e.at[1], 8, 4, 8)

    node = (sums[6].end() + q[hubq, :]) * dg0[hubq, :]
    put_pair(dmh, dml, hubq, slice(0, hid), owned(node))
    node = node * inv[hubq, :]
    for h in both:
        put_split(eb.at[h], hubq, node[:, lanes(h)])

    def back_one(h):
        exchange_wait(send_e.at[h], recv_e.at[h], 7 + h)
        put_split(tb.at[h], halos, recv_e[h].reshape(halo, LANES))

        def body(r):
            rows = pl.ds(r, 256)
            node = (q[rows, lanes(h)] + added(dot(selt[rows, :], tb[h, halos, :]))) * dg0[rows, lanes(h)]
            put_pair(dmh, dml, rows, lanes(h), node)
            put_split(eb.at[h], rows, node * inv[rows, :])

        tiles(nd, 256, body)
        send_halo(send_f.at[h], 1.0, h)

    back_one(0)
    exchange_start(send_f.at[0], recv_f.at[0], 9)
    two.receive(0)
    two.send(1)
    back_one(1)
    exchange_start(send_f.at[1], recv_f.at[1], 10, 0, 4)
    two.receive(1)
    two.send(2)
    for h in both:
        top = three(dot, (xth[...], xtl[...]), (dmh[:, lanes(h)], dml[:, lanes(h)]))
        upper.source[h * z.frows : (h + 1) * z.frows, :] = top[0 : z.frows, :]
        upper.source[at_bias + h : at_bias + h + 1, :] = column_sums(lanes(h))
    upper.send(0)
    exchange_start(send_f.at[1], recv_f.at[1], 10, 4, 8)
    two.receive(2)
    two.spread(2)

    def own_last(r):
        rows = pl.ds(r, 256)
        for h in both:
            gown[rows, lanes(h)] = added(dot(abt[rows, :], eb[h]))

    tiles(nd, 256, own_last)
    for h in both:
        put_pair(dmh, dml, hubq, lanes(h), added(dot(abt[hubr, :], eb[h])))
    upper.receive(0)
    upper.send(1)
    two.collect(2)
    two.spread(1)

    def last(h):
        exchange_wait(send_f.at[h], recv_f.at[h], 9 + h)
        put_split(tb.at[h], halos, recv_f[h].reshape(halo, LANES))

        def body(r):
            rows = pl.ds(r, 256)
            put_pair(dmh, dml, rows, lanes(h), gown[rows, lanes(h)] + added(dot(selt[rows, :], tb[h, halos, :])))

        tiles(nd, 256, body)
        bottom = three(dot, (xth[...], xtl[...]), (dmh[:, lanes(h)], dml[:, lanes(h)]))
        start = h * z.brows + z.shift
        lower.source[start : start + fin, :] = bottom[0:fin, :]

    last(0)
    two.collect(1)
    two.spread(0)
    upper.receive(1)
    upper.send(2)
    last(1)
    lower.send(0)
    exchange_start(send_g, recv_g, 5, 6, 8)
    upper.receive(2)
    upper.spread(2)
    two.collect(0)
    two_copy = pltpu.make_async_copy(two.out, two_hbm, lsem.at[1])
    two_copy.start()
    lower.receive(0)
    lower.send(1)
    upper.collect(2)
    upper.spread(1)
    lower.receive(1)
    lower.send(2)
    upper.collect(1)
    upper.spread(0)
    lower.receive(2)
    lower.spread(2)
    exchange_wait(send_g, recv_g, 5)
    stale[1] = KEEP * stale[1] + (1.0 - KEEP) * recv_g[...].reshape(halo, hid)
    fresh_copy = pltpu.make_async_copy(stale, fresh_hbm, lsem.at[2])
    fresh_copy.start()
    lower.collect(2)
    lower.spread(1)
    upper.collect(0)
    upper_copy = pltpu.make_async_copy(upper.out, upper_hbm, lsem.at[3])
    upper_copy.start()
    lower.collect(1)
    lower.spread(0)
    lower.collect(0)
    lower_copy = pltpu.make_async_copy(lower.out, lower_hbm, lsem.at[4])
    lower_copy.start()
    two_copy.wait()
    fresh_copy.wait()
    upper_copy.wait()
    lower_copy.wait()


def train(z, *args):
    b, f, i = BF16, F32, jnp.int32
    vmem = pltpu.VMEM
    n, rows, tab, hid, halo = z.nodes, z.rows, z.table, z.hid, z.halo
    wide = (z.halves, z.devices, z.blk, LANES)
    bulk = (z.devices, z.blk, hid)
    thin = (z.devices, z.cblk, LANES)

    def hub_buffers(count):
        width = count * LANES
        return [
            vmem((z.dom, z.part, width), f),
            vmem((z.dom, z.part, width), f),
            vmem((z.sub, z.part, width), f),
            vmem((z.dom, z.part, width), f),
        ]

    def flat_buffers(total):
        landed, parts, rest = [], [], total
        for size in z.levels:
            rest = rest // size
            landed.append(vmem((size, rest, LANES), f))
            parts.append(vmem((rest, LANES), f))
        return [vmem((total, LANES), f), vmem((total, LANES), f), *landed, *parts[:2]]

    def pairs(count, *shape):
        return [vmem(shape, b) for _ in range(2 * count)]

    scratch = [
        vmem((rows, tab), b), vmem((tab, rows), b), vmem((halo, n), b), vmem((n, halo), b), vmem((halo, 1), i),
        vmem((LANES, rows), i), vmem((rows, LANES), i),
        *pairs(1, rows, z.fpad), *pairs(1, z.fpad, rows), *pairs(1, z.fpad, 2 * hid), *pairs(1, 2 * hid, hid),
        vmem((LANES, 2 * hid), f), *pairs(1, 2 * hid, LANES),
        vmem((z.halves, tab, 2 * LANES), b), vmem((tab, 2 * LANES), b), vmem((rows, 1), f), vmem((rows, hid), f),
        vmem((rows, hid), f),
        *pairs(3, rows, hid),
        vmem((rows, hid), f), vmem((rows, hid), f),
        *pairs(2, rows, hid),
        vmem((z.halves, rows, 2 * LANES), b), vmem((n, hid), f), vmem((hid, 2 * LANES), f),
        vmem((2, halo, hid), f),
        vmem((halo, LANES), f), vmem((n, LANES), f), vmem((n, 1), i), vmem((n, 1), f), vmem((8, hid), f),
        *[vmem(shape, f) for shape in (wide, wide, wide, wide, thin, thin, thin, thin, wide, wide, bulk, bulk)],
    ]
    for count in HUB_SUMS:
        scratch += hub_buffers(count)
    for total in z.flat:
        scratch += flat_buffers(total)
    dma = pltpu.SemaphoreType.DMA
    scratch += [
        dma((11,)), dma((11,)), dma((len(HUB_SUMS), 3)), dma((len(HUB_SUMS), 3)), dma((3, 6)), dma((3, 6)), dma((5,))
    ]
    inside = pl.BlockSpec(memory_space=pltpu.VMEM)
    outside = pl.BlockSpec(memory_space=pl.ANY)
    return pl.pallas_call(
        functools.partial(train_kernel, z),
        out_shape=(
            *[jax.ShapeDtypeStruct((total, LANES), f) for total in z.flat],
            jax.ShapeDtypeStruct((2, halo, hid), f),
            jax.ShapeDtypeStruct((8, LANES), f),
        ),
        in_specs=[inside] * 11 + [outside] + [inside] * 4,
        out_specs=(outside, outside, outside, outside, inside),
        scratch_shapes=scratch,
        compiler_params=pltpu.CompilerParams(
            collective_id=0, has_side_effects=True, vmem_limit_bytes=62 * 1024 * 1024
        ),
        name="train",
    )(*args)


def update_kernel(z, two, upper, lower, misc, fresh, w1, w2, w3, bs, m1, m2, m3, mb, v1, v2, v3, vb,
                  o_norm, o_loss, o_count, o_fresh, o1, o2, o3, ob, n1, n2, n3, nb, s1, s2, s3, sb, c1, c2, c3, cb,
                  held, sem):
    taken = pltpu.make_async_copy(fresh, held, sem.at[0])
    taken.start()

    def squares(values):
        return jnp.sum(jnp.sum(values * values, axis=0, keepdims=True), axis=1, keepdims=True)

    at_loss = z.at_bias + 2 * z.halves + 1
    norm = jnp.sqrt(squares(two[...]) + squares(upper[0:at_loss, :]) + squares(lower[...]))
    o_norm[...] = norm
    o_loss[...] = upper[at_loss : at_loss + 1, 0:1]
    o_count[...] = misc[0:1, 1:2]
    factor = jnp.minimum(1.0, CLIP / (norm + 1e-06))

    def renew(rows, lanes, grad, w, m, v, ow, om, ov, oc=None):
        clipped = grad * factor
        moment = 0.5 * m[rows, lanes] + 0.5 * clipped
        second = 0.5 * v[rows, lanes] + 0.5 * clipped * clipped
        old = w[rows, lanes]
        om[rows, lanes] = moment
        ov[rows, lanes] = second
        fresh_weight = old - RATE * ((moment / CORRECT) / (jnp.sqrt(second / CORRECT) + EPSILON) + DECAY * old)
        ow[rows, lanes] = fresh_weight
        if oc is not None:
            oc[rows, lanes] = fresh_weight.astype(BF16)

    taken.wait()
    moved = pltpu.make_async_copy(held, o_fresh, sem.at[1])
    moved.start()
    low = z.fin - z.shift
    for half in range(z.halves):
        lanes = slice(half * LANES, (half + 1) * LANES)
        u0, l0 = half * z.frows, half * z.brows
        one = (w1, m1, v1, o1, n1, s1)
        renew(slice(0, low), lanes, upper[u0 : u0 + low, :], *one)
        if z.shift:
            renew(slice(low, low + 8), lanes, upper[u0 + low : u0 + low + 8, :] + lower[l0 : l0 + 8, :], *one)
            renew(slice(low + 8, 2 * z.fin), lanes, lower[l0 + 8 : l0 + z.fin + z.shift, :], *one)
        else:
            renew(slice(low, 2 * z.fin), lanes, lower[l0 : l0 + z.fin, :], *one)
        start = half * 2 * z.hid
        renew(slice(0, 2 * z.hid), lanes, two[start : start + 2 * z.hid, :], w2, m2, v2, o2, n2, s2, c2)
    packed = two[z.at_three : z.at_three + z.hid, :].T
    for half in range(2):
        grad = packed[half * (LANES // 2) : half * (LANES // 2) + z.cls, :]
        renew(slice(0, z.cls), slice(half * z.hid, (half + 1) * z.hid), grad, w3, m3, v3, o3, n3, s3, c3)
    c1[...] = o1[...].astype(BF16)
    size = bs.shape[0]
    line = jnp.concatenate([upper[z.at_bias + k : z.at_bias + k + 1, :] for k in range(2 * z.halves + 1)], axis=1)
    clipped = line[:, 0:size] * factor
    flat = lambda ref: ref[...].reshape(1, size)
    moment = 0.5 * flat(mb) + 0.5 * clipped
    second = 0.5 * flat(vb) + 0.5 * clipped * clipped
    old = flat(bs)
    fresh_bias = old - RATE * ((moment / CORRECT) / (jnp.sqrt(second / CORRECT) + EPSILON) + DECAY * old)
    ob[...] = fresh_bias.reshape(size)
    nb[...] = moment.reshape(size)
    sb[...] = second.reshape(size)
    cb[...] = ob[...].astype(BF16)
    moved.wait()


def update(z, *args):
    weights = args[5:9]
    same = [jax.ShapeDtypeStruct(w.shape, F32) for w in weights]
    copies = [jax.ShapeDtypeStruct(w.shape, BF16) for w in weights]
    inside = pl.BlockSpec(memory_space=pltpu.VMEM)
    outside = pl.BlockSpec(memory_space=pl.ANY)
    scalar = jax.ShapeDtypeStruct((1, 1), F32)
    shapes = [scalar, scalar, scalar, jax.ShapeDtypeStruct(args[4].shape, F32), *same, *same, *same, *copies]
    return pl.pallas_call(
        functools.partial(update_kernel, z),
        out_shape=tuple(shapes),
        in_specs=[inside] * 4 + [outside] + [inside] * (len(args) - 5),
        out_specs=tuple([inside] * 3 + [outside] + [inside] * (len(shapes) - 4)),
        scratch_shapes=[pltpu.VMEM(args[4].shape, F32), pltpu.SemaphoreType.DMA((2,))],
        compiler_params=pltpu.CompilerParams(vmem_limit_bytes=62 * 1024 * 1024),
        name="update",
    )(*args)


def solution(mesh):
    def local(
        features, hub_features, low_lists, low_masks, high_lists, high_masks, hub_lists, hub_masks, send_rows,
        labels, train_mask, stale_rows, weight_one, weight_two, weight_three, biases,
        mean_one, mean_two, mean_three, mean_biases, square_one, square_two, square_three, square_biases,
    ):
        z = Sizes(mesh, features, low_lists, high_lists, hub_lists, send_rows, weight_one, weight_three)
        three_t = weight_three.T
        two, upper, lower, renewed, misc = train(
            z, features.T, hub_features.T, low_lists.T, low_masks.T, high_lists.T, high_masks.T,
            hub_lists[0].T, hub_masks[0].T, send_rows[0],
            labels.reshape(-1, LANES), train_mask.reshape(-1, LANES), stale_rows,
            weight_one, weight_two, three_t, biases,
        )
        norm, loss, count, renewed, o1, o2, o3, ob, n1, n2, n3, nb, s1, s2, s3, sb, c1, c2, c3, cb = update(
            z, two, upper, lower, misc, renewed, weight_one, weight_two, three_t, biases,
            mean_one, mean_two, mean_three.T, mean_biases, square_one, square_two, square_three.T, square_biases,
        )
        return (
            norm[0, 0], loss[0, 0], count[0, 0],
            o1, o2, o3.T, ob, n1, n2, n3.T, nb, s1, s2, s3.T, sb, c1, c2, c3.T, cb, renewed,
        )

    spread = ("dom", "sub")
    rows, all_same, cube = P(spread, None), P(), P(spread, None, None)
    stale = P(None, spread, None)
    in_specs = (
        rows, all_same, rows, rows, rows, rows, cube, cube, cube, P(spread), P(spread), stale, *[all_same] * 12
    )
    out_specs = (*[all_same] * 19, stale)
    return jax.shard_map(local, mesh=mesh, in_specs=in_specs, out_specs=out_specs, check_vma=False)
```

```python
import functools

import jax
import jax.numpy as jnp
from jax import lax
from jax.experimental import pallas as pl
from jax.experimental.pallas import tpu as pltpu
from jax.sharding import PartitionSpec as P

MESH = pl.DeviceIdType.MESH
F32 = jnp.float32
BF16 = jnp.bfloat16

STEP = 5
KEEP = 0.95
SMOOTH = 0.1
CLIP = 0.02
RATE = 0.03
DECAY = 0.01
EPSILON = 1e-08
CORRECT = 1.0 - 0.5**STEP
GELU_A = 0.7978845608
GELU_B = 0.044715
LANES = 128


def up(value, unit):
    return -(-value // unit) * unit


def split(values):
    high = values.astype(BF16)
    return high, (values - high.astype(F32)).astype(BF16)


def dot(left, right):
    return jnp.dot(left, right, preferred_element_type=F32)


def dot_nt(left, right):
    return lax.dot_general(left, right, (((1,), (1,)), ((), ())), preferred_element_type=F32)


def dot_tn(left, right):
    return lax.dot_general(left, right, (((0,), (0,)), ((), ())), preferred_element_type=F32)


def three(product, left, right):
    return (
        product(left[0], right[1]) + product(left[1], right[0])
    ) + product(left[0], right[0])


def gelu(v):
    return 0.5 * v * (1.0 + jnp.tanh(GELU_A * (v + GELU_B * (v * v * v))))


def gelu_slope(v):
    t = jnp.tanh(GELU_A * (v + GELU_B * (v * v * v)))
    return 0.5 * (1.0 + t) + (0.5 * GELU_A) * v * (1.0 - t * t) * (1.0 + (3.0 * GELU_B) * (v * v))


def tiles(total, step, body):
    @pl.loop(0, total // step)
    def _(index):
        body(pl.multiple_of(index * step, step))


class Sizes:
    def __init__(self, mesh, features, low_lists, high_lists, hub_lists, send_rows, weight_one, weight_three):
        self.dom, self.sub = mesh.shape["dom"], mesh.shape["sub"]
        self.devices = self.dom * self.sub
        self.nodes, self.fin = features.shape
        self.low, self.k_low = low_lists.shape
        self.high, self.k_high = high_lists.shape
        self.hubs, self.k_hub = hub_lists.shape[1:]
        self.blk = send_rows.shape[2]
        self.halo = self.devices * self.blk
        self.hid = weight_one.shape[1]
        self.halves = self.hid // LANES
        self.cls = weight_three.shape[1]
        self.rows = self.nodes + self.hubs
        self.table = self.nodes + self.halo + self.hubs
        self.fpad = up(self.fin, LANES)
        self.frows = up(self.fin, 8)
        self.shift = self.fin % 8
        self.brows = up(self.fin + self.shift, 8)
        self.part = self.hubs // self.dom
        self.count_rows = self.hubs // LANES
        self.packed = self.blk % 16 == 0
        self.cblk = self.blk // 2 if self.packed else self.blk
        unit = 8 * self.devices
        self.at_three = self.halves * 2 * self.hid
        self.at_bias = self.halves * self.frows
        self.flat = (
            up(self.at_three + self.hid, unit),
            up(self.at_bias + 8, unit),
            *[up(self.brows, unit)] * self.halves,
        )
        three, four = (2, self.dom // 2, self.sub), (2, self.dom // 2, 2, self.sub // 2)
        self.levels = (four, four, *[three] * self.halves)


class HubSum:
    def __init__(self, z, place, remote, buffers, sems, index):
        self.z, self.place, self.remote = z, place, remote
        self.source, self.ra, self.rb, self.out = buffers
        self.sent, self.got = sems
        self.index = index

    def put(self, values):
        self.source[...] = values.reshape(self.source.shape)

    def sems(self, phase):
        return self.sent.at[self.index, phase], self.got.at[self.index, phase]

    def over_dom(self, start, phase):
        d, s = self.place

        @pl.loop(1, self.z.dom)
        def _(k):
            pd = lax.rem(d + k, self.z.dom)
            src, dst = start(pd)
            self.remote(src, dst, *self.sems(phase), pd, s).start()

    def dom_done(self, ref, phase):
        d, s = self.place
        some = ref.at[pl.ds(0, self.z.dom - 1)]
        copy = self.remote(some, some, *self.sems(phase), lax.rem(d + 1, self.z.dom), s)
        copy.wait_recv()
        copy.wait_send()

    def scatter(self):
        d, s = self.place
        self.over_dom(lambda pd: (self.source.at[pd], self.ra.at[d]), 0)

    def swap(self):
        d, s = self.place
        self.dom_done(self.ra, 0)
        total = self.source[d]
        for k in range(1, self.z.dom):
            total = total + self.ra[lax.rem(d + k, self.z.dom)]
        self.rb[s] = total

        @pl.loop(1, self.z.sub)
        def _(k):
            ps = lax.rem(s + k, self.z.sub)
            self.remote(self.rb.at[s], self.rb.at[s], *self.sems(1), d, ps).start()

    def gather(self):
        d, s = self.place
        some = self.rb.at[pl.ds(0, self.z.sub - 1)]
        copy = self.remote(some, some, *self.sems(1), d, lax.rem(s + 1, self.z.sub))
        copy.wait_recv()
        copy.wait_send()
        total = self.rb[0]
        for k in range(1, self.z.sub):
            total = total + self.rb[k]
        self.out[d] = total
        self.over_dom(lambda pd: (self.out.at[d], self.out.at[d]), 2)

    def end(self):
        self.dom_done(self.out, 2)
        return self.out[:, 0 : self.z.part, :].reshape(self.z.hubs, self.out.shape[-1])


class FlatSum:
    def __init__(self, z, place, remote, buffers, sems, index):
        d, s = place
        self.remote, self.index = remote, index
        self.source, self.out = buffers[0], buffers[1]
        depth = len(z.levels[index])
        self.landed, self.parts = buffers[2 : 2 + depth], (buffers[0], *buffers[2 + depth :])
        self.sent, self.got = sems
        pair = lax.rem(d, 2)
        chip = d // 2
        self.levels = (
            (2, pair, lambda j: (chip * 2 + j, s)),
            (z.dom // 2, chip, lambda j: (j * 2 + pair, s)),
            (z.sub, s, lambda j: (d, j)),
        )
        if depth == 4:
            near, far = lax.rem(s, 2), s // 2
            self.levels = (
                *self.levels[:2],
                (2, near, lambda j: (d, far * 2 + j)),
                (z.sub // 2, far, lambda j: (d, j * 2 + near)),
            )
        self.first, offset, rows = [], 0, self.source.shape[0]
        for size, mine, _ in self.levels:
            rows = rows // size
            self.first.append((offset, rows))
            offset = offset + mine * rows

    def sems(self, phase):
        return self.sent.at[self.index, phase], self.got.at[self.index, phase]

    def rows(self, start, count):
        return pl.ds(pl.multiple_of(start, 8), count)

    def send(self, level):
        size, mine, peer = self.levels[level]
        count = self.first[level][1]

        @pl.loop(1, size)
        def _(k):
            j = lax.rem(mine + k, size)
            self.remote(
                self.parts[level].at[self.rows(j * count, count)],
                self.landed[level].at[mine],
                *self.sems(level),
                *peer(j),
            ).start()

    def receive(self, level):
        size, mine, peer = self.levels[level]
        offset, count = self.first[level]
        ref = self.landed[level]
        some = ref.at[pl.ds(0, size - 1)]
        copy = self.remote(some, some, *self.sems(level), *peer(lax.rem(mine + 1, size)))
        copy.wait_recv()
        copy.wait_send()
        total = self.parts[level][self.rows(mine * count, count), :]
        for k in range(1, size):
            total = total + ref[lax.rem(mine + k, size)]
        if level + 1 < len(self.levels):
            self.parts[level + 1][...] = total
        else:
            self.out[self.rows(offset + mine * count, count), :] = total

    def spread(self, level):
        size, mine, peer = self.levels[level]
        offset, count = self.first[level]
        held = self.out.at[self.rows(offset + mine * count, count)]

        @pl.loop(1, size)
        def _(k):
            j = lax.rem(mine + k, size)
            self.remote(held, held, *self.sems(4 + level), *peer(j)).start()

    def collect(self, level):
        size, mine, peer = self.levels[level]
        some = self.out.at[pl.ds(0, (size - 1) * self.first[level][1])]
        copy = self.remote(some, some, *self.sems(4 + level), *peer(lax.rem(mine + 1, size)))
        copy.wait_recv()
        copy.wait_send()


HUB_SUMS = (1, 1, 1, 1, 1, 2)


def train_kernel(
    z,
    feat, hubf, lowl, lowm, highl, highm, hubl, hubm, send, lab, tmask, stale_hbm, w1, w2, w3, bias,
    two_hbm, upper_hbm, lower_hbm, tail_hbm, fresh_hbm, misc,
    ab, abt, sel, selt, colb, keyt, keys, xh, xl, xth, xtl, w1h, w1l, w2h, w2l, w3t, w3h, w3l,
    tb, tc, inv, q, magg, h1h, h1l, m1h, m1l, h2h, h2l, dg0, dg1, dph, dpl, dmh, dml, eb, gown, gthree, stale,
    zst, pself, labc, trainw, brow,
    send_a, recv_a, send_b, recv_b, send_c, recv_c, send_d, recv_d, recv_e, recv_f, send_g, recv_g,
    *rest_refs,
):
    hub_refs, flat_refs = rest_refs[: 4 * len(HUB_SUMS)], rest_refs[4 * len(HUB_SUMS) : -7]
    xs, xr, hsem_s, hsem_r, gsem_s, gsem_r, lsem = rest_refs[-7:]
    send_e, send_f = send_a, send_b
    d = lax.axis_index("dom")
    s = lax.axis_index("sub")
    me = d * z.sub + s
    nd, halo, hubs, hid, fin = z.nodes, z.halo, z.hubs, z.hid, z.fin
    halo0, hub0 = nd, nd + halo
    own, halos, hubr = slice(0, nd), slice(halo0, hub0), slice(hub0, z.table)
    hubq = slice(nd, z.rows)
    up_rows, low_rows = slice(0, hid), slice(hid, 2 * hid)
    i32 = jnp.int32
    both = range(z.halves)

    def lanes(h):
        return slice(h * LANES, (h + 1) * LANES)

    barrier = pltpu.get_barrier_semaphore()

    @pl.loop(1, z.devices)
    def _(k):
        pl.semaphore_signal(
            barrier,
            inc=1,
            device_id=(lax.rem(d + k // z.sub, z.dom), lax.rem(s + k % z.sub, z.sub)),
            device_id_type=MESH,
        )

    stale_copy = pltpu.make_async_copy(stale_hbm, stale, lsem.at[0])
    stale_copy.start()

    def remote(src, dst, ssem, rsem, pd, ps):
        return pltpu.make_async_remote_copy(
            src_ref=src, dst_ref=dst, send_sem=ssem, recv_sem=rsem, device_id=(pd, ps), device_id_type=MESH
        )

    place = (d, s)
    sums = [
        HubSum(z, place, remote, hub_refs[4 * i : 4 * i + 4], (hsem_s, hsem_r), i) for i in range(len(HUB_SUMS))
    ]
    grads, start = [], 0
    for i in range(len(z.flat)):
        refs = flat_refs[start : start + 1 + 2 * len(z.levels[i])]
        grads.append(FlatSum(z, place, remote, refs, (gsem_s, gsem_r), i))
        start += len(refs)
    two, upper, *lowers = grads

    def part_of(portion):
        return 1 + (z.devices - 1) * portion // 8

    def exchange_start(src, dst, i, first=0, last=8):
        @pl.loop(part_of(first), part_of(last))
        def _(k):
            pd = lax.rem(d + k // z.sub, z.dom)
            ps = lax.rem(s + k % z.sub, z.sub)
            remote(src.at[pd * z.sub + ps], dst.at[me], xs.at[i], xr.at[i], pd, ps).start()

        if first == 0:
            dst[me] = src[me]

    def exchange_wait(src, dst, i):
        some = pl.ds(0, z.devices - 1)
        copy = remote(src.at[some], dst.at[some], xs.at[i], xr.at[i], lax.rem(d + 1, z.dom), s)
        copy.wait_recv()
        copy.wait_send()

    def put_split(ref, rows, values):
        width = values.shape[1]
        high, rest = split(values)
        ref[rows, 0:width] = high
        ref[rows, width : 2 * width] = rest

    def put_pair(high_ref, rest_ref, rows, columns, values):
        high, rest = split(values)
        high_ref[rows, columns] = high
        rest_ref[rows, columns] = rest
        return high, rest

    def added(product):
        return product[:, :LANES] + product[:, LANES:]

    per_tile = 256 // z.blk

    def turn(source, target, r_count, c_count, c_start=0, step=128):
        def body(r):
            for c in range(c_start, c_count, step):
                target[c : c + step, pl.ds(r, step)] = source[pl.ds(r, step), c : c + step].T

        tiles(r_count, step, body)

    pad0 = fin // 16 * 16
    xth[pad0 : z.fpad, :] = jnp.zeros((z.fpad - pad0, z.rows), BF16)
    xtl[pad0 : z.fpad, :] = jnp.zeros((z.fpad - pad0, z.rows), BF16)
    w1h[pad0 : z.fpad, :] = jnp.zeros((z.fpad - pad0, 2 * hid), BF16)
    w1l[pad0 : z.fpad, :] = jnp.zeros((z.fpad - pad0, 2 * hid), BF16)
    put_pair(xth, xtl, slice(0, fin), own, feat[...])
    turn(xth, xh, z.fpad, nd)
    turn(xtl, xl, z.fpad, nd)
    put_pair(w1h, w1l, slice(0, fin), low_rows, w1[fin : 2 * fin, :])

    def project(rows, columns):
        return three(dot, (xh[rows, :], xl[rows, :]), (w1h[:, columns], w1l[:, columns]))

    def put_halves(rows, values):
        for h in both:
            put_split(tb.at[h], rows, values[:, lanes(h)])

    tiles(nd, 256, lambda r: put_halves(pl.ds(r, 256), project(pl.ds(r, 256), low_rows)))

    colb[0 : z.devices, 0 : z.blk] = send[...]
    turned = colb[...].T

    for tile in range(halo // 256):
        first = tile * per_tile
        column = jnp.concatenate([turned[0 : z.blk, p : p + 1] for p in range(first, first + per_tile)], axis=0)
        hit = column == lax.broadcasted_iota(i32, (256, nd), 1)
        sel[tile * 256 : tile * 256 + 256, :] = jnp.where(hit, 1.0, 0.0).astype(BF16)

    def pick(source, target):
        def body(r):
            values = added(dot(sel[pl.ds(r, 256), :], source[own, :]))
            target[pl.ds(r // z.blk, per_tile)] = values.reshape(per_tile, z.blk, LANES)

        tiles(halo, 256, body)

    pick(tb.at[0], send_a.at[0])
    pl.semaphore_wait(barrier, z.devices - 1)
    for h in both:
        if h:
            pick(tb.at[h], send_a.at[h])
        exchange_start(send_a.at[h], recv_a.at[h], h)

    keyt[...] = jnp.full(keyt.shape, -1, i32)
    keyt[0 : z.k_low, 0 : z.low] = jnp.where(lowm[...] > 0, lowl[...], -1)
    keyt[0 : z.k_high, z.low : nd] = jnp.where(highm[...] > 0, highl[...], -1)
    keyt[0 : z.k_hub, hubq] = jnp.where(hubm[...] > 0, hubl[...], -1)
    for block in range(z.rows // LANES):
        keys[lanes(block), :] = keyt[:, lanes(block)].T
    counts = jnp.sum(jnp.where(keys[...] >= 0, 1.0, 0.0), axis=1, keepdims=True)
    inv[own, :] = 1.0 / jnp.maximum(counts[own, :], 1.0)
    train_local = jnp.sum(jnp.sum(tmask[...].astype(F32), axis=1, keepdims=True), axis=0, keepdims=True)
    used_slots = jnp.sum(jnp.where(keyt[0 : z.k_hub, hubq] >= 0, 1.0, 0.0), axis=0, keepdims=True)
    extra = [used_slots[:, lanes(c)] for c in range(z.count_rows)] + [jnp.broadcast_to(train_local, (1, LANES))]
    extra.append(jnp.zeros((8 - len(extra), LANES), F32))
    extra = jnp.concatenate(extra, axis=0)
    for block in range(z.dom):
        sums[0].source[block, z.part : z.part + 8, :] = extra

    def build(first, count, slots):
        def group(r):
            rows = pl.ds(first + r, 16)
            key = keys[rows, :].astype(jnp.int16)
            spot = lax.broadcasted_iota(i32, (16, z.table), 1).astype(jnp.int16)
            one, none = jnp.ones((16, z.table), BF16), jnp.zeros((16, z.table), BF16)
            total = none
            for k in range(slots):
                total = total + jnp.where(jnp.broadcast_to(key[:, k : k + 1], (16, z.table)) == spot, one, none)
            ab[rows, :] = total

        tiles(count, 16, group)

    build(0, z.low, z.k_low)
    build(nd, hubs, z.k_hub)
    build(z.low, z.high, z.k_high)

    put_pair(xth, xtl, slice(0, fin), hubq, hubf[...])
    turn(xth, xh, z.fpad, z.rows, nd)
    turn(xtl, xl, z.fpad, z.rows, nd)
    put_pair(w1h, w1l, slice(0, fin), up_rows, w1[0:fin, :])
    brow[...] = jnp.zeros(brow.shape, F32)
    line = bias[...].reshape(1, 2 * hid + z.cls)
    brow[0:1, :] = line[:, 0:hid]
    brow[1:2, :] = line[:, hid : 2 * hid]
    brow[2:3, 0 : z.cls] = line[:, 2 * hid : 2 * hid + z.cls]
    put_halves(hubr, project(hubq, low_rows))

    def own_tile(r):
        rows = pl.ds(r, 256)
        q[rows, :] = project(rows, up_rows) + brow[0:1, :]

    tiles(nd, 256, own_tile)

    def gather_local(h):
        def body(r):
            rows = pl.ds(r, 256)
            magg[rows, lanes(h)] = added(dot(ab[rows, own], tb[h, own, :]) + dot(ab[rows, hubr], tb[h, hubr, :]))

        tiles(z.rows, 256, body)

    gather_local(0)

    def with_halo(rows, h):
        return magg[rows, lanes(h)] + added(dot(ab[rows, halos], tb[h, halos, :]))

    def layer_one(h):
        def body(r):
            rows = pl.ds(r, 256)
            pre = q[rows, lanes(h)] + with_halo(rows, h) * inv[rows, :]
            q[rows, lanes(h)] = pre
            high, rest = put_pair(h1h, h1l, rows, lanes(h), gelu(pre))
            tb[h, rows, 0:LANES] = high
            tb[h, rows, LANES : 2 * LANES] = rest

        tiles(nd, 256, body)

    exchange_wait(send_a.at[0], recv_a.at[0], 0)
    put_split(tb.at[0], halos, recv_a[0].reshape(halo, LANES))
    sums[0].source[:, 0 : z.part, :] = with_halo(hubq, 0).reshape(z.dom, z.part, LANES)
    sums[0].scatter()
    layer_one(0)
    pick(tb.at[0], send_b.at[0])
    exchange_start(send_b.at[0], recv_b.at[0], 2, 0, 4)
    gather_local(1)
    own_tile(nd)
    turn(sel, selt, halo, nd)
    exchange_wait(send_a.at[1], recv_a.at[1], 1)
    put_split(tb.at[1], halos, recv_a[1].reshape(halo, LANES))
    sums[1].put(with_halo(hubq, 1))
    sums[1].scatter()
    exchange_start(send_b.at[0], recv_b.at[0], 2, 4, 8)
    layer_one(1)
    pick(tb.at[1], send_b.at[1])
    sums[0].swap()
    sums[1].swap()
    exchange_start(send_b.at[1], recv_b.at[1], 3, 0, 4)
    put_pair(w2h, w2l, slice(0, 2 * hid), slice(0, hid), w2[...])
    w3t[...] = jnp.zeros(w3t.shape, F32)
    w3t[0 : z.cls, :] = w3[...]
    put_pair(w3h, w3l, slice(0, 2 * hid), slice(0, LANES), w3t[...].T)
    turn(ab, abt, z.rows, z.table)
    sums[0].gather()
    sums[1].gather()
    exchange_start(send_b.at[1], recv_b.at[1], 3, 4, 8)
    for grad in grads:
        grad.source[...] = jnp.zeros(grad.source.shape, F32)

    stale_copy.wait()
    zst[...] = three(dot, split(KEEP * stale[1]), (w3h[low_rows, :], w3l[low_rows, :]))
    dg0[own, :] = gelu_slope(q[own, :])
    for block in range(nd // LANES):
        diag = lax.broadcasted_iota(i32, (LANES, LANES), 0) == lax.broadcasted_iota(i32, (LANES, LANES), 1)
        line = jnp.broadcast_to(lab[block : block + 1, :], (LANES, LANES))
        labc[lanes(block), :] = jnp.sum(jnp.where(diag, line, 0), axis=1, keepdims=True)
        line = jnp.broadcast_to(tmask[block : block + 1, :].astype(F32), (LANES, LANES))
        trainw[lanes(block), :] = jnp.sum(jnp.where(diag, line, 0.0), axis=1, keepdims=True)
    first_hub = sums[0].end()
    misc[...] = sums[0].out[0, z.part : z.part + 8, :]
    colb[0:8, :] = misc[...].astype(i32)
    turned_counts = colb[...].T
    for c in range(z.count_rows):
        inv[nd + c * LANES : nd + (c + 1) * LANES, :] = 1.0 / turned_counts[:, c : c + 1].astype(F32)
    hub_ends = (first_hub, sums[1].end())
    for h in both:
        pre = q[hubq, lanes(h)] + hub_ends[h] * inv[hubq, :]
        dg0[hubq, lanes(h)] = gelu_slope(pre)
        high, rest = put_pair(h1h, h1l, hubq, lanes(h), gelu(pre))
        tb[h, hubr, 0:LANES] = high
        tb[h, hubr, LANES : 2 * LANES] = rest

    for h in both:
        gather_local(h)

    def own_two(r):
        rows = pl.ds(r, 256)
        q[rows, :] = three(dot, (h1h[rows, :], h1l[rows, :]), (w2h[up_rows, :], w2l[up_rows, :])) + brow[1:2, :]

    tiles(z.rows, 256, own_two)

    def second(h):
        exchange_wait(send_b.at[h], recv_b.at[h], 2 + h)
        renewed = KEEP * stale[0, :, lanes(h)] + (1.0 - KEEP) * recv_b[h].reshape(halo, LANES)
        stale[0, :, lanes(h)] = renewed
        put_split(tb.at[h], halos, renewed)
        sums[2 + h].put(with_halo(hubq, h))
        sums[2 + h].scatter()

        def body(r):
            rows = pl.ds(r, 256)
            put_pair(m1h, m1l, rows, lanes(h), with_halo(rows, h) * inv[rows, :])

        tiles(nd, 256, body)

    second(0)
    second(1)
    sums[2].swap()

    def layer_two(r):
        rows = pl.ds(r, 256)
        pre = q[rows, :] + three(dot, (m1h[rows, :], m1l[rows, :]), (w2h[low_rows, :], w2l[low_rows, :]))
        q[rows, :] = pre
        high, rest = put_pair(h2h, h2l, rows, slice(0, hid), gelu(pre))
        put_split(tc, rows, three(dot, (high, rest), (w3h[low_rows, :], w3l[low_rows, :])))

    tiles(nd, 256, layer_two)
    class_lane = lax.broadcasted_iota(i32, (1, 1, LANES), 2) < LANES // 2

    def pack(values):
        blocks = values.reshape(values.shape[0] // z.blk, z.blk, LANES)
        if z.packed:
            return blocks[:, : z.cblk] + pltpu.roll(blocks[:, z.cblk :], LANES // 2, 2)
        return blocks

    def unpack(blocks):
        if z.packed:
            first = jnp.where(class_lane, blocks, 0.0)
            second = jnp.where(class_lane, pltpu.roll(blocks, LANES // 2, 2), 0.0)
            blocks = jnp.concatenate([first, second], axis=1)
        return blocks.reshape(halo, LANES)

    def pick_class(r):
        send_c[pl.ds(r // z.blk, per_tile)] = pack(added(dot(sel[pl.ds(r, 256), :], tc[own, :])))

    tiles(halo, 256, pick_class)
    sums[3].swap()
    sums[2].gather()
    exchange_start(send_c, recv_c, 4)

    def pick_wide(r):
        chosen = sel[pl.ds(r, 256), :]
        values = dot(chosen, h2l[own, :]) + dot(chosen, h2h[own, :])
        send_g[pl.ds(r // z.blk, per_tile)] = values.reshape(per_tile, z.blk, hid)


    def own_three(r):
        rows = pl.ds(r, 256)
        pself[rows, :] = three(dot, (h2h[rows, :], h2l[rows, :]), (w3h[up_rows, :], w3l[up_rows, :])) + brow[2:3, 0:LANES]

    tiles(nd, 256, own_three)

    def class_local(r):
        rows = pl.ds(r, 256)
        magg[rows, 0:LANES] = added(dot(ab[rows, own], tc[own, :]))

    tiles(nd, 256, class_local)
    sums[3].gather()
    tiles(halo, 256, pick_wide)
    exchange_start(send_g, recv_g, 5, 0, 2)
    dg1[own, :] = gelu_slope(q[own, :])
    for h in both:
        put_pair(m1h, m1l, hubq, lanes(h), sums[2 + h].end() * inv[hubq, :])
    pre = q[hubq, :] + three(dot, (m1h[hubq, :], m1l[hubq, :]), (w2h[low_rows, :], w2l[low_rows, :]))
    high, rest = put_pair(h2h, h2l, hubq, slice(0, hid), gelu(pre))
    put_split(tc, hubr, three(dot, (high, rest), (w3h[low_rows, :], w3l[low_rows, :])))
    q[hubq, :] = pre

    exchange_wait(send_c, recv_c, 4)
    exchange_start(send_g, recv_g, 5, 2, 3)
    put_split(tc, halos, zst[...] + (1.0 - KEEP) * unpack(recv_c[...]))
    used = lax.broadcasted_iota(i32, (256, LANES), 1)
    train_total = misc[z.count_rows : z.count_rows + 1, 0:1]
    at_bias = z.at_bias

    def head(r):
        rows = pl.ds(r, 256)
        logits = pself[rows, :] + (magg[rows, 0:LANES] + added(dot(ab[rows, halo0:], tc[halo0:, :]))) * inv[rows, :]
        valid = used < z.cls
        top = jnp.max(jnp.where(valid, logits, -1e30), axis=1, keepdims=True)
        shifted = logits - top
        powers = jnp.where(valid, jnp.exp(jnp.where(valid, shifted, 0.0)), 0.0)
        total = jnp.sum(powers, axis=1, keepdims=True)
        log_probs = jnp.where(valid, shifted - jnp.log(total), 0.0)
        target = jnp.where(used == labc[rows, :], 1.0 - SMOOTH, 0.0) + SMOOTH / z.cls
        weight = trainw[rows, :]
        losses = jnp.sum(jnp.where(valid, -target * log_probs, 0.0), axis=1, keepdims=True) * weight
        grad = jnp.where(valid, powers / total - target, 0.0) * weight / train_total
        at = at_bias + 2 * z.halves
        upper.source[at : at + 1, :] = upper.source[at : at + 1, :] + jnp.sum(grad, axis=0, keepdims=True)
        at = at + 1
        upper.source[at : at + 1, :] = upper.source[at : at + 1, :] + jnp.sum(losses, axis=0, keepdims=True)
        put_pair(dph, dpl, rows, slice(0, LANES), grad)
        put_split(eb.at[0], rows, grad * inv[rows, :])

    tiles(nd, 256, head)

    sums[4].put(added(dot(abt[hubr, own], eb[0, own, :])))
    sums[4].scatter()

    def back_class(r):
        values = added(dot(abt[pl.ds(halo0 + r, 256), own], eb[0, own, :]))
        put_split(tc, pl.ds(halo0 + r, 256), values)
        send_d[pl.ds(r // z.blk, per_tile)] = pack((1.0 - KEEP) * values)

    tiles(halo, 256, back_class)
    sums[4].swap()
    exchange_start(send_d, recv_d, 6)
    gown[own, 0:LANES] = added(dot(abt[own, own], eb[0, own, :]))

    gthree[:, 0:LANES] = three(dot_tn, split(KEEP * stale[1]), (tc[halos, 0:LANES], tc[halos, LANES : 2 * LANES]))
    sums[4].gather()
    exchange_start(send_g, recv_g, 5, 3, 5)
    hub_class = split(sums[4].source[...].reshape(hubs, LANES))
    gthree[:, 0:LANES] = gthree[:, 0:LANES] + three(dot_tn, (h2h[hubq, :], h2l[hubq, :]), hub_class)
    gthree[:, LANES : 2 * LANES] = three(dot_tn, (h2h[own, :], h2l[own, :]), (dph[own, 0:LANES], dpl[own, 0:LANES]))
    dg1[hubq, :] = gelu_slope(q[hubq, :])

    def self_two(r):
        rows = pl.ds(r, 256)
        magg[rows, :] = three(
            dot_nt, (dph[rows, 0:LANES], dpl[rows, 0:LANES]), (w3h[up_rows, :], w3l[up_rows, :])
        )

    tiles(nd, 256, self_two)

    def owned(values):
        row = lax.broadcasted_iota(i32, (hubs, 1), 0)
        share = hubs // z.devices
        mine = jnp.where(row >= me * share, 1.0, 0.0) * jnp.where(row < (me + 1) * share, 1.0, 0.0)
        return values * mine

    def column_sums(columns):
        return jnp.sum(dmh[:, columns].astype(F32) + dml[:, columns].astype(F32), axis=0, keepdims=True)

    node = three(dot_nt, split(sums[4].end()), (w3h[low_rows, :], w3l[low_rows, :])) * dg1[hubq, :]
    put_pair(dph, dpl, hubq, slice(0, hid), node)
    put_pair(dmh, dml, hubq, slice(0, hid), owned(node))

    def spread(rows):
        values = three(dot_nt, (dph[rows, :], dpl[rows, :]), (w2h[low_rows, :], w2l[low_rows, :])) * inv[rows, :]
        for h in both:
            put_split(eb.at[h], rows, values[:, lanes(h)])

    spread(hubq)
    exchange_wait(send_d, recv_d, 6)
    exchange_start(send_g, recv_g, 5, 5, 6)
    put_split(tc, halos, unpack(recv_d[...]))

    def back_two(r):
        rows = pl.ds(r, 256)
        own_class = gown[rows, 0:LANES] + added(dot(selt[rows, :], tc[halos, :]))
        gown[rows, 0:LANES] = own_class
        node = (
            three(dot_nt, split(own_class), (w3h[low_rows, :], w3l[low_rows, :])) + magg[rows, :]
        ) * dg1[rows, :]
        high, rest = put_pair(dph, dpl, rows, slice(0, hid), node)
        dmh[rows, :] = high
        dml[rows, :] = rest
        spread(rows)

    tiles(nd, 256, back_two)

    for h in both:
        sums[5].source[:, :, lanes(h)] = added(dot(abt[hubr, :], eb[h])).reshape(z.dom, z.part, LANES)
    sums[5].scatter()

    def send_halo(target, factor, h):
        def body(r):
            values = added(dot(abt[pl.ds(halo0 + r, 256), :], eb[h])) * factor
            target[pl.ds(r // z.blk, per_tile)] = values.reshape(per_tile, z.blk, LANES)

        tiles(halo, 256, body)

    send_halo(send_e.at[0], 1.0 - KEEP, 0)
    exchange_start(send_e.at[0], recv_e.at[0], 7, 0, 4)
    send_halo(send_e.at[1], 1.0 - KEEP, 1)
    sums[5].swap()
    exchange_start(send_e.at[0], recv_e.at[0], 7, 4, 8)

    def own_back(r):
        rows = pl.ds(r, 256)
        q[rows, :] = three(dot_nt, (dph[rows, :], dpl[rows, :]), (w2h[up_rows, :], w2l[up_rows, :]))

    tiles(z.rows, 256, own_back)

    def own_table(r):
        rows = pl.ds(r, 256)
        for h in both:
            q[rows, lanes(h)] = q[rows, lanes(h)] + added(dot(abt[rows, :], eb[h]))

    tiles(nd, 256, own_table)
    gthree[:, 0:LANES] = gthree[:, 0:LANES] + three(dot_tn, (h2h[own, :], h2l[own, :]), split(gown[own, 0:LANES]))
    two.source[z.at_three : z.at_three + hid, :] = gthree[:, LANES : 2 * LANES] + pltpu.roll(
        gthree[:, 0:LANES], LANES // 2, 1
    )
    for h in both:
        start = h * 2 * hid
        pair = (dmh[:, lanes(h)], dml[:, lanes(h)])
        two.source[start : start + hid, :] = three(dot_tn, (h1h[...], h1l[...]), pair)
        two.source[start + hid : start + 2 * hid, :] = three(dot_tn, (m1h[...], m1l[...]), pair)
        at = at_bias + z.halves + h
        upper.source[at : at + 1, :] = column_sums(lanes(h))
    sums[5].gather()
    two.send(0)
    exchange_start(send_e.at[1], recv_e.at[1], 8, 0, 4)
    node = (sums[5].end() + q[hubq, :]) * dg0[hubq, :]
    put_pair(dmh, dml, hubq, slice(0, hid), owned(node))
    node = node * inv[hubq, :]
    for h in both:
        put_split(eb.at[h], hubq, node[:, lanes(h)])
    two.receive(0)
    two.send(1)
    exchange_start(send_e.at[1], recv_e.at[1], 8, 4, 8)

    def back_one(h):
        exchange_wait(send_e.at[h], recv_e.at[h], 7 + h)
        put_split(tb.at[h], halos, recv_e[h].reshape(halo, LANES))

        def body(r):
            rows = pl.ds(r, 256)
            node = (q[rows, lanes(h)] + added(dot(selt[rows, :], tb[h, halos, :]))) * dg0[rows, lanes(h)]
            put_pair(dmh, dml, rows, lanes(h), node)
            put_split(eb.at[h], rows, node * inv[rows, :])

        tiles(nd, 256, body)
        send_halo(send_f.at[h], 1.0, h)

    back_one(0)
    exchange_start(send_f.at[0], recv_f.at[0], 9, 0, 4)
    two.receive(1)
    two.send(2)
    exchange_start(send_f.at[0], recv_f.at[0], 9, 4, 8)
    back_one(1)
    two.receive(2)
    two.send(3)
    for h in both:
        top = three(dot, (xth[...], xtl[...]), (dmh[:, lanes(h)], dml[:, lanes(h)]))
        upper.source[h * z.frows : (h + 1) * z.frows, :] = top[0 : z.frows, :]
        upper.source[at_bias + h : at_bias + h + 1, :] = column_sums(lanes(h))
    upper.send(0)
    two.receive(3)
    two.spread(3)
    exchange_start(send_f.at[1], recv_f.at[1], 10, 0, 4)

    def own_last(r):
        rows = pl.ds(r, 256)
        for h in both:
            gown[rows, lanes(h)] = added(dot(abt[rows, :], eb[h]))

    tiles(nd, 256, own_last)
    for h in both:
        put_pair(dmh, dml, hubq, lanes(h), added(dot(abt[hubr, :], eb[h])))
    upper.receive(0)
    upper.send(1)
    two.collect(3)
    two.spread(2)

    def last(h):
        exchange_wait(send_f.at[h], recv_f.at[h], 9 + h)
        put_split(tb.at[h], halos, recv_f[h].reshape(halo, LANES))

        def body(r):
            rows = pl.ds(r, 256)
            put_pair(dmh, dml, rows, lanes(h), gown[rows, lanes(h)] + added(dot(selt[rows, :], tb[h, halos, :])))

        tiles(nd, 256, body)
        bottom = three(dot, (xth[...], xtl[...]), (dmh[:, lanes(h)], dml[:, lanes(h)]))
        lowers[h].source[z.shift : z.shift + fin, :] = bottom[0:fin, :]

    last(0)
    low_first, low_second = lowers
    low_first.send(0)
    exchange_start(send_f.at[1], recv_f.at[1], 10, 4, 8)
    upper.receive(1)
    upper.send(2)
    two.collect(2)
    two.spread(1)
    low_first.receive(0)
    low_first.send(1)
    last(1)
    low_second.send(0)
    upper.receive(2)
    upper.send(3)
    two.collect(1)
    two.spread(0)
    low_first.receive(1)
    low_first.send(2)
    exchange_start(send_g, recv_g, 5, 6, 7)
    upper.receive(3)
    upper.spread(3)
    low_second.receive(0)
    low_second.send(1)
    two.collect(0)
    two_copy = pltpu.make_async_copy(two.out, two_hbm, lsem.at[1])
    two_copy.start()
    upper.collect(3)
    upper.spread(2)
    low_first.receive(2)
    low_first.spread(2)
    exchange_start(send_g, recv_g, 5, 7, 8)
    low_second.receive(1)
    low_second.send(2)
    low_first.collect(2)
    low_first.spread(1)
    upper.collect(2)
    upper.spread(1)
    low_second.receive(2)
    low_second.spread(2)
    exchange_wait(send_g, recv_g, 5)
    stale[1] = KEEP * stale[1] + (1.0 - KEEP) * recv_g[...].reshape(halo, hid)
    fresh_copy = pltpu.make_async_copy(stale, fresh_hbm, lsem.at[2])
    fresh_copy.start()
    low_first.collect(1)
    low_first.spread(0)
    low_second.collect(2)
    low_second.spread(1)
    upper.collect(1)
    upper.spread(0)
    low_first.collect(0)
    lower_copy = pltpu.make_async_copy(low_first.out, lower_hbm, lsem.at[4])
    lower_copy.start()
    upper.collect(0)
    upper_copy = pltpu.make_async_copy(upper.out, upper_hbm, lsem.at[3])
    upper_copy.start()
    low_second.collect(1)
    low_second.spread(0)
    low_second.collect(0)
    tail_copy = pltpu.make_async_copy(low_second.out, tail_hbm, lsem.at[5])
    tail_copy.start()
    two_copy.wait()
    fresh_copy.wait()
    upper_copy.wait()
    lower_copy.wait()
    tail_copy.wait()


def train(z, *args):
    b, f, i = BF16, F32, jnp.int32
    vmem = pltpu.VMEM
    n, rows, tab, hid, halo = z.nodes, z.rows, z.table, z.hid, z.halo
    wide = (z.halves, z.devices, z.blk, LANES)
    bulk = (z.devices, z.blk, hid)
    thin = (z.devices, z.cblk, LANES)

    def hub_buffers(count, more):
        width = count * LANES
        return [vmem((size, z.part + more, width), f) for size in (z.dom, z.dom, z.sub, z.dom)]

    def flat_buffers(total, levels):
        landed, parts, rest = [], [], total
        for size in levels:
            rest = rest // size
            landed.append(vmem((size, rest, LANES), f))
            parts.append(vmem((rest, LANES), f))
        return [vmem((total, LANES), f), vmem((total, LANES), f), *landed, *parts[:-1]]

    def pairs(count, *shape):
        return [vmem(shape, b) for _ in range(2 * count)]

    scratch = [
        vmem((rows, tab), b), vmem((tab, rows), b), vmem((halo, n), b), vmem((n, halo), b), vmem((LANES, LANES), i),
        vmem((LANES, rows), i), vmem((rows, LANES), i),
        *pairs(1, rows, z.fpad), *pairs(1, z.fpad, rows), *pairs(1, z.fpad, 2 * hid), *pairs(1, 2 * hid, hid),
        vmem((LANES, 2 * hid), f), *pairs(1, 2 * hid, LANES),
        vmem((z.halves, tab, 2 * LANES), b), vmem((tab, 2 * LANES), b), vmem((rows, 1), f), vmem((rows, hid), f),
        vmem((rows, hid), f),
        *pairs(3, rows, hid),
        vmem((rows, hid), f), vmem((rows, hid), f),
        *pairs(2, rows, hid),
        vmem((z.halves, rows, 2 * LANES), b), vmem((n, hid), f), vmem((hid, 2 * LANES), f),
        vmem((2, halo, hid), f),
        vmem((halo, LANES), f), vmem((n, LANES), f), vmem((n, 1), i), vmem((n, 1), f), vmem((8, hid), f),
        *[vmem(shape, f) for shape in (wide, wide, wide, wide, thin, thin, thin, thin, wide, wide, bulk, bulk)],
    ]
    for index, count in enumerate(HUB_SUMS):
        scratch += hub_buffers(count, 0 if index else 8)
    for total, levels in zip(z.flat, z.levels):
        scratch += flat_buffers(total, levels)
    dma = pltpu.SemaphoreType.DMA
    scratch += [
        dma((11,)), dma((11,)), dma((len(HUB_SUMS), 3)), dma((len(HUB_SUMS), 3)), dma((len(z.flat), 8)), dma((len(z.flat), 8)), dma((4 + z.halves,))
    ]
    inside = pl.BlockSpec(memory_space=pltpu.VMEM)
    outside = pl.BlockSpec(memory_space=pl.ANY)
    return pl.pallas_call(
        functools.partial(train_kernel, z),
        out_shape=(
            *[jax.ShapeDtypeStruct((total, LANES), f) for total in z.flat],
            jax.ShapeDtypeStruct((2, halo, hid), f),
            jax.ShapeDtypeStruct((8, LANES), f),
        ),
        in_specs=[inside] * 11 + [outside] + [inside] * 4,
        out_specs=(outside, outside, outside, outside, outside, inside),
        scratch_shapes=scratch,
        compiler_params=pltpu.CompilerParams(
            collective_id=0, has_side_effects=True, vmem_limit_bytes=62 * 1024 * 1024
        ),
        name="train",
    )(*args)


def update_kernel(
    z,
    two_hbm, upper_hbm, low_a_hbm, low_b_hbm, fresh_hbm, w1_hbm, m1_hbm, v1_hbm, w2_hbm, m2_hbm, v2_hbm,
    misc, w3, m3, v3, bs, mb, vb,
    o1, n1, s1, c1, o2, n2, s2, c2, o_fresh,
    o_norm, o_loss, o_count, o3, n3, s3, c3, ob, nb, sb, cb,
    two, upper, low_a, low_b, held, w1, m1, v1, w2, m2, v2, d1, d2, in_sem, out_sem,
):
    inward = [
        pltpu.make_async_copy(src, dst, in_sem.at[i])
        for i, (src, dst) in enumerate(
            (
                (two_hbm, two), (upper_hbm, upper), (low_a_hbm, low_a), (low_b_hbm, low_b),
                (w1_hbm, w1), (m1_hbm, m1), (v1_hbm, v1), (w2_hbm, w2), (m2_hbm, m2), (v2_hbm, v2), (fresh_hbm, held),
            )
        )
    ]
    for copy in inward:
        copy.start()
    outward = []

    def leave(src, dst, rows=None):
        if rows is not None:
            src, dst = src.at[rows], dst.at[rows]
        outward.append(pltpu.make_async_copy(src, dst, out_sem.at[len(outward)]))
        outward[-1].start()

    def squares(values):
        return jnp.sum(jnp.sum(values * values, axis=0, keepdims=True), axis=1, keepdims=True)

    at_loss = z.at_bias + 2 * z.halves + 1
    for copy in inward[:4]:
        copy.wait()
    norm = jnp.sqrt(
        squares(two[...]) + squares(upper[0:at_loss, :]) + squares(low_a[...]) + squares(low_b[...])
    )
    o_norm[...] = norm
    o_loss[...] = upper[at_loss : at_loss + 1, 0:1]
    o_count[...] = misc[z.count_rows : z.count_rows + 1, 0:1]
    factor = jnp.minimum(1.0, CLIP / (norm + 1e-06))

    def step(grad, old, first, second):
        clipped = grad * factor
        moment = 0.5 * first + 0.5 * clipped
        squared = 0.5 * second + 0.5 * clipped * clipped
        fresh = old - RATE * ((moment / CORRECT) / (jnp.sqrt(squared / CORRECT) + EPSILON) + DECAY * old)
        return fresh, moment, squared

    def renew(rows, lanes, grad, w, m, v):
        w[rows, lanes], m[rows, lanes], v[rows, lanes] = step(grad, w[rows, lanes], m[rows, lanes], v[rows, lanes])

    def lane_half(half):
        return slice(half * LANES, (half + 1) * LANES)

    low = z.fin - z.shift
    lows = (low_a, low_b)
    for copy in inward[4:7]:
        copy.wait()
    for half in range(z.halves):
        u0 = half * z.frows
        renew(slice(0, low), lane_half(half), upper[u0 : u0 + low, :], w1, m1, v1)
    for src, dst in ((w1, o1), (m1, n1), (v1, s1)):
        leave(src, dst, pl.ds(0, low))
    for half in range(z.halves):
        u0, lower, lanes = half * z.frows, lows[half], lane_half(half)
        if z.shift:
            renew(slice(low, low + 8), lanes, upper[u0 + low : u0 + low + 8, :] + lower[0:8, :], w1, m1, v1)
            renew(slice(low + 8, 2 * z.fin), lanes, lower[8 : z.fin + z.shift, :], w1, m1, v1)
        else:
            renew(slice(low, 2 * z.fin), lanes, lower[0 : z.fin, :], w1, m1, v1)
    for src, dst in ((w1, o1), (m1, n1), (v1, s1)):
        leave(src, dst, pl.ds(low, 2 * z.fin - low))
    d1[...] = w1[...].astype(BF16)
    leave(d1, c1)
    for copy in inward[7:10]:
        copy.wait()
    for half in range(z.halves):
        start = half * 2 * z.hid
        renew(slice(0, 2 * z.hid), lane_half(half), two[start : start + 2 * z.hid, :], w2, m2, v2)
    for src, dst in ((w2, o2), (m2, n2), (v2, s2)):
        leave(src, dst)
    d2[...] = w2[...].astype(BF16)
    leave(d2, c2)
    inward[10].wait()
    leave(held, o_fresh)
    packed = two[z.at_three : z.at_three + z.hid, :].T
    for half in range(2):
        grad = packed[half * (LANES // 2) : half * (LANES // 2) + z.cls, :]
        part = slice(half * z.hid, (half + 1) * z.hid)
        fresh, moment, squared = step(grad, w3[:, part], m3[:, part], v3[:, part])
        o3[:, part] = fresh
        n3[:, part] = moment
        s3[:, part] = squared
        c3[:, part] = fresh.astype(BF16)
    size = bs.shape[0]
    line = jnp.concatenate([upper[z.at_bias + k : z.at_bias + k + 1, :] for k in range(2 * z.halves + 1)], axis=1)
    flat = lambda ref: ref[...].reshape(1, size)
    fresh, moment, squared = step(line[:, 0:size], flat(bs), flat(mb), flat(vb))
    ob[...] = fresh.reshape(size)
    nb[...] = moment.reshape(size)
    sb[...] = squared.reshape(size)
    cb[...] = ob[...].astype(BF16)
    for copy in outward:
        copy.wait()


def update(z, *args):
    inside = pl.BlockSpec(memory_space=pltpu.VMEM)
    outside = pl.BlockSpec(memory_space=pl.ANY)
    shape = jax.ShapeDtypeStruct
    one, two, three_t, line = args[5].shape, args[8].shape, args[12].shape, args[15].shape

    def group(size):
        return [shape(size, F32)] * 3 + [shape(size, BF16)]

    shapes = [
        *group(one), *group(two), shape(args[4].shape, F32), *[shape((1, 1), F32)] * 3, *group(three_t), *group(line)
    ]
    return pl.pallas_call(
        functools.partial(update_kernel, z),
        out_shape=tuple(shapes),
        in_specs=[outside] * 11 + [inside] * 7,
        out_specs=tuple([outside] * 9 + [inside] * 11),
        scratch_shapes=[
            *[pltpu.VMEM(a.shape, F32) for a in args[:11]],
            pltpu.VMEM(one, BF16), pltpu.VMEM(two, BF16),
            pltpu.SemaphoreType.DMA((11,)), pltpu.SemaphoreType.DMA((12,)),
        ],
        compiler_params=pltpu.CompilerParams(vmem_limit_bytes=62 * 1024 * 1024),
        name="update",
    )(*args)


def solution(mesh):
    def local(
        features, hub_features, low_lists, low_masks, high_lists, high_masks, hub_lists, hub_masks, send_rows,
        labels, train_mask, stale_rows, weight_one, weight_two, weight_three, biases,
        mean_one, mean_two, mean_three, mean_biases, square_one, square_two, square_three, square_biases,
    ):
        z = Sizes(mesh, features, low_lists, high_lists, hub_lists, send_rows, weight_one, weight_three)
        three_t = weight_three.T
        two, upper, low_first, low_second, renewed, misc = train(
            z, features.T, hub_features.T, low_lists.T, low_masks.T, high_lists.T, high_masks.T,
            hub_lists[0].T, hub_masks[0].T, send_rows[0],
            labels.reshape(-1, LANES), train_mask.reshape(-1, LANES), stale_rows,
            weight_one, weight_two, three_t, biases,
        )
        o1, n1, s1, c1, o2, n2, s2, c2, renewed, norm, loss, count, o3, n3, s3, c3, ob, nb, sb, cb = update(
            z, two, upper, low_first, low_second, renewed, weight_one, mean_one, square_one,
            weight_two, mean_two, square_two, misc, three_t, mean_three.T, square_three.T,
            biases, mean_biases, square_biases,
        )
        return (
            norm[0, 0], loss[0, 0], count[0, 0],
            o1, o2, o3.T, ob, n1, n2, n3.T, nb, s1, s2, s3.T, sb, c1, c2, c3.T, cb, renewed,
        )

    spread = ("dom", "sub")
    rows, all_same, cube = P(spread, None), P(), P(spread, None, None)
    stale = P(None, spread, None)
    in_specs = (
        rows, all_same, rows, rows, rows, rows, cube, cube, cube, P(spread), P(spread), stale, *[all_same] * 12
    )
    out_specs = (*[all_same] * 19, stale)
    return jax.shard_map(local, mesh=mesh, in_specs=in_specs, out_specs=out_specs, check_vma=False)
```

```python
import functools

import jax
import jax.numpy as jnp
from jax import lax
from jax.experimental import pallas as pl
from jax.experimental.pallas import tpu as pltpu
from jax.sharding import PartitionSpec as P

MESH = pl.DeviceIdType.MESH
F32 = jnp.float32
BF16 = jnp.bfloat16

STEP = 5
KEEP = 0.95
SMOOTH = 0.1
CLIP = 0.02
RATE = 0.03
DECAY = 0.01
EPSILON = 1e-08
CORRECT = 1.0 - 0.5**STEP
GELU_A = 0.7978845608
GELU_B = 0.044715
LANES = 128


def up(value, unit):
    return -(-value // unit) * unit


def split(values):
    high = values.astype(BF16)
    return high, (values - high.astype(F32)).astype(BF16)


def dot(left, right):
    return jnp.dot(left, right, preferred_element_type=F32)


def dot_nt(left, right):
    return lax.dot_general(left, right, (((1,), (1,)), ((), ())), preferred_element_type=F32)


def dot_tn(left, right):
    return lax.dot_general(left, right, (((0,), (0,)), ((), ())), preferred_element_type=F32)


def three(product, left, right):
    return (
        product(left[0], right[1]) + product(left[1], right[0])
    ) + product(left[0], right[0])


def gelu(v):
    return 0.5 * v * (1.0 + jnp.tanh(GELU_A * (v + GELU_B * (v * v * v))))


def gelu_slope(v):
    t = jnp.tanh(GELU_A * (v + GELU_B * (v * v * v)))
    return 0.5 * (1.0 + t) + (0.5 * GELU_A) * v * (1.0 - t * t) * (1.0 + (3.0 * GELU_B) * (v * v))


def tiles(total, step, body):
    @pl.loop(0, total // step)
    def _(index):
        body(pl.multiple_of(index * step, step))


class Sizes:
    def __init__(self, mesh, features, low_lists, high_lists, hub_lists, send_rows, weight_one, weight_three):
        self.dom, self.sub = mesh.shape["dom"], mesh.shape["sub"]
        self.devices = self.dom * self.sub
        self.nodes, self.fin = features.shape
        self.low, self.k_low = low_lists.shape
        self.high, self.k_high = high_lists.shape
        self.hubs, self.k_hub = hub_lists.shape[1:]
        self.blk = send_rows.shape[2]
        self.halo = self.devices * self.blk
        self.hid = weight_one.shape[1]
        self.halves = self.hid // LANES
        self.cls = weight_three.shape[1]
        self.rows = self.nodes + self.hubs
        self.table = self.nodes + self.halo + self.hubs
        self.fpad = up(self.fin, LANES)
        self.frows = up(self.fin, 8)
        self.shift = self.fin % 8
        self.brows = up(self.fin + self.shift, 8)
        self.part = self.hubs // self.dom
        self.count_rows = self.hubs // LANES
        self.paired = self.part % 16 == 0
        self.class_part = self.part // 2 if self.paired else self.part
        self.packed = self.blk % 16 == 0
        self.cblk = self.blk // 2 if self.packed else self.blk
        unit = 8 * self.devices
        self.at_three = self.halves * 2 * self.hid
        self.at_bias = self.halves * self.frows
        self.flat = (
            up(self.at_three + self.hid, unit),
            up(self.at_bias + 8, unit),
            *[up(self.brows, unit)] * self.halves,
        )
        three, four = (2, self.dom // 2, self.sub), (2, self.dom // 2, 2, self.sub // 2)
        self.levels = (four, four, *[three] * self.halves)


class HubSum:
    def __init__(self, z, place, remote, buffers, sems, index):
        self.z, self.place, self.remote = z, place, remote
        self.source, self.ra, self.rb, self.out = buffers
        self.sent, self.got = sems
        self.index = index

    def put(self, values):
        self.source[...] = values.reshape(self.source.shape)

    def sems(self, phase):
        return self.sent.at[self.index, phase], self.got.at[self.index, phase]

    def over_dom(self, start, phase):
        d, s = self.place

        @pl.loop(1, self.z.dom)
        def _(k):
            pd = lax.rem(d + k, self.z.dom)
            src, dst = start(pd)
            self.remote(src, dst, *self.sems(phase), pd, s).start()

    def dom_done(self, ref, phase):
        d, s = self.place
        some = ref.at[pl.ds(0, self.z.dom - 1)]
        copy = self.remote(some, some, *self.sems(phase), lax.rem(d + 1, self.z.dom), s)
        copy.wait_recv()
        copy.wait_send()

    def scatter(self):
        d, s = self.place
        self.over_dom(lambda pd: (self.source.at[pd], self.ra.at[d]), 0)

    def swap(self):
        d, s = self.place
        self.dom_done(self.ra, 0)
        total = self.source[d]
        for k in range(1, self.z.dom):
            total = total + self.ra[lax.rem(d + k, self.z.dom)]
        self.rb[s] = total

        @pl.loop(1, self.z.sub)
        def _(k):
            ps = lax.rem(s + k, self.z.sub)
            self.remote(self.rb.at[s], self.rb.at[s], *self.sems(1), d, ps).start()

    def gather(self):
        d, s = self.place
        some = self.rb.at[pl.ds(0, self.z.sub - 1)]
        copy = self.remote(some, some, *self.sems(1), d, lax.rem(s + 1, self.z.sub))
        copy.wait_recv()
        copy.wait_send()
        total = self.rb[0]
        for k in range(1, self.z.sub):
            total = total + self.rb[k]
        self.out[d] = total
        self.over_dom(lambda pd: (self.out.at[d], self.out.at[d]), 2)

    def finish(self):
        self.dom_done(self.out, 2)

    def end(self):
        self.finish()
        return self.out[:, 0 : self.z.part, :].reshape(self.z.hubs, self.out.shape[-1])


class FlatSum:
    def __init__(self, z, place, remote, buffers, sems, index):
        d, s = place
        self.remote, self.index = remote, index
        self.source, self.out = buffers[0], buffers[1]
        depth = len(z.levels[index])
        self.landed, self.parts = buffers[2 : 2 + depth], (buffers[0], *buffers[2 + depth :])
        self.sent, self.got = sems
        pair = lax.rem(d, 2)
        chip = d // 2
        self.levels = (
            (2, pair, lambda j: (chip * 2 + j, s)),
            (z.dom // 2, chip, lambda j: (j * 2 + pair, s)),
            (z.sub, s, lambda j: (d, j)),
        )
        if depth == 4:
            near, far = lax.rem(s, 2), s // 2
            self.levels = (
                *self.levels[:2],
                (2, near, lambda j: (d, far * 2 + j)),
                (z.sub // 2, far, lambda j: (d, j * 2 + near)),
            )
        self.first, offset, rows = [], 0, self.source.shape[0]
        for size, mine, _ in self.levels:
            rows = rows // size
            self.first.append((offset, rows))
            offset = offset + mine * rows

    def sems(self, phase):
        return self.sent.at[self.index, phase], self.got.at[self.index, phase]

    def rows(self, start, count):
        return pl.ds(pl.multiple_of(start, 8), count)

    def send(self, level):
        size, mine, peer = self.levels[level]
        count = self.first[level][1]

        @pl.loop(1, size)
        def _(k):
            j = lax.rem(mine + k, size)
            self.remote(
                self.parts[level].at[self.rows(j * count, count)],
                self.landed[level].at[mine],
                *self.sems(level),
                *peer(j),
            ).start()

    def receive(self, level):
        size, mine, peer = self.levels[level]
        offset, count = self.first[level]
        ref = self.landed[level]
        some = ref.at[pl.ds(0, size - 1)]
        copy = self.remote(some, some, *self.sems(level), *peer(lax.rem(mine + 1, size)))
        copy.wait_recv()
        copy.wait_send()
        total = self.parts[level][self.rows(mine * count, count), :]
        for k in range(1, size):
            total = total + ref[lax.rem(mine + k, size)]
        if level + 1 < len(self.levels):
            self.parts[level + 1][...] = total
        else:
            self.out[self.rows(offset + mine * count, count), :] = total

    def spread(self, level):
        size, mine, peer = self.levels[level]
        offset, count = self.first[level]
        held = self.out.at[self.rows(offset + mine * count, count)]

        @pl.loop(1, size)
        def _(k):
            j = lax.rem(mine + k, size)
            self.remote(held, held, *self.sems(4 + level), *peer(j)).start()

    def collect(self, level):
        size, mine, peer = self.levels[level]
        some = self.out.at[pl.ds(0, (size - 1) * self.first[level][1])]
        copy = self.remote(some, some, *self.sems(4 + level), *peer(lax.rem(mine + 1, size)))
        copy.wait_recv()
        copy.wait_send()


HUB_SUMS = (1, 1, 1, 1, 1, 2)


def train_kernel(
    z,
    feat, hubf, lowl, lowm, highl, highm, hubl, hubm, send, lab, tmask, stale_hbm, w1, w2, w3, bias,
    two_hbm, upper_hbm, lower_hbm, tail_hbm, fresh_hbm, misc,
    ab, abt, sel, selt, colb, keyt, keys, xh, xl, xth, xtl, w1h, w1l, w2h, w2l, w3t, w3h, w3l,
    tb, tc, inv, q, magg, h1h, h1l, m1h, m1l, h2h, h2l, dg0, dg1, dph, dpl, dmh, dml, eb, gown, gthree, stale,
    zst, pself, labc, trainw, brow,
    send_a, recv_a, send_b, recv_b, send_c, recv_c, send_d, recv_d, recv_e, recv_f, send_g, recv_g,
    *rest_refs,
):
    hub_refs, flat_refs = rest_refs[: 4 * len(HUB_SUMS)], rest_refs[4 * len(HUB_SUMS) : -7]
    xs, xr, hsem_s, hsem_r, gsem_s, gsem_r, lsem = rest_refs[-7:]
    send_e, send_f = send_a, send_b
    d = lax.axis_index("dom")
    s = lax.axis_index("sub")
    me = d * z.sub + s
    nd, halo, hubs, hid, fin = z.nodes, z.halo, z.hubs, z.hid, z.fin
    halo0, hub0 = nd, nd + halo
    own, halos, hubr = slice(0, nd), slice(halo0, hub0), slice(hub0, z.table)
    hubq = slice(nd, z.rows)
    up_rows, low_rows = slice(0, hid), slice(hid, 2 * hid)
    i32 = jnp.int32
    both = range(z.halves)

    def lanes(h):
        return slice(h * LANES, (h + 1) * LANES)

    barrier = pltpu.get_barrier_semaphore()

    @pl.loop(1, z.devices)
    def _(k):
        pl.semaphore_signal(
            barrier,
            inc=1,
            device_id=(lax.rem(d + k // z.sub, z.dom), lax.rem(s + k % z.sub, z.sub)),
            device_id_type=MESH,
        )

    stale_copy = pltpu.make_async_copy(stale_hbm, stale, lsem.at[0])
    stale_copy.start()

    def remote(src, dst, ssem, rsem, pd, ps):
        return pltpu.make_async_remote_copy(
            src_ref=src, dst_ref=dst, send_sem=ssem, recv_sem=rsem, device_id=(pd, ps), device_id_type=MESH
        )

    place = (d, s)
    sums = [
        HubSum(z, place, remote, hub_refs[4 * i : 4 * i + 4], (hsem_s, hsem_r), i) for i in range(len(HUB_SUMS))
    ]
    grads, start = [], 0
    for i in range(len(z.flat)):
        refs = flat_refs[start : start + 1 + 2 * len(z.levels[i])]
        grads.append(FlatSum(z, place, remote, refs, (gsem_s, gsem_r), i))
        start += len(refs)
    two, upper, *lowers = grads

    def part_of(portion):
        return 1 + (z.devices - 1) * portion // 8

    def exchange_start(src, dst, i, first=0, last=8):
        @pl.loop(part_of(first), part_of(last))
        def _(k):
            mixed = lax.rem(k * 5, z.devices)
            pd = lax.rem(d + mixed // z.sub, z.dom)
            ps = lax.rem(s + mixed % z.sub, z.sub)
            remote(src.at[pd * z.sub + ps], dst.at[me], xs.at[i], xr.at[i], pd, ps).start()

        if first == 0:
            dst[me] = src[me]

    def exchange_wait(src, dst, i):
        some = pl.ds(0, z.devices - 1)
        copy = remote(src.at[some], dst.at[some], xs.at[i], xr.at[i], lax.rem(d + 1, z.dom), s)
        copy.wait_recv()
        copy.wait_send()

    def put_split(ref, rows, values):
        width = values.shape[1]
        high, rest = split(values)
        ref[rows, 0:width] = high
        ref[rows, width : 2 * width] = rest

    def put_pair(high_ref, rest_ref, rows, columns, values):
        high, rest = split(values)
        high_ref[rows, columns] = high
        rest_ref[rows, columns] = rest
        return high, rest

    def added(product):
        return product[:, :LANES] + product[:, LANES:]

    per_tile = 256 // z.blk

    def turn(source, target, r_count, c_count, c_start=0, step=128):
        def body(r):
            for c in range(c_start, c_count, step):
                target[c : c + step, pl.ds(r, step)] = source[pl.ds(r, step), c : c + step].T

        tiles(r_count, step, body)

    pad0 = fin // 16 * 16
    xth[pad0 : z.fpad, :] = jnp.zeros((z.fpad - pad0, z.rows), BF16)
    xtl[pad0 : z.fpad, :] = jnp.zeros((z.fpad - pad0, z.rows), BF16)
    w1h[pad0 : z.fpad, :] = jnp.zeros((z.fpad - pad0, 2 * hid), BF16)
    w1l[pad0 : z.fpad, :] = jnp.zeros((z.fpad - pad0, 2 * hid), BF16)
    put_pair(xth, xtl, slice(0, fin), own, feat[...])
    turn(xth, xh, z.fpad, nd)
    turn(xtl, xl, z.fpad, nd)
    put_pair(w1h, w1l, slice(0, fin), low_rows, w1[fin : 2 * fin, :])

    def project(rows, columns):
        return three(dot, (xh[rows, :], xl[rows, :]), (w1h[:, columns], w1l[:, columns]))

    def put_halves(rows, values):
        for h in both:
            put_split(tb.at[h], rows, values[:, lanes(h)])

    tiles(nd, 256, lambda r: put_halves(pl.ds(r, 256), project(pl.ds(r, 256), low_rows)))

    colb[0 : z.devices, 0 : z.blk] = send[...]
    turned = colb[...].T

    for tile in range(halo // 256):
        first = tile * per_tile
        column = jnp.concatenate([turned[0 : z.blk, p : p + 1] for p in range(first, first + per_tile)], axis=0)
        hit = column == lax.broadcasted_iota(i32, (256, nd), 1)
        sel[tile * 256 : tile * 256 + 256, :] = jnp.where(hit, 1.0, 0.0).astype(BF16)

    def pick(source, target):
        def body(r):
            values = added(dot(sel[pl.ds(r, 256), :], source[own, :]))
            target[pl.ds(r // z.blk, per_tile)] = values.reshape(per_tile, z.blk, LANES)

        tiles(halo, 256, body)

    pick(tb.at[0], send_a.at[0])
    pl.semaphore_wait(barrier, z.devices - 1)
    for h in both:
        if h:
            pick(tb.at[h], send_a.at[h])
        exchange_start(send_a.at[h], recv_a.at[h], h)

    keyt[...] = jnp.full(keyt.shape, -1, i32)
    keyt[0 : z.k_low, 0 : z.low] = jnp.where(lowm[...] > 0, lowl[...], -1)
    keyt[0 : z.k_high, z.low : nd] = jnp.where(highm[...] > 0, highl[...], -1)
    keyt[0 : z.k_hub, hubq] = jnp.where(hubm[...] > 0, hubl[...], -1)
    for block in range(z.rows // LANES):
        keys[lanes(block), :] = keyt[:, lanes(block)].T
    counts = jnp.sum(jnp.where(keys[...] >= 0, 1.0, 0.0), axis=1, keepdims=True)
    inv[own, :] = 1.0 / jnp.maximum(counts[own, :], 1.0)
    train_local = jnp.sum(jnp.sum(tmask[...].astype(F32), axis=1, keepdims=True), axis=0, keepdims=True)
    used_slots = jnp.sum(jnp.where(keyt[0 : z.k_hub, hubq] >= 0, 1.0, 0.0), axis=0, keepdims=True)
    extra = [used_slots[:, lanes(c)] for c in range(z.count_rows)] + [jnp.broadcast_to(train_local, (1, LANES))]
    extra.append(jnp.zeros((8 - len(extra), LANES), F32))
    extra = jnp.concatenate(extra, axis=0)
    for block in range(z.dom):
        sums[0].source[block, z.part : z.part + 8, :] = extra

    def build(first, count, slots):
        def group(r):
            rows = pl.ds(first + r, 16)
            key = keys[rows, :].astype(jnp.int16)
            spot = lax.broadcasted_iota(i32, (16, z.table), 1).astype(jnp.int16)
            one, none = jnp.ones((16, z.table), BF16), jnp.zeros((16, z.table), BF16)
            total = none
            for k in range(slots):
                total = total + jnp.where(jnp.broadcast_to(key[:, k : k + 1], (16, z.table)) == spot, one, none)
            ab[rows, :] = total

        tiles(count, 16, group)

    build(0, z.low, z.k_low)
    build(nd, hubs, z.k_hub)
    build(z.low, z.high, z.k_high)

    put_pair(xth, xtl, slice(0, fin), hubq, hubf[...])
    turn(xth, xh, z.fpad, z.rows, nd)
    turn(xtl, xl, z.fpad, z.rows, nd)
    put_pair(w1h, w1l, slice(0, fin), up_rows, w1[0:fin, :])
    brow[...] = jnp.zeros(brow.shape, F32)
    line = bias[...].reshape(1, 2 * hid + z.cls)
    brow[0:1, :] = line[:, 0:hid]
    brow[1:2, :] = line[:, hid : 2 * hid]
    brow[2:3, 0 : z.cls] = line[:, 2 * hid : 2 * hid + z.cls]
    put_halves(hubr, project(hubq, low_rows))

    def own_tile(r):
        rows = pl.ds(r, 256)
        q[rows, :] = project(rows, up_rows) + brow[0:1, :]

    tiles(nd, 256, own_tile)

    def gather_local(h):
        def body(r):
            rows = pl.ds(r, 256)
            magg[rows, lanes(h)] = added(dot(ab[rows, own], tb[h, own, :]) + dot(ab[rows, hubr], tb[h, hubr, :]))

        tiles(z.rows, 256, body)

    gather_local(0)

    def with_halo(rows, h):
        return magg[rows, lanes(h)] + added(dot(ab[rows, halos], tb[h, halos, :]))

    def layer_one(h):
        def body(r):
            rows = pl.ds(r, 256)
            pre = q[rows, lanes(h)] + with_halo(rows, h) * inv[rows, :]
            q[rows, lanes(h)] = pre
            high, rest = put_pair(h1h, h1l, rows, lanes(h), gelu(pre))
            tb[h, rows, 0:LANES] = high
            tb[h, rows, LANES : 2 * LANES] = rest

        tiles(nd, 256, body)

    exchange_wait(send_a.at[0], recv_a.at[0], 0)
    put_split(tb.at[0], halos, recv_a[0].reshape(halo, LANES))
    sums[0].source[:, 0 : z.part, :] = with_halo(hubq, 0).reshape(z.dom, z.part, LANES)
    sums[0].scatter()
    layer_one(0)
    pick(tb.at[0], send_b.at[0])
    exchange_start(send_b.at[0], recv_b.at[0], 2, 0, 4)
    gather_local(1)
    own_tile(nd)
    turn(sel, selt, halo, nd)
    exchange_wait(send_a.at[1], recv_a.at[1], 1)
    put_split(tb.at[1], halos, recv_a[1].reshape(halo, LANES))
    sums[1].put(with_halo(hubq, 1))
    sums[1].scatter()
    exchange_start(send_b.at[0], recv_b.at[0], 2, 4, 8)
    layer_one(1)
    pick(tb.at[1], send_b.at[1])
    sums[0].swap()
    sums[1].swap()
    exchange_start(send_b.at[1], recv_b.at[1], 3, 0, 4)
    put_pair(w2h, w2l, slice(0, 2 * hid), slice(0, hid), w2[...])
    w3t[...] = jnp.zeros(w3t.shape, F32)
    w3t[0 : z.cls, :] = w3[...]
    put_pair(w3h, w3l, slice(0, 2 * hid), slice(0, LANES), w3t[...].T)
    turn(ab, abt, z.rows, z.table)
    sums[0].gather()
    sums[1].gather()
    exchange_start(send_b.at[1], recv_b.at[1], 3, 4, 8)
    for grad in grads:
        grad.source[...] = jnp.zeros(grad.source.shape, F32)

    stale_copy.wait()
    zst[...] = three(dot, split(KEEP * stale[1]), (w3h[low_rows, :], w3l[low_rows, :]))
    dg0[own, :] = gelu_slope(q[own, :])
    for block in range(nd // LANES):
        diag = lax.broadcasted_iota(i32, (LANES, LANES), 0) == lax.broadcasted_iota(i32, (LANES, LANES), 1)
        line = jnp.broadcast_to(lab[block : block + 1, :], (LANES, LANES))
        labc[lanes(block), :] = jnp.sum(jnp.where(diag, line, 0), axis=1, keepdims=True)
        line = jnp.broadcast_to(tmask[block : block + 1, :].astype(F32), (LANES, LANES))
        trainw[lanes(block), :] = jnp.sum(jnp.where(diag, line, 0.0), axis=1, keepdims=True)
    first_hub = sums[0].end()
    misc[...] = sums[0].out[0, z.part : z.part + 8, :]
    colb[0:8, :] = misc[...].astype(i32)
    turned_counts = colb[...].T
    for c in range(z.count_rows):
        inv[nd + c * LANES : nd + (c + 1) * LANES, :] = 1.0 / turned_counts[:, c : c + 1].astype(F32)
    hub_ends = (first_hub, sums[1].end())
    for h in both:
        pre = q[hubq, lanes(h)] + hub_ends[h] * inv[hubq, :]
        dg0[hubq, lanes(h)] = gelu_slope(pre)
        high, rest = put_pair(h1h, h1l, hubq, lanes(h), gelu(pre))
        tb[h, hubr, 0:LANES] = high
        tb[h, hubr, LANES : 2 * LANES] = rest

    for h in both:
        gather_local(h)

    def own_two(r):
        rows = pl.ds(r, 256)
        q[rows, :] = three(dot, (h1h[rows, :], h1l[rows, :]), (w2h[up_rows, :], w2l[up_rows, :])) + brow[1:2, :]

    tiles(z.rows, 256, own_two)

    def second(h):
        exchange_wait(send_b.at[h], recv_b.at[h], 2 + h)
        renewed = KEEP * stale[0, :, lanes(h)] + (1.0 - KEEP) * recv_b[h].reshape(halo, LANES)
        stale[0, :, lanes(h)] = renewed
        put_split(tb.at[h], halos, renewed)
        sums[2 + h].put(with_halo(hubq, h))
        sums[2 + h].scatter()

        def body(r):
            rows = pl.ds(r, 256)
            put_pair(m1h, m1l, rows, lanes(h), with_halo(rows, h) * inv[rows, :])

        tiles(nd, 256, body)

    second(0)
    second(1)
    sums[2].swap()

    def layer_two(r):
        rows = pl.ds(r, 256)
        pre = q[rows, :] + three(dot, (m1h[rows, :], m1l[rows, :]), (w2h[low_rows, :], w2l[low_rows, :]))
        q[rows, :] = pre
        high, rest = put_pair(h2h, h2l, rows, slice(0, hid), gelu(pre))
        put_split(tc, rows, three(dot, (high, rest), (w3h[low_rows, :], w3l[low_rows, :])))

    tiles(nd, 256, layer_two)
    class_lane = lax.broadcasted_iota(i32, (1, 1, LANES), 2) < LANES // 2

    def pack(values):
        blocks = values.reshape(values.shape[0] // z.blk, z.blk, LANES)
        if z.packed:
            return blocks[:, : z.cblk] + pltpu.roll(blocks[:, z.cblk :], LANES // 2, 2)
        return blocks

    def unpack(blocks):
        if z.packed:
            first = jnp.where(class_lane, blocks, 0.0)
            second = jnp.where(class_lane, pltpu.roll(blocks, LANES // 2, 2), 0.0)
            blocks = jnp.concatenate([first, second], axis=1)
        return blocks.reshape(halo, LANES)

    def pick_class(r):
        send_c[pl.ds(r // z.blk, per_tile)] = pack(added(dot(sel[pl.ds(r, 256), :], tc[own, :])))

    tiles(halo, 256, pick_class)
    sums[3].swap()
    sums[2].gather()
    exchange_start(send_c, recv_c, 4)

    def pick_wide(r):
        chosen = sel[pl.ds(r, 256), :]
        values = dot(chosen, h2l[own, :]) + dot(chosen, h2h[own, :])
        send_g[pl.ds(r // z.blk, per_tile)] = values.reshape(per_tile, z.blk, hid)


    def own_three(r):
        rows = pl.ds(r, 256)
        pself[rows, :] = three(dot, (h2h[rows, :], h2l[rows, :]), (w3h[up_rows, :], w3l[up_rows, :])) + brow[2:3, 0:LANES]

    tiles(nd, 256, own_three)

    def class_local(r):
        rows = pl.ds(r, 256)
        magg[rows, 0:LANES] = added(dot(ab[rows, own], tc[own, :]))

    tiles(nd, 256, class_local)
    sums[3].gather()
    tiles(halo, 256, pick_wide)
    exchange_start(send_g, recv_g, 5, 0, 3)
    dg1[own, :] = gelu_slope(q[own, :])
    for h in both:
        put_pair(m1h, m1l, hubq, lanes(h), sums[2 + h].end() * inv[hubq, :])
    pre = q[hubq, :] + three(dot, (m1h[hubq, :], m1l[hubq, :]), (w2h[low_rows, :], w2l[low_rows, :]))
    high, rest = put_pair(h2h, h2l, hubq, slice(0, hid), gelu(pre))
    put_split(tc, hubr, three(dot, (high, rest), (w3h[low_rows, :], w3l[low_rows, :])))
    q[hubq, :] = pre

    exchange_wait(send_c, recv_c, 4)
    put_split(tc, halos, zst[...] + (1.0 - KEEP) * unpack(recv_c[...]))
    used = lax.broadcasted_iota(i32, (256, LANES), 1)
    train_total = misc[z.count_rows : z.count_rows + 1, 0:1]
    at_bias = z.at_bias

    def head(r):
        rows = pl.ds(r, 256)
        logits = pself[rows, :] + (magg[rows, 0:LANES] + added(dot(ab[rows, halo0:], tc[halo0:, :]))) * inv[rows, :]
        valid = used < z.cls
        top = jnp.max(jnp.where(valid, logits, -1e30), axis=1, keepdims=True)
        shifted = logits - top
        powers = jnp.where(valid, jnp.exp(jnp.where(valid, shifted, 0.0)), 0.0)
        total = jnp.sum(powers, axis=1, keepdims=True)
        log_probs = jnp.where(valid, shifted - jnp.log(total), 0.0)
        target = jnp.where(used == labc[rows, :], 1.0 - SMOOTH, 0.0) + SMOOTH / z.cls
        weight = trainw[rows, :]
        losses = jnp.sum(jnp.where(valid, -target * log_probs, 0.0), axis=1, keepdims=True) * weight
        grad = jnp.where(valid, powers / total - target, 0.0) * weight / train_total
        at = at_bias + 2 * z.halves
        upper.source[at : at + 1, :] = upper.source[at : at + 1, :] + jnp.sum(grad, axis=0, keepdims=True)
        at = at + 1
        upper.source[at : at + 1, :] = upper.source[at : at + 1, :] + jnp.sum(losses, axis=0, keepdims=True)
        put_pair(dph, dpl, rows, slice(0, LANES), grad)
        put_split(eb.at[0], rows, grad * inv[rows, :])

    tiles(nd, 256, head)


    def pack_hubs(values):
        blocks = values.reshape(z.dom, z.part, LANES)
        if z.paired:
            return blocks[:, : z.class_part] + pltpu.roll(blocks[:, z.class_part :], LANES // 2, 2)
        return blocks

    def unpack_hubs(blocks):
        if z.paired:
            first = jnp.where(class_lane, blocks, 0.0)
            second = jnp.where(class_lane, pltpu.roll(blocks, LANES // 2, 2), 0.0)
            blocks = jnp.concatenate([first, second], axis=1)
        return blocks.reshape(hubs, LANES)

    sums[4].put(pack_hubs(added(dot(abt[hubr, own], eb[0, own, :]))))
    sums[4].scatter()

    def back_class(r):
        values = added(dot(abt[pl.ds(halo0 + r, 256), own], eb[0, own, :]))
        put_split(tc, pl.ds(halo0 + r, 256), values)
        send_d[pl.ds(r // z.blk, per_tile)] = pack((1.0 - KEEP) * values)

    tiles(halo, 256, back_class)
    sums[4].swap()
    exchange_start(send_d, recv_d, 6)
    gown[own, 0:LANES] = added(dot(abt[own, own], eb[0, own, :]))

    gthree[:, 0:LANES] = three(dot_tn, split(KEEP * stale[1]), (tc[halos, 0:LANES], tc[halos, LANES : 2 * LANES]))
    sums[4].gather()
    exchange_start(send_g, recv_g, 5, 3, 6)
    hub_class = split(unpack_hubs(sums[4].source[...]))
    gthree[:, 0:LANES] = gthree[:, 0:LANES] + three(dot_tn, (h2h[hubq, :], h2l[hubq, :]), hub_class)
    gthree[:, LANES : 2 * LANES] = three(dot_tn, (h2h[own, :], h2l[own, :]), (dph[own, 0:LANES], dpl[own, 0:LANES]))
    dg1[hubq, :] = gelu_slope(q[hubq, :])

    def self_two(r):
        rows = pl.ds(r, 256)
        magg[rows, :] = three(
            dot_nt, (dph[rows, 0:LANES], dpl[rows, 0:LANES]), (w3h[up_rows, :], w3l[up_rows, :])
        )

    tiles(nd, 256, self_two)

    def owned(values):
        row = lax.broadcasted_iota(i32, (hubs, 1), 0)
        share = hubs // z.devices
        mine = jnp.where(row >= me * share, 1.0, 0.0) * jnp.where(row < (me + 1) * share, 1.0, 0.0)
        return values * mine

    def column_sums(columns):
        return jnp.sum(dmh[:, columns].astype(F32) + dml[:, columns].astype(F32), axis=0, keepdims=True)

    sums[4].finish()
    node = three(dot_nt, split(unpack_hubs(sums[4].out[...])), (w3h[low_rows, :], w3l[low_rows, :])) * dg1[hubq, :]
    put_pair(dph, dpl, hubq, slice(0, hid), node)
    put_pair(dmh, dml, hubq, slice(0, hid), owned(node))

    def spread(rows):
        values = three(dot_nt, (dph[rows, :], dpl[rows, :]), (w2h[low_rows, :], w2l[low_rows, :])) * inv[rows, :]
        for h in both:
            put_split(eb.at[h], rows, values[:, lanes(h)])

    spread(hubq)
    exchange_wait(send_d, recv_d, 6)
    put_split(tc, halos, unpack(recv_d[...]))

    def back_two(r):
        rows = pl.ds(r, 256)
        own_class = gown[rows, 0:LANES] + added(dot(selt[rows, :], tc[halos, :]))
        gown[rows, 0:LANES] = own_class
        node = (
            three(dot_nt, split(own_class), (w3h[low_rows, :], w3l[low_rows, :])) + magg[rows, :]
        ) * dg1[rows, :]
        high, rest = put_pair(dph, dpl, rows, slice(0, hid), node)
        dmh[rows, :] = high
        dml[rows, :] = rest
        spread(rows)

    tiles(nd, 256, back_two)

    for h in both:
        sums[5].source[:, :, lanes(h)] = added(dot(abt[hubr, :], eb[h])).reshape(z.dom, z.part, LANES)
    sums[5].scatter()

    def send_halo(target, factor, h):
        def body(r):
            values = added(dot(abt[pl.ds(halo0 + r, 256), :], eb[h])) * factor
            target[pl.ds(r // z.blk, per_tile)] = values.reshape(per_tile, z.blk, LANES)

        tiles(halo, 256, body)

    send_halo(send_e.at[0], 1.0 - KEEP, 0)
    exchange_start(send_e.at[0], recv_e.at[0], 7, 0, 4)
    send_halo(send_e.at[1], 1.0 - KEEP, 1)
    sums[5].swap()
    exchange_start(send_e.at[0], recv_e.at[0], 7, 4, 8)

    def own_back(r):
        rows = pl.ds(r, 256)
        q[rows, :] = three(dot_nt, (dph[rows, :], dpl[rows, :]), (w2h[up_rows, :], w2l[up_rows, :]))

    tiles(z.rows, 256, own_back)

    def own_table(r):
        rows = pl.ds(r, 256)
        for h in both:
            q[rows, lanes(h)] = q[rows, lanes(h)] + added(dot(abt[rows, :], eb[h]))

    tiles(nd, 256, own_table)
    gthree[:, 0:LANES] = gthree[:, 0:LANES] + three(dot_tn, (h2h[own, :], h2l[own, :]), split(gown[own, 0:LANES]))
    two.source[z.at_three : z.at_three + hid, :] = gthree[:, LANES : 2 * LANES] + pltpu.roll(
        gthree[:, 0:LANES], LANES // 2, 1
    )
    for h in both:
        start = h * 2 * hid
        pair = (dmh[:, lanes(h)], dml[:, lanes(h)])
        two.source[start : start + hid, :] = three(dot_tn, (h1h[...], h1l[...]), pair)
        two.source[start + hid : start + 2 * hid, :] = three(dot_tn, (m1h[...], m1l[...]), pair)
        at = at_bias + z.halves + h
        upper.source[at : at + 1, :] = column_sums(lanes(h))
    sums[5].gather()
    exchange_start(send_e.at[1], recv_e.at[1], 8, 0, 4)
    node = (sums[5].end() + q[hubq, :]) * dg0[hubq, :]
    put_pair(dmh, dml, hubq, slice(0, hid), owned(node))
    node = node * inv[hubq, :]
    for h in both:
        put_split(eb.at[h], hubq, node[:, lanes(h)])
    two.send(0)
    exchange_start(send_e.at[1], recv_e.at[1], 8, 4, 8)

    def back_one(h):
        exchange_wait(send_e.at[h], recv_e.at[h], 7 + h)
        put_split(tb.at[h], halos, recv_e[h].reshape(halo, LANES))

        def body(r):
            rows = pl.ds(r, 256)
            node = (q[rows, lanes(h)] + added(dot(selt[rows, :], tb[h, halos, :]))) * dg0[rows, lanes(h)]
            put_pair(dmh, dml, rows, lanes(h), node)
            put_split(eb.at[h], rows, node * inv[rows, :])

        tiles(nd, 256, body)
        send_halo(send_f.at[h], 1.0, h)

    back_one(0)
    exchange_start(send_f.at[0], recv_f.at[0], 9, 0, 4)
    two.receive(0)
    two.send(1)
    exchange_start(send_f.at[0], recv_f.at[0], 9, 4, 8)
    back_one(1)
    two.receive(1)
    two.send(2)
    for h in both:
        top = three(dot, (xth[...], xtl[...]), (dmh[:, lanes(h)], dml[:, lanes(h)]))
        upper.source[h * z.frows : (h + 1) * z.frows, :] = top[0 : z.frows, :]
        upper.source[at_bias + h : at_bias + h + 1, :] = column_sums(lanes(h))
    upper.send(0)
    two.receive(2)
    two.send(3)
    exchange_start(send_f.at[1], recv_f.at[1], 10, 0, 4)

    def own_last(r):
        rows = pl.ds(r, 256)
        for h in both:
            gown[rows, lanes(h)] = added(dot(abt[rows, :], eb[h]))

    tiles(nd, 256, own_last)
    for h in both:
        put_pair(dmh, dml, hubq, lanes(h), added(dot(abt[hubr, :], eb[h])))
    upper.receive(0)
    upper.send(1)
    two.receive(3)
    two.spread(3)

    def last(h):
        exchange_wait(send_f.at[h], recv_f.at[h], 9 + h)
        put_split(tb.at[h], halos, recv_f[h].reshape(halo, LANES))

        def body(r):
            rows = pl.ds(r, 256)
            put_pair(dmh, dml, rows, lanes(h), gown[rows, lanes(h)] + added(dot(selt[rows, :], tb[h, halos, :])))

        tiles(nd, 256, body)
        bottom = three(dot, (xth[...], xtl[...]), (dmh[:, lanes(h)], dml[:, lanes(h)]))
        lowers[h].source[z.shift : z.shift + fin, :] = bottom[0:fin, :]

    last(0)
    low_first, low_second = lowers
    low_first.send(0)
    exchange_start(send_f.at[1], recv_f.at[1], 10, 4, 8)
    exchange_start(send_g, recv_g, 5, 6, 8)
    upper.receive(1)
    upper.send(2)
    two.collect(3)
    two.spread(2)
    low_first.receive(0)
    low_first.send(1)
    last(1)
    low_second.send(0)
    upper.receive(2)
    upper.send(3)
    two.collect(2)
    two.spread(1)
    low_first.receive(1)
    low_first.send(2)
    upper.receive(3)
    upper.spread(3)
    low_second.receive(0)
    low_second.send(1)
    two.collect(1)
    two.spread(0)
    two_copy = pltpu.make_async_copy(two.out, two_hbm, lsem.at[1])
    upper.collect(3)
    upper.spread(2)
    low_first.receive(2)
    low_first.spread(2)
    low_second.receive(1)
    low_second.send(2)
    low_first.collect(2)
    low_first.spread(1)
    upper.collect(2)
    upper.spread(1)
    low_second.receive(2)
    low_second.spread(2)
    exchange_wait(send_g, recv_g, 5)
    stale[1] = KEEP * stale[1] + (1.0 - KEEP) * recv_g[...].reshape(halo, hid)
    fresh_copy = pltpu.make_async_copy(stale, fresh_hbm, lsem.at[2])
    fresh_copy.start()
    low_first.collect(1)
    low_first.spread(0)
    low_second.collect(2)
    low_second.spread(1)
    upper.collect(1)
    upper.spread(0)
    two.collect(0)
    two_copy.start()
    low_first.collect(0)
    lower_copy = pltpu.make_async_copy(low_first.out, lower_hbm, lsem.at[4])
    lower_copy.start()
    upper.collect(0)
    upper_copy = pltpu.make_async_copy(upper.out, upper_hbm, lsem.at[3])
    upper_copy.start()
    low_second.collect(1)
    low_second.spread(0)
    low_second.collect(0)
    tail_copy = pltpu.make_async_copy(low_second.out, tail_hbm, lsem.at[5])
    tail_copy.start()
    two_copy.wait()
    fresh_copy.wait()
    upper_copy.wait()
    lower_copy.wait()
    tail_copy.wait()


def train(z, *args):
    b, f, i = BF16, F32, jnp.int32
    vmem = pltpu.VMEM
    n, rows, tab, hid, halo = z.nodes, z.rows, z.table, z.hid, z.halo
    wide = (z.halves, z.devices, z.blk, LANES)
    bulk = (z.devices, z.blk, hid)
    thin = (z.devices, z.cblk, LANES)

    def hub_buffers(count, more):
        width = count * LANES
        return [vmem((size, z.part + more, width), f) for size in (z.dom, z.dom, z.sub, z.dom)]

    def flat_buffers(total, levels):
        landed, parts, rest = [], [], total
        for size in levels:
            rest = rest // size
            landed.append(vmem((size, rest, LANES), f))
            parts.append(vmem((rest, LANES), f))
        return [vmem((total, LANES), f), vmem((total, LANES), f), *landed, *parts[:-1]]

    def pairs(count, *shape):
        return [vmem(shape, b) for _ in range(2 * count)]

    scratch = [
        vmem((rows, tab), b), vmem((tab, rows), b), vmem((halo, n), b), vmem((n, halo), b), vmem((LANES, LANES), i),
        vmem((LANES, rows), i), vmem((rows, LANES), i),
        *pairs(1, rows, z.fpad), *pairs(1, z.fpad, rows), *pairs(1, z.fpad, 2 * hid), *pairs(1, 2 * hid, hid),
        vmem((LANES, 2 * hid), f), *pairs(1, 2 * hid, LANES),
        vmem((z.halves, tab, 2 * LANES), b), vmem((tab, 2 * LANES), b), vmem((rows, 1), f), vmem((rows, hid), f),
        vmem((rows, hid), f),
        *pairs(3, rows, hid),
        vmem((rows, hid), f), vmem((rows, hid), f),
        *pairs(2, rows, hid),
        vmem((z.halves, rows, 2 * LANES), b), vmem((n, hid), f), vmem((hid, 2 * LANES), f),
        vmem((2, halo, hid), f),
        vmem((halo, LANES), f), vmem((n, LANES), f), vmem((n, 1), i), vmem((n, 1), f), vmem((8, hid), f),
        *[vmem(shape, f) for shape in (wide, wide, wide, wide, thin, thin, thin, thin, wide, wide, bulk, bulk)],
    ]
    for index, count in enumerate(HUB_SUMS):
        scratch += hub_buffers(count, {0: 8, 4: z.class_part - z.part}.get(index, 0))
    for total, levels in zip(z.flat, z.levels):
        scratch += flat_buffers(total, levels)
    dma = pltpu.SemaphoreType.DMA
    scratch += [
        dma((11,)), dma((11,)), dma((len(HUB_SUMS), 3)), dma((len(HUB_SUMS), 3)), dma((len(z.flat), 8)), dma((len(z.flat), 8)), dma((4 + z.halves,))
    ]
    inside = pl.BlockSpec(memory_space=pltpu.VMEM)
    outside = pl.BlockSpec(memory_space=pl.ANY)
    return pl.pallas_call(
        functools.partial(train_kernel, z),
        out_shape=(
            *[jax.ShapeDtypeStruct((total, LANES), f) for total in z.flat],
            jax.ShapeDtypeStruct((2, halo, hid), f),
            jax.ShapeDtypeStruct((8, LANES), f),
        ),
        in_specs=[inside] * 11 + [outside] + [inside] * 4,
        out_specs=(outside, outside, outside, outside, outside, inside),
        scratch_shapes=scratch,
        compiler_params=pltpu.CompilerParams(
            collective_id=0, has_side_effects=True, vmem_limit_bytes=62 * 1024 * 1024
        ),
        name="train",
    )(*args)


def update_kernel(
    z,
    two_hbm, upper_hbm, low_a_hbm, low_b_hbm, fresh_hbm, w1_hbm, m1_hbm, v1_hbm, w2_hbm, m2_hbm, v2_hbm,
    misc, w3, m3, v3, bs, mb, vb,
    o1, n1, s1, c1, o2, n2, s2, c2, o_fresh,
    o_norm, o_loss, o_count, o3, n3, s3, c3, ob, nb, sb, cb,
    two, upper, low_a, low_b, held, w1, m1, v1, w2, m2, v2, d1, d2, in_sem, out_sem,
):
    inward = [
        pltpu.make_async_copy(src, dst, in_sem.at[i])
        for i, (src, dst) in enumerate(
            (
                (two_hbm, two), (upper_hbm, upper), (low_a_hbm, low_a), (low_b_hbm, low_b),
                (w1_hbm, w1), (m1_hbm, m1), (v1_hbm, v1), (w2_hbm, w2), (m2_hbm, m2), (v2_hbm, v2), (fresh_hbm, held),
            )
        )
    ]
    for copy in inward:
        copy.start()
    outward = []

    def leave(src, dst, rows=None):
        if rows is not None:
            src, dst = src.at[rows], dst.at[rows]
        outward.append(pltpu.make_async_copy(src, dst, out_sem.at[len(outward)]))
        outward[-1].start()

    def squares(values):
        return jnp.sum(jnp.sum(values * values, axis=0, keepdims=True), axis=1, keepdims=True)

    at_loss = z.at_bias + 2 * z.halves + 1
    for copy in inward[:4]:
        copy.wait()
    norm = jnp.sqrt(
        squares(two[...]) + squares(upper[0:at_loss, :]) + squares(low_a[...]) + squares(low_b[...])
    )
    o_norm[...] = norm
    o_loss[...] = upper[at_loss : at_loss + 1, 0:1]
    o_count[...] = misc[z.count_rows : z.count_rows + 1, 0:1]
    factor = jnp.minimum(1.0, CLIP / (norm + 1e-06))

    def step(grad, old, first, second):
        clipped = grad * factor
        moment = 0.5 * first + 0.5 * clipped
        squared = 0.5 * second + 0.5 * clipped * clipped
        below = jnp.sqrt(squared * (1.0 / CORRECT)) + EPSILON
        fresh = old * (1.0 - RATE * DECAY) - (moment * (RATE / CORRECT)) / below
        return fresh, moment, squared

    def renew(rows, lanes, grad, w, m, v):
        w[rows, lanes], m[rows, lanes], v[rows, lanes] = step(grad, w[rows, lanes], m[rows, lanes], v[rows, lanes])

    def lane_half(half):
        return slice(half * LANES, (half + 1) * LANES)

    low = z.fin - z.shift
    lows = (low_a, low_b)
    for copy in inward[4:7]:
        copy.wait()
    for half in range(z.halves):
        u0 = half * z.frows
        renew(slice(0, low), lane_half(half), upper[u0 : u0 + low, :], w1, m1, v1)
    for src, dst in ((w1, o1), (m1, n1), (v1, s1)):
        leave(src, dst, pl.ds(0, low))
    for half in range(z.halves):
        u0, lower, lanes = half * z.frows, lows[half], lane_half(half)
        if z.shift:
            renew(slice(low, low + 8), lanes, upper[u0 + low : u0 + low + 8, :] + lower[0:8, :], w1, m1, v1)
            renew(slice(low + 8, 2 * z.fin), lanes, lower[8 : z.fin + z.shift, :], w1, m1, v1)
        else:
            renew(slice(low, 2 * z.fin), lanes, lower[0 : z.fin, :], w1, m1, v1)
    for src, dst in ((w1, o1), (m1, n1), (v1, s1)):
        leave(src, dst, pl.ds(low, 2 * z.fin - low))
    d1[...] = w1[...].astype(BF16)
    leave(d1, c1)
    for copy in inward[7:10]:
        copy.wait()
    for half in range(z.halves):
        start = half * 2 * z.hid
        renew(slice(0, 2 * z.hid), lane_half(half), two[start : start + 2 * z.hid, :], w2, m2, v2)
    for src, dst in ((w2, o2), (m2, n2), (v2, s2)):
        leave(src, dst)
    d2[...] = w2[...].astype(BF16)
    leave(d2, c2)
    inward[10].wait()
    leave(held, o_fresh)
    packed = two[z.at_three : z.at_three + z.hid, :].T
    for half in range(2):
        grad = packed[half * (LANES // 2) : half * (LANES // 2) + z.cls, :]
        part = slice(half * z.hid, (half + 1) * z.hid)
        fresh, moment, squared = step(grad, w3[:, part], m3[:, part], v3[:, part])
        o3[:, part] = fresh
        n3[:, part] = moment
        s3[:, part] = squared
        c3[:, part] = fresh.astype(BF16)
    size = bs.shape[0]
    line = jnp.concatenate([upper[z.at_bias + k : z.at_bias + k + 1, :] for k in range(2 * z.halves + 1)], axis=1)
    flat = lambda ref: ref[...].reshape(1, size)
    fresh, moment, squared = step(line[:, 0:size], flat(bs), flat(mb), flat(vb))
    ob[...] = fresh.reshape(size)
    nb[...] = moment.reshape(size)
    sb[...] = squared.reshape(size)
    cb[...] = ob[...].astype(BF16)
    for copy in outward:
        copy.wait()


def update(z, *args):
    inside = pl.BlockSpec(memory_space=pltpu.VMEM)
    outside = pl.BlockSpec(memory_space=pl.ANY)
    shape = jax.ShapeDtypeStruct
    one, two, three_t, line = args[5].shape, args[8].shape, args[12].shape, args[15].shape

    def group(size):
        return [shape(size, F32)] * 3 + [shape(size, BF16)]

    shapes = [
        *group(one), *group(two), shape(args[4].shape, F32), *[shape((1, 1), F32)] * 3, *group(three_t), *group(line)
    ]
    return pl.pallas_call(
        functools.partial(update_kernel, z),
        out_shape=tuple(shapes),
        in_specs=[outside] * 11 + [inside] * 7,
        out_specs=tuple([outside] * 9 + [inside] * 11),
        scratch_shapes=[
            *[pltpu.VMEM(a.shape, F32) for a in args[:11]],
            pltpu.VMEM(one, BF16), pltpu.VMEM(two, BF16),
            pltpu.SemaphoreType.DMA((11,)), pltpu.SemaphoreType.DMA((12,)),
        ],
        compiler_params=pltpu.CompilerParams(vmem_limit_bytes=62 * 1024 * 1024),
        name="update",
    )(*args)


def solution(mesh):
    def local(
        features, hub_features, low_lists, low_masks, high_lists, high_masks, hub_lists, hub_masks, send_rows,
        labels, train_mask, stale_rows, weight_one, weight_two, weight_three, biases,
        mean_one, mean_two, mean_three, mean_biases, square_one, square_two, square_three, square_biases,
    ):
        z = Sizes(mesh, features, low_lists, high_lists, hub_lists, send_rows, weight_one, weight_three)
        three_t = weight_three.T
        two, upper, low_first, low_second, renewed, misc = train(
            z, features.T, hub_features.T, low_lists.T, low_masks.T, high_lists.T, high_masks.T,
            hub_lists[0].T, hub_masks[0].T, send_rows[0],
            labels.reshape(-1, LANES), train_mask.reshape(-1, LANES), stale_rows,
            weight_one, weight_two, three_t, biases,
        )
        o1, n1, s1, c1, o2, n2, s2, c2, renewed, norm, loss, count, o3, n3, s3, c3, ob, nb, sb, cb = update(
            z, two, upper, low_first, low_second, renewed, weight_one, mean_one, square_one,
            weight_two, mean_two, square_two, misc, three_t, mean_three.T, square_three.T,
            biases, mean_biases, square_biases,
        )
        return (
            norm[0, 0], loss[0, 0], count[0, 0],
            o1, o2, o3.T, ob, n1, n2, n3.T, nb, s1, s2, s3.T, sb, c1, c2, c3.T, cb, renewed,
        )

    spread = ("dom", "sub")
    rows, all_same, cube = P(spread, None), P(), P(spread, None, None)
    stale = P(None, spread, None)
    in_specs = (
        rows, all_same, rows, rows, rows, rows, cube, cube, cube, P(spread), P(spread), stale, *[all_same] * 12
    )
    out_specs = (*[all_same] * 19, stale)
    return jax.shard_map(local, mesh=mesh, in_specs=in_specs, out_specs=out_specs, check_vma=False)
```

```python
import functools

import jax
import jax.numpy as jnp
from jax import lax
from jax.experimental import pallas as pl
from jax.experimental.pallas import tpu as pltpu
from jax.sharding import PartitionSpec as P

MESH = pl.DeviceIdType.MESH
F32 = jnp.float32
BF16 = jnp.bfloat16

STEP = 5
KEEP = 0.95
SMOOTH = 0.1
CLIP = 0.02
RATE = 0.03
DECAY = 0.01
EPSILON = 1e-08
CORRECT = 1.0 - 0.5**STEP
GELU_A = 0.7978845608
GELU_B = 0.044715
LANES = 128
LIMIT = 4


def up(value, unit):
    return -(-value // unit) * unit


def split(values):
    high = values.astype(BF16)
    return high, (values - high.astype(F32)).astype(BF16)


def dot(left, right):
    return jnp.dot(left, right, preferred_element_type=F32)


def dot_nt(left, right):
    return lax.dot_general(left, right, (((1,), (1,)), ((), ())), preferred_element_type=F32)


def dot_tn(left, right):
    return lax.dot_general(left, right, (((0,), (0,)), ((), ())), preferred_element_type=F32)


def three(product, left, right):
    return (
        product(left[0], right[1]) + product(left[1], right[0])
    ) + product(left[0], right[0])


def gelu(v):
    return 0.5 * v * (1.0 + jnp.tanh(GELU_A * (v + GELU_B * (v * v * v))))


def gelu_slope(v):
    t = jnp.tanh(GELU_A * (v + GELU_B * (v * v * v)))
    return 0.5 * (1.0 + t) + (0.5 * GELU_A) * v * (1.0 - t * t) * (1.0 + (3.0 * GELU_B) * (v * v))


def tiles(total, step, body):
    if total // step <= LIMIT:
        for index in range(total // step):
            body(index * step)
        return

    @pl.loop(0, total // step)
    def _(index):
        body(pl.multiple_of(index * step, step))


class Sizes:
    def __init__(self, mesh, features, low_lists, high_lists, hub_lists, send_rows, weight_one, weight_three):
        self.dom, self.sub = mesh.shape["dom"], mesh.shape["sub"]
        self.devices = self.dom * self.sub
        self.nodes, self.fin = features.shape
        self.low, self.k_low = low_lists.shape
        self.high, self.k_high = high_lists.shape
        self.hubs, self.k_hub = hub_lists.shape[1:]
        self.blk = send_rows.shape[2]
        self.halo = self.devices * self.blk
        self.hid = weight_one.shape[1]
        self.halves = self.hid // LANES
        self.cls = weight_three.shape[1]
        self.rows = self.nodes + self.hubs
        self.table = self.nodes + self.halo + self.hubs
        self.fpad = up(self.fin, LANES)
        self.frows = up(self.fin, 8)
        self.shift = self.fin % 8
        self.brows = up(self.fin + self.shift, 8)
        self.part = self.hubs // self.dom
        self.count_rows = self.hubs // LANES
        self.paired = self.part % 16 == 0
        self.class_part = self.part // 2 if self.paired else self.part
        self.packed = self.blk % 16 == 0
        self.cblk = self.blk // 2 if self.packed else self.blk
        unit = 8 * self.devices
        self.at_three = self.halves * 2 * self.hid
        self.at_bias = self.halves * self.frows
        self.flat = (
            up(self.at_three + self.hid, unit),
            up(self.at_bias + 8, unit),
            *[up(self.brows, unit)] * self.halves,
        )
        three, four = (2, self.dom // 2, self.sub), (2, self.dom // 2, 2, self.sub // 2)
        self.levels = (four, four, *[three] * self.halves)


class HubSum:
    def __init__(self, z, place, remote, buffers, sems, index):
        self.z, self.place, self.remote = z, place, remote
        self.source, self.ra, self.rb, self.out = buffers
        self.sent, self.got = sems
        self.index = index

    def put(self, values):
        self.source[...] = values.reshape(self.source.shape)

    def sems(self, phase):
        return self.sent.at[self.index, phase], self.got.at[self.index, phase]

    def over_dom(self, start, phase):
        d, s = self.place

        @pl.loop(1, self.z.dom)
        def _(k):
            pd = lax.rem(d + k, self.z.dom)
            src, dst = start(pd)
            self.remote(src, dst, *self.sems(phase), pd, s).start()

    def dom_done(self, ref, phase):
        d, s = self.place
        some = ref.at[pl.ds(0, self.z.dom - 1)]
        copy = self.remote(some, some, *self.sems(phase), lax.rem(d + 1, self.z.dom), s)
        copy.wait_recv()
        copy.wait_send()

    def scatter(self):
        d, s = self.place
        self.over_dom(lambda pd: (self.source.at[pd], self.ra.at[d]), 0)

    def swap(self):
        d, s = self.place
        self.dom_done(self.ra, 0)
        total = self.source[d]
        for k in range(1, self.z.dom):
            total = total + self.ra[lax.rem(d + k, self.z.dom)]
        self.rb[s] = total

        @pl.loop(1, self.z.sub)
        def _(k):
            ps = lax.rem(s + k, self.z.sub)
            self.remote(self.rb.at[s], self.rb.at[s], *self.sems(1), d, ps).start()

    def gather(self):
        d, s = self.place
        some = self.rb.at[pl.ds(0, self.z.sub - 1)]
        copy = self.remote(some, some, *self.sems(1), d, lax.rem(s + 1, self.z.sub))
        copy.wait_recv()
        copy.wait_send()
        total = self.rb[0]
        for k in range(1, self.z.sub):
            total = total + self.rb[k]
        self.out[d] = total
        self.over_dom(lambda pd: (self.out.at[d], self.out.at[d]), 2)

    def finish(self):
        self.dom_done(self.out, 2)

    def end(self):
        self.finish()
        return self.out[:, 0 : self.z.part, :].reshape(self.z.hubs, self.out.shape[-1])


class FlatSum:
    def __init__(self, z, place, remote, buffers, sems, index):
        d, s = place
        self.remote, self.index = remote, index
        self.source, self.out = buffers[0], buffers[1]
        depth = len(z.levels[index])
        self.landed, self.parts = buffers[2 : 2 + depth], (buffers[0], *buffers[2 + depth :])
        self.sent, self.got = sems
        pair = lax.rem(d, 2)
        chip = d // 2
        self.levels = (
            (2, pair, lambda j: (chip * 2 + j, s)),
            (z.dom // 2, chip, lambda j: (j * 2 + pair, s)),
            (z.sub, s, lambda j: (d, j)),
        )
        if depth == 4:
            near, far = lax.rem(s, 2), s // 2
            self.levels = (
                *self.levels[:2],
                (2, near, lambda j: (d, far * 2 + j)),
                (z.sub // 2, far, lambda j: (d, j * 2 + near)),
            )
        self.first, offset, rows = [], 0, self.source.shape[0]
        for size, mine, _ in self.levels:
            rows = rows // size
            self.first.append((offset, rows))
            offset = offset + mine * rows

    def sems(self, phase):
        return self.sent.at[self.index, phase], self.got.at[self.index, phase]

    def rows(self, start, count):
        return pl.ds(pl.multiple_of(start, 8), count)

    def send(self, level):
        size, mine, peer = self.levels[level]
        count = self.first[level][1]

        @pl.loop(1, size)
        def _(k):
            j = lax.rem(mine + k, size)
            self.remote(
                self.parts[level].at[self.rows(j * count, count)],
                self.landed[level].at[mine],
                *self.sems(level),
                *peer(j),
            ).start()

    def receive(self, level):
        size, mine, peer = self.levels[level]
        offset, count = self.first[level]
        ref = self.landed[level]
        some = ref.at[pl.ds(0, size - 1)]
        copy = self.remote(some, some, *self.sems(level), *peer(lax.rem(mine + 1, size)))
        copy.wait_recv()
        copy.wait_send()
        total = self.parts[level][self.rows(mine * count, count), :]
        for k in range(1, size):
            total = total + ref[lax.rem(mine + k, size)]
        if level + 1 < len(self.levels):
            self.parts[level + 1][...] = total
        else:
            self.out[self.rows(offset + mine * count, count), :] = total

    def spread(self, level):
        size, mine, peer = self.levels[level]
        offset, count = self.first[level]
        held = self.out.at[self.rows(offset + mine * count, count)]

        @pl.loop(1, size)
        def _(k):
            j = lax.rem(mine + k, size)
            self.remote(held, held, *self.sems(4 + level), *peer(j)).start()

    def collect(self, level):
        size, mine, peer = self.levels[level]
        some = self.out.at[pl.ds(0, (size - 1) * self.first[level][1])]
        copy = self.remote(some, some, *self.sems(4 + level), *peer(lax.rem(mine + 1, size)))
        copy.wait_recv()
        copy.wait_send()


HUB_SUMS = (1, 1, 1, 1, 1, 2)


def train_kernel(
    z,
    feat, hubf, lowl, lowm, highl, highm, hubl, hubm, send, lab, tmask, stale_hbm, w1, w2, w3, bias,
    two_hbm, upper_hbm, lower_hbm, tail_hbm, fresh_hbm, misc,
    ab, abt, sel, selt, colb, keyt, keys, xh, xl, xth, xtl, w1h, w1l, w2h, w2l, w3t, w3h, w3l,
    tb, tc, inv, q, magg, h1h, h1l, m1h, m1l, h2h, h2l, dg0, dg1, dph, dpl, dmh, dml, eb, gown, gthree, stale,
    zst, pself, labc, trainw, brow,
    send_a, recv_a, send_b, recv_b, send_c, recv_c, send_d, recv_d, recv_e, recv_f, send_g, recv_g,
    *rest_refs,
):
    hub_refs, flat_refs = rest_refs[: 4 * len(HUB_SUMS)], rest_refs[4 * len(HUB_SUMS) : -7]
    xs, xr, hsem_s, hsem_r, gsem_s, gsem_r, lsem = rest_refs[-7:]
    send_e, send_f = send_a, send_b
    d = lax.axis_index("dom")
    s = lax.axis_index("sub")
    me = d * z.sub + s
    nd, halo, hubs, hid, fin = z.nodes, z.halo, z.hubs, z.hid, z.fin
    halo0, hub0 = nd, nd + halo
    own, halos, hubr = slice(0, nd), slice(halo0, hub0), slice(hub0, z.table)
    hubq = slice(nd, z.rows)
    up_rows, low_rows = slice(0, hid), slice(hid, 2 * hid)
    i32 = jnp.int32
    both = range(z.halves)

    def lanes(h):
        return slice(h * LANES, (h + 1) * LANES)

    barrier = pltpu.get_barrier_semaphore()

    @pl.loop(1, z.devices)
    def _(k):
        pl.semaphore_signal(
            barrier,
            inc=1,
            device_id=(lax.rem(d + k // z.sub, z.dom), lax.rem(s + k % z.sub, z.sub)),
            device_id_type=MESH,
        )

    stale_copy = pltpu.make_async_copy(stale_hbm, stale, lsem.at[0])
    stale_copy.start()

    def remote(src, dst, ssem, rsem, pd, ps):
        return pltpu.make_async_remote_copy(
            src_ref=src, dst_ref=dst, send_sem=ssem, recv_sem=rsem, device_id=(pd, ps), device_id_type=MESH
        )

    place = (d, s)
    sums = [
        HubSum(z, place, remote, hub_refs[4 * i : 4 * i + 4], (hsem_s, hsem_r), i) for i in range(len(HUB_SUMS))
    ]
    grads, start = [], 0
    for i in range(len(z.flat)):
        refs = flat_refs[start : start + 1 + 2 * len(z.levels[i])]
        grads.append(FlatSum(z, place, remote, refs, (gsem_s, gsem_r), i))
        start += len(refs)
    two, upper, *lowers = grads

    def part_of(portion):
        return 1 + (z.devices - 1) * portion // 8

    def exchange_start(src, dst, i, first=0, last=8):
        @pl.loop(part_of(first), part_of(last))
        def _(k):
            mixed = lax.rem(k * 5, z.devices)
            pd = lax.rem(d + mixed // z.sub, z.dom)
            ps = lax.rem(s + mixed % z.sub, z.sub)
            remote(src.at[pd * z.sub + ps], dst.at[me], xs.at[i], xr.at[i], pd, ps).start()

        if first == 0:
            dst[me] = src[me]

    def exchange_wait(src, dst, i):
        some = pl.ds(0, z.devices - 1)
        copy = remote(src.at[some], dst.at[some], xs.at[i], xr.at[i], lax.rem(d + 1, z.dom), s)
        copy.wait_recv()
        copy.wait_send()

    def put_split(ref, rows, values):
        width = values.shape[1]
        high, rest = split(values)
        ref[rows, 0:width] = high
        ref[rows, width : 2 * width] = rest

    def put_pair(high_ref, rest_ref, rows, columns, values):
        high, rest = split(values)
        high_ref[rows, columns] = high
        rest_ref[rows, columns] = rest
        return high, rest

    def added(product):
        return product[:, :LANES] + product[:, LANES:]

    per_tile = 256 // z.blk

    def turn(source, target, r_count, c_count, c_start=0, step=128):
        def body(r):
            for c in range(c_start, c_count, step):
                target[c : c + step, pl.ds(r, step)] = source[pl.ds(r, step), c : c + step].T

        tiles(r_count, step, body)

    pad0 = fin // 16 * 16
    xth[pad0 : z.fpad, :] = jnp.zeros((z.fpad - pad0, z.rows), BF16)
    xtl[pad0 : z.fpad, :] = jnp.zeros((z.fpad - pad0, z.rows), BF16)
    w1h[pad0 : z.fpad, :] = jnp.zeros((z.fpad - pad0, 2 * hid), BF16)
    w1l[pad0 : z.fpad, :] = jnp.zeros((z.fpad - pad0, 2 * hid), BF16)
    put_pair(xth, xtl, slice(0, fin), own, feat[...])
    turn(xth, xh, z.fpad, nd)
    turn(xtl, xl, z.fpad, nd)
    put_pair(w1h, w1l, slice(0, fin), low_rows, w1[fin : 2 * fin, :])

    def project(rows, columns):
        return three(dot, (xh[rows, :], xl[rows, :]), (w1h[:, columns], w1l[:, columns]))

    def put_halves(rows, values):
        for h in both:
            put_split(tb.at[h], rows, values[:, lanes(h)])

    tiles(nd, 256, lambda r: put_halves(pl.ds(r, 256), project(pl.ds(r, 256), low_rows)))

    colb[0 : z.devices, 0 : z.blk] = send[...]
    turned = colb[...].T

    for tile in range(halo // 256):
        first = tile * per_tile
        column = jnp.concatenate([turned[0 : z.blk, p : p + 1] for p in range(first, first + per_tile)], axis=0)
        hit = column == lax.broadcasted_iota(i32, (256, nd), 1)
        sel[tile * 256 : tile * 256 + 256, :] = jnp.where(hit, 1.0, 0.0).astype(BF16)

    def pick(source, target):
        def body(r):
            values = added(dot(sel[pl.ds(r, 256), :], source[own, :]))
            target[pl.ds(r // z.blk, per_tile)] = values.reshape(per_tile, z.blk, LANES)

        tiles(halo, 256, body)

    pick(tb.at[0], send_a.at[0])
    pl.semaphore_wait(barrier, z.devices - 1)
    for h in both:
        if h:
            pick(tb.at[h], send_a.at[h])
        exchange_start(send_a.at[h], recv_a.at[h], h)

    keyt[...] = jnp.full(keyt.shape, -1, i32)
    keyt[0 : z.k_low, 0 : z.low] = jnp.where(lowm[...] > 0, lowl[...], -1)
    keyt[0 : z.k_high, z.low : nd] = jnp.where(highm[...] > 0, highl[...], -1)
    keyt[0 : z.k_hub, hubq] = jnp.where(hubm[...] > 0, hubl[...], -1)
    for block in range(z.rows // LANES):
        keys[lanes(block), :] = keyt[:, lanes(block)].T
    counts = jnp.sum(jnp.where(keys[...] >= 0, 1.0, 0.0), axis=1, keepdims=True)
    inv[own, :] = 1.0 / jnp.maximum(counts[own, :], 1.0)
    train_local = jnp.sum(jnp.sum(tmask[...].astype(F32), axis=1, keepdims=True), axis=0, keepdims=True)
    used_slots = jnp.sum(jnp.where(keyt[0 : z.k_hub, hubq] >= 0, 1.0, 0.0), axis=0, keepdims=True)
    extra = [used_slots[:, lanes(c)] for c in range(z.count_rows)] + [jnp.broadcast_to(train_local, (1, LANES))]
    extra.append(jnp.zeros((8 - len(extra), LANES), F32))
    extra = jnp.concatenate(extra, axis=0)
    for block in range(z.dom):
        sums[0].source[block, z.part : z.part + 8, :] = extra

    def build(first, count, slots):
        def group(r):
            rows = pl.ds(first + r, 16)
            key = keys[rows, :].astype(jnp.int16)
            spot = lax.broadcasted_iota(i32, (16, z.table), 1).astype(jnp.int16)
            one, none = jnp.ones((16, z.table), BF16), jnp.zeros((16, z.table), BF16)
            total = none
            for k in range(slots):
                total = total + jnp.where(jnp.broadcast_to(key[:, k : k + 1], (16, z.table)) == spot, one, none)
            ab[rows, :] = total

        tiles(count, 16, group)

    build(0, z.low, z.k_low)
    build(nd, hubs, z.k_hub)
    build(z.low, z.high, z.k_high)

    put_pair(xth, xtl, slice(0, fin), hubq, hubf[...])
    turn(xth, xh, z.fpad, z.rows, nd)
    turn(xtl, xl, z.fpad, z.rows, nd)
    put_pair(w1h, w1l, slice(0, fin), up_rows, w1[0:fin, :])
    brow[...] = jnp.zeros(brow.shape, F32)
    line = bias[...].reshape(1, 2 * hid + z.cls)
    brow[0:1, :] = line[:, 0:hid]
    brow[1:2, :] = line[:, hid : 2 * hid]
    brow[2:3, 0 : z.cls] = line[:, 2 * hid : 2 * hid + z.cls]
    put_halves(hubr, project(hubq, low_rows))

    def own_tile(r):
        rows = pl.ds(r, 256)
        q[rows, :] = project(rows, up_rows) + brow[0:1, :]

    tiles(nd, 256, own_tile)

    def gather_local(h):
        def body(r):
            rows = pl.ds(r, 256)
            magg[rows, lanes(h)] = added(dot(ab[rows, own], tb[h, own, :]) + dot(ab[rows, hubr], tb[h, hubr, :]))

        tiles(z.rows, 256, body)

    gather_local(0)

    def with_halo(rows, h):
        return magg[rows, lanes(h)] + added(dot(ab[rows, halos], tb[h, halos, :]))

    def layer_one(h):
        def body(r):
            rows = pl.ds(r, 256)
            pre = q[rows, lanes(h)] + with_halo(rows, h) * inv[rows, :]
            q[rows, lanes(h)] = pre
            high, rest = put_pair(h1h, h1l, rows, lanes(h), gelu(pre))
            tb[h, rows, 0:LANES] = high
            tb[h, rows, LANES : 2 * LANES] = rest

        tiles(nd, 256, body)

    exchange_wait(send_a.at[0], recv_a.at[0], 0)
    put_split(tb.at[0], halos, recv_a[0].reshape(halo, LANES))
    sums[0].source[:, 0 : z.part, :] = with_halo(hubq, 0).reshape(z.dom, z.part, LANES)
    sums[0].scatter()
    layer_one(0)
    pick(tb.at[0], send_b.at[0])
    exchange_start(send_b.at[0], recv_b.at[0], 2, 0, 4)
    gather_local(1)
    own_tile(nd)
    turn(sel, selt, halo, nd)
    exchange_wait(send_a.at[1], recv_a.at[1], 1)
    put_split(tb.at[1], halos, recv_a[1].reshape(halo, LANES))
    sums[1].put(with_halo(hubq, 1))
    sums[1].scatter()
    exchange_start(send_b.at[0], recv_b.at[0], 2, 4, 8)
    layer_one(1)
    pick(tb.at[1], send_b.at[1])
    sums[0].swap()
    sums[1].swap()
    exchange_start(send_b.at[1], recv_b.at[1], 3, 0, 4)
    put_pair(w2h, w2l, slice(0, 2 * hid), slice(0, hid), w2[...])
    w3t[...] = jnp.zeros(w3t.shape, F32)
    w3t[0 : z.cls, :] = w3[...]
    put_pair(w3h, w3l, slice(0, 2 * hid), slice(0, LANES), w3t[...].T)
    turn(ab, abt, z.rows, z.table)
    sums[0].gather()
    sums[1].gather()
    exchange_start(send_b.at[1], recv_b.at[1], 3, 4, 8)
    for grad in grads:
        grad.source[...] = jnp.zeros(grad.source.shape, F32)

    stale_copy.wait()
    zst[...] = three(dot, split(KEEP * stale[1]), (w3h[low_rows, :], w3l[low_rows, :]))
    dg0[own, :] = gelu_slope(q[own, :])
    for block in range(nd // LANES):
        diag = lax.broadcasted_iota(i32, (LANES, LANES), 0) == lax.broadcasted_iota(i32, (LANES, LANES), 1)
        line = jnp.broadcast_to(lab[block : block + 1, :], (LANES, LANES))
        labc[lanes(block), :] = jnp.sum(jnp.where(diag, line, 0), axis=1, keepdims=True)
        line = jnp.broadcast_to(tmask[block : block + 1, :].astype(F32), (LANES, LANES))
        trainw[lanes(block), :] = jnp.sum(jnp.where(diag, line, 0.0), axis=1, keepdims=True)
    first_hub = sums[0].end()
    misc[...] = sums[0].out[0, z.part : z.part + 8, :]
    colb[0:8, :] = misc[...].astype(i32)
    turned_counts = colb[...].T
    for c in range(z.count_rows):
        inv[nd + c * LANES : nd + (c + 1) * LANES, :] = 1.0 / turned_counts[:, c : c + 1].astype(F32)
    hub_ends = (first_hub, sums[1].end())
    for h in both:
        pre = q[hubq, lanes(h)] + hub_ends[h] * inv[hubq, :]
        dg0[hubq, lanes(h)] = gelu_slope(pre)
        high, rest = put_pair(h1h, h1l, hubq, lanes(h), gelu(pre))
        tb[h, hubr, 0:LANES] = high
        tb[h, hubr, LANES : 2 * LANES] = rest

    for h in both:
        gather_local(h)

    def own_two(r):
        rows = pl.ds(r, 256)
        q[rows, :] = three(dot, (h1h[rows, :], h1l[rows, :]), (w2h[up_rows, :], w2l[up_rows, :])) + brow[1:2, :]

    tiles(z.rows, 256, own_two)

    def second(h):
        exchange_wait(send_b.at[h], recv_b.at[h], 2 + h)
        renewed = KEEP * stale[0, :, lanes(h)] + (1.0 - KEEP) * recv_b[h].reshape(halo, LANES)
        stale[0, :, lanes(h)] = renewed
        put_split(tb.at[h], halos, renewed)
        sums[2 + h].put(with_halo(hubq, h))
        sums[2 + h].scatter()

        def body(r):
            rows = pl.ds(r, 256)
            put_pair(m1h, m1l, rows, lanes(h), with_halo(rows, h) * inv[rows, :])

        tiles(nd, 256, body)

    second(0)
    second(1)
    sums[2].swap()

    def layer_two(r):
        rows = pl.ds(r, 256)
        pre = q[rows, :] + three(dot, (m1h[rows, :], m1l[rows, :]), (w2h[low_rows, :], w2l[low_rows, :]))
        q[rows, :] = pre
        high, rest = put_pair(h2h, h2l, rows, slice(0, hid), gelu(pre))
        put_split(tc, rows, three(dot, (high, rest), (w3h[low_rows, :], w3l[low_rows, :])))

    tiles(nd, 256, layer_two)
    class_lane = lax.broadcasted_iota(i32, (1, 1, LANES), 2) < LANES // 2

    def pack(values):
        blocks = values.reshape(values.shape[0] // z.blk, z.blk, LANES)
        if z.packed:
            return blocks[:, : z.cblk] + pltpu.roll(blocks[:, z.cblk :], LANES // 2, 2)
        return blocks

    def unpack(blocks):
        if z.packed:
            first = jnp.where(class_lane, blocks, 0.0)
            second = jnp.where(class_lane, pltpu.roll(blocks, LANES // 2, 2), 0.0)
            blocks = jnp.concatenate([first, second], axis=1)
        return blocks.reshape(halo, LANES)

    def pick_class(r):
        send_c[pl.ds(r // z.blk, per_tile)] = pack(added(dot(sel[pl.ds(r, 256), :], tc[own, :])))

    tiles(halo, 256, pick_class)
    sums[3].swap()
    sums[2].gather()
    exchange_start(send_c, recv_c, 4)

    def pick_wide(r):
        chosen = sel[pl.ds(r, 256), :]
        values = dot(chosen, h2l[own, :]) + dot(chosen, h2h[own, :])
        send_g[pl.ds(r // z.blk, per_tile)] = values.reshape(per_tile, z.blk, hid)


    def own_three(r):
        rows = pl.ds(r, 256)
        pself[rows, :] = three(dot, (h2h[rows, :], h2l[rows, :]), (w3h[up_rows, :], w3l[up_rows, :])) + brow[2:3, 0:LANES]

    tiles(nd, 256, own_three)

    def class_local(r):
        rows = pl.ds(r, 256)
        magg[rows, 0:LANES] = added(dot(ab[rows, own], tc[own, :]))

    tiles(nd, 256, class_local)
    sums[3].gather()
    tiles(halo, 256, pick_wide)
    exchange_start(send_g, recv_g, 5, 0, 3)
    dg1[own, :] = gelu_slope(q[own, :])
    for h in both:
        put_pair(m1h, m1l, hubq, lanes(h), sums[2 + h].end() * inv[hubq, :])
    pre = q[hubq, :] + three(dot, (m1h[hubq, :], m1l[hubq, :]), (w2h[low_rows, :], w2l[low_rows, :]))
    high, rest = put_pair(h2h, h2l, hubq, slice(0, hid), gelu(pre))
    put_split(tc, hubr, three(dot, (high, rest), (w3h[low_rows, :], w3l[low_rows, :])))
    q[hubq, :] = pre

    exchange_wait(send_c, recv_c, 4)
    put_split(tc, halos, zst[...] + (1.0 - KEEP) * unpack(recv_c[...]))
    used = lax.broadcasted_iota(i32, (256, LANES), 1)
    train_total = misc[z.count_rows : z.count_rows + 1, 0:1]
    at_bias = z.at_bias

    def head(r):
        rows = pl.ds(r, 256)
        logits = pself[rows, :] + (magg[rows, 0:LANES] + added(dot(ab[rows, halo0:], tc[halo0:, :]))) * inv[rows, :]
        valid = used < z.cls
        top = jnp.max(jnp.where(valid, logits, -1e30), axis=1, keepdims=True)
        shifted = logits - top
        powers = jnp.where(valid, jnp.exp(jnp.where(valid, shifted, 0.0)), 0.0)
        total = jnp.sum(powers, axis=1, keepdims=True)
        log_probs = jnp.where(valid, shifted - jnp.log(total), 0.0)
        target = jnp.where(used == labc[rows, :], 1.0 - SMOOTH, 0.0) + SMOOTH / z.cls
        weight = trainw[rows, :]
        losses = jnp.sum(jnp.where(valid, -target * log_probs, 0.0), axis=1, keepdims=True) * weight
        grad = jnp.where(valid, powers / total - target, 0.0) * weight / train_total
        at = at_bias + 2 * z.halves
        upper.source[at : at + 1, :] = upper.source[at : at + 1, :] + jnp.sum(grad, axis=0, keepdims=True)
        at = at + 1
        upper.source[at : at + 1, :] = upper.source[at : at + 1, :] + jnp.sum(losses, axis=0, keepdims=True)
        put_pair(dph, dpl, rows, slice(0, LANES), grad)
        put_split(eb.at[0], rows, grad * inv[rows, :])

    tiles(nd, 256, head)


    def pack_hubs(values):
        blocks = values.reshape(z.dom, z.part, LANES)
        if z.paired:
            return blocks[:, : z.class_part] + pltpu.roll(blocks[:, z.class_part :], LANES // 2, 2)
        return blocks

    def unpack_hubs(blocks):
        if z.paired:
            first = jnp.where(class_lane, blocks, 0.0)
            second = jnp.where(class_lane, pltpu.roll(blocks, LANES // 2, 2), 0.0)
            blocks = jnp.concatenate([first, second], axis=1)
        return blocks.reshape(hubs, LANES)

    sums[4].put(pack_hubs(added(dot(abt[hubr, own], eb[0, own, :]))))
    sums[4].scatter()

    def back_class(r):
        values = added(dot(abt[pl.ds(halo0 + r, 256), own], eb[0, own, :]))
        put_split(tc, pl.ds(halo0 + r, 256), values)
        send_d[pl.ds(r // z.blk, per_tile)] = pack((1.0 - KEEP) * values)

    tiles(halo, 256, back_class)
    sums[4].swap()
    exchange_start(send_d, recv_d, 6)
    gown[own, 0:LANES] = added(dot(abt[own, own], eb[0, own, :]))

    gthree[:, 0:LANES] = three(dot_tn, split(KEEP * stale[1]), (tc[halos, 0:LANES], tc[halos, LANES : 2 * LANES]))
    sums[4].gather()
    exchange_start(send_g, recv_g, 5, 3, 6)
    hub_class = split(unpack_hubs(sums[4].source[...]))
    gthree[:, 0:LANES] = gthree[:, 0:LANES] + three(dot_tn, (h2h[hubq, :], h2l[hubq, :]), hub_class)
    gthree[:, LANES : 2 * LANES] = three(dot_tn, (h2h[own, :], h2l[own, :]), (dph[own, 0:LANES], dpl[own, 0:LANES]))
    dg1[hubq, :] = gelu_slope(q[hubq, :])

    def self_two(r):
        rows = pl.ds(r, 256)
        magg[rows, :] = three(
            dot_nt, (dph[rows, 0:LANES], dpl[rows, 0:LANES]), (w3h[up_rows, :], w3l[up_rows, :])
        )

    tiles(nd, 256, self_two)

    def owned(values):
        row = lax.broadcasted_iota(i32, (hubs, 1), 0)
        share = hubs // z.devices
        mine = jnp.where(row >= me * share, 1.0, 0.0) * jnp.where(row < (me + 1) * share, 1.0, 0.0)
        return values * mine

    def column_sums(columns):
        return jnp.sum(dmh[:, columns].astype(F32) + dml[:, columns].astype(F32), axis=0, keepdims=True)

    sums[4].finish()
    node = three(dot_nt, split(unpack_hubs(sums[4].out[...])), (w3h[low_rows, :], w3l[low_rows, :])) * dg1[hubq, :]
    put_pair(dph, dpl, hubq, slice(0, hid), node)
    put_pair(dmh, dml, hubq, slice(0, hid), owned(node))

    def spread(rows):
        values = three(dot_nt, (dph[rows, :], dpl[rows, :]), (w2h[low_rows, :], w2l[low_rows, :])) * inv[rows, :]
        for h in both:
            put_split(eb.at[h], rows, values[:, lanes(h)])

    spread(hubq)
    exchange_wait(send_d, recv_d, 6)
    put_split(tc, halos, unpack(recv_d[...]))

    def back_two(r):
        rows = pl.ds(r, 256)
        own_class = gown[rows, 0:LANES] + added(dot(selt[rows, :], tc[halos, :]))
        gown[rows, 0:LANES] = own_class
        node = (
            three(dot_nt, split(own_class), (w3h[low_rows, :], w3l[low_rows, :])) + magg[rows, :]
        ) * dg1[rows, :]
        high, rest = put_pair(dph, dpl, rows, slice(0, hid), node)
        dmh[rows, :] = high
        dml[rows, :] = rest
        spread(rows)

    tiles(nd, 256, back_two)

    for h in both:
        sums[5].source[:, :, lanes(h)] = added(dot(abt[hubr, :], eb[h])).reshape(z.dom, z.part, LANES)
    sums[5].scatter()

    def send_halo(target, factor, h):
        def body(r):
            values = added(dot(abt[pl.ds(halo0 + r, 256), :], eb[h])) * factor
            target[pl.ds(r // z.blk, per_tile)] = values.reshape(per_tile, z.blk, LANES)

        tiles(halo, 256, body)

    send_halo(send_e.at[0], 1.0 - KEEP, 0)
    exchange_start(send_e.at[0], recv_e.at[0], 7, 0, 4)
    send_halo(send_e.at[1], 1.0 - KEEP, 1)
    sums[5].swap()
    exchange_start(send_e.at[0], recv_e.at[0], 7, 4, 8)

    def own_back(r):
        rows = pl.ds(r, 256)
        q[rows, :] = three(dot_nt, (dph[rows, :], dpl[rows, :]), (w2h[up_rows, :], w2l[up_rows, :]))

    tiles(z.rows, 256, own_back)

    def own_table(r):
        rows = pl.ds(r, 256)
        for h in both:
            q[rows, lanes(h)] = q[rows, lanes(h)] + added(dot(abt[rows, :], eb[h]))

    tiles(nd, 256, own_table)
    gthree[:, 0:LANES] = gthree[:, 0:LANES] + three(dot_tn, (h2h[own, :], h2l[own, :]), split(gown[own, 0:LANES]))
    two.source[z.at_three : z.at_three + hid, :] = gthree[:, LANES : 2 * LANES] + pltpu.roll(
        gthree[:, 0:LANES], LANES // 2, 1
    )
    for h in both:
        start = h * 2 * hid
        pair = (dmh[:, lanes(h)], dml[:, lanes(h)])
        two.source[start : start + hid, :] = three(dot_tn, (h1h[...], h1l[...]), pair)
        two.source[start + hid : start + 2 * hid, :] = three(dot_tn, (m1h[...], m1l[...]), pair)
        at = at_bias + z.halves + h
        upper.source[at : at + 1, :] = column_sums(lanes(h))
    sums[5].gather()
    exchange_start(send_e.at[1], recv_e.at[1], 8, 0, 4)
    node = (sums[5].end() + q[hubq, :]) * dg0[hubq, :]
    put_pair(dmh, dml, hubq, slice(0, hid), owned(node))
    node = node * inv[hubq, :]
    for h in both:
        put_split(eb.at[h], hubq, node[:, lanes(h)])
    two.send(0)
    exchange_start(send_e.at[1], recv_e.at[1], 8, 4, 8)

    def back_one(h):
        exchange_wait(send_e.at[h], recv_e.at[h], 7 + h)
        put_split(tb.at[h], halos, recv_e[h].reshape(halo, LANES))

        def body(r):
            rows = pl.ds(r, 256)
            node = (q[rows, lanes(h)] + added(dot(selt[rows, :], tb[h, halos, :]))) * dg0[rows, lanes(h)]
            put_pair(dmh, dml, rows, lanes(h), node)
            put_split(eb.at[h], rows, node * inv[rows, :])

        tiles(nd, 256, body)
        send_halo(send_f.at[h], 1.0, h)

    back_one(0)
    exchange_start(send_f.at[0], recv_f.at[0], 9, 0, 4)
    two.receive(0)
    two.send(1)
    exchange_start(send_f.at[0], recv_f.at[0], 9, 4, 8)
    back_one(1)
    two.receive(1)
    two.send(2)
    for h in both:
        top = three(dot, (xth[...], xtl[...]), (dmh[:, lanes(h)], dml[:, lanes(h)]))
        upper.source[h * z.frows : (h + 1) * z.frows, :] = top[0 : z.frows, :]
        upper.source[at_bias + h : at_bias + h + 1, :] = column_sums(lanes(h))
    upper.send(0)
    two.receive(2)
    two.send(3)
    exchange_start(send_f.at[1], recv_f.at[1], 10, 0, 4)

    def own_last(r):
        rows = pl.ds(r, 256)
        for h in both:
            gown[rows, lanes(h)] = added(dot(abt[rows, :], eb[h]))

    tiles(nd, 256, own_last)
    for h in both:
        put_pair(dmh, dml, hubq, lanes(h), added(dot(abt[hubr, :], eb[h])))
    upper.receive(0)
    upper.send(1)
    two.receive(3)
    two.spread(3)

    def last(h):
        exchange_wait(send_f.at[h], recv_f.at[h], 9 + h)
        put_split(tb.at[h], halos, recv_f[h].reshape(halo, LANES))

        def body(r):
            rows = pl.ds(r, 256)
            put_pair(dmh, dml, rows, lanes(h), gown[rows, lanes(h)] + added(dot(selt[rows, :], tb[h, halos, :])))

        tiles(nd, 256, body)
        bottom = three(dot, (xth[...], xtl[...]), (dmh[:, lanes(h)], dml[:, lanes(h)]))
        lowers[h].source[z.shift : z.shift + fin, :] = bottom[0:fin, :]

    last(0)
    low_first, low_second = lowers
    low_first.send(0)
    exchange_start(send_f.at[1], recv_f.at[1], 10, 4, 8)
    exchange_start(send_g, recv_g, 5, 6, 8)
    upper.receive(1)
    upper.send(2)
    two.collect(3)
    two.spread(2)
    low_first.receive(0)
    low_first.send(1)
    last(1)
    low_second.send(0)
    upper.receive(2)
    upper.send(3)
    two.collect(2)
    two.spread(1)
    low_first.receive(1)
    low_first.send(2)
    upper.receive(3)
    upper.spread(3)
    low_second.receive(0)
    low_second.send(1)
    two.collect(1)
    two.spread(0)
    two_copy = pltpu.make_async_copy(two.out, two_hbm, lsem.at[1])
    upper.collect(3)
    upper.spread(2)
    low_first.receive(2)
    low_first.spread(2)
    low_second.receive(1)
    low_second.send(2)
    low_first.collect(2)
    low_first.spread(1)
    upper.collect(2)
    upper.spread(1)
    low_second.receive(2)
    low_second.spread(2)
    exchange_wait(send_g, recv_g, 5)
    stale[1] = KEEP * stale[1] + (1.0 - KEEP) * recv_g[...].reshape(halo, hid)
    fresh_copy = pltpu.make_async_copy(stale, fresh_hbm, lsem.at[2])
    fresh_copy.start()
    low_first.collect(1)
    low_first.spread(0)
    low_second.collect(2)
    low_second.spread(1)
    upper.collect(1)
    upper.spread(0)
    two.collect(0)
    two_copy.start()
    low_first.collect(0)
    lower_copy = pltpu.make_async_copy(low_first.out, lower_hbm, lsem.at[4])
    lower_copy.start()
    upper.collect(0)
    upper_copy = pltpu.make_async_copy(upper.out, upper_hbm, lsem.at[3])
    upper_copy.start()
    low_second.collect(1)
    low_second.spread(0)
    low_second.collect(0)
    tail_copy = pltpu.make_async_copy(low_second.out, tail_hbm, lsem.at[5])
    tail_copy.start()
    two_copy.wait()
    fresh_copy.wait()
    upper_copy.wait()
    lower_copy.wait()
    tail_copy.wait()


def train(z, *args):
    b, f, i = BF16, F32, jnp.int32
    vmem = pltpu.VMEM
    n, rows, tab, hid, halo = z.nodes, z.rows, z.table, z.hid, z.halo
    wide = (z.halves, z.devices, z.blk, LANES)
    bulk = (z.devices, z.blk, hid)
    thin = (z.devices, z.cblk, LANES)

    def hub_buffers(count, more):
        width = count * LANES
        return [vmem((size, z.part + more, width), f) for size in (z.dom, z.dom, z.sub, z.dom)]

    def flat_buffers(total, levels):
        landed, parts, rest = [], [], total
        for size in levels:
            rest = rest // size
            landed.append(vmem((size, rest, LANES), f))
            parts.append(vmem((rest, LANES), f))
        return [vmem((total, LANES), f), vmem((total, LANES), f), *landed, *parts[:-1]]

    def pairs(count, *shape):
        return [vmem(shape, b) for _ in range(2 * count)]

    scratch = [
        vmem((rows, tab), b), vmem((tab, rows), b), vmem((halo, n), b), vmem((n, halo), b), vmem((LANES, LANES), i),
        vmem((LANES, rows), i), vmem((rows, LANES), i),
        *pairs(1, rows, z.fpad), *pairs(1, z.fpad, rows), *pairs(1, z.fpad, 2 * hid), *pairs(1, 2 * hid, hid),
        vmem((LANES, 2 * hid), f), *pairs(1, 2 * hid, LANES),
        vmem((z.halves, tab, 2 * LANES), b), vmem((tab, 2 * LANES), b), vmem((rows, 1), f), vmem((rows, hid), f),
        vmem((rows, hid), f),
        *pairs(3, rows, hid),
        vmem((rows, hid), f), vmem((rows, hid), f),
        *pairs(2, rows, hid),
        vmem((z.halves, rows, 2 * LANES), b), vmem((n, hid), f), vmem((hid, 2 * LANES), f),
        vmem((2, halo, hid), f),
        vmem((halo, LANES), f), vmem((n, LANES), f), vmem((n, 1), i), vmem((n, 1), f), vmem((8, hid), f),
        *[vmem(shape, f) for shape in (wide, wide, wide, wide, thin, thin, thin, thin, wide, wide, bulk, bulk)],
    ]
    for index, count in enumerate(HUB_SUMS):
        scratch += hub_buffers(count, {0: 8, 4: z.class_part - z.part}.get(index, 0))
    for total, levels in zip(z.flat, z.levels):
        scratch += flat_buffers(total, levels)
    dma = pltpu.SemaphoreType.DMA
    scratch += [
        dma((11,)), dma((11,)), dma((len(HUB_SUMS), 3)), dma((len(HUB_SUMS), 3)), dma((len(z.flat), 8)), dma((len(z.flat), 8)), dma((4 + z.halves,))
    ]
    inside = pl.BlockSpec(memory_space=pltpu.VMEM)
    outside = pl.BlockSpec(memory_space=pl.ANY)
    return pl.pallas_call(
        functools.partial(train_kernel, z),
        out_shape=(
            *[jax.ShapeDtypeStruct((total, LANES), f) for total in z.flat],
            jax.ShapeDtypeStruct((2, halo, hid), f),
            jax.ShapeDtypeStruct((8, LANES), f),
        ),
        in_specs=[inside] * 11 + [outside] + [inside] * 4,
        out_specs=(outside, outside, outside, outside, outside, inside),
        scratch_shapes=scratch,
        compiler_params=pltpu.CompilerParams(
            collective_id=0, has_side_effects=True, vmem_limit_bytes=62 * 1024 * 1024
        ),
        name="train",
    )(*args)


def update_kernel(
    z,
    two_hbm, upper_hbm, low_a_hbm, low_b_hbm, fresh_hbm, w1_hbm, m1_hbm, v1_hbm, w2_hbm, m2_hbm, v2_hbm,
    misc, w3, m3, v3, bs, mb, vb,
    o1, n1, s1, c1, o2, n2, s2, c2, o_fresh,
    o_norm, o_loss, o_count, o3, n3, s3, c3, ob, nb, sb, cb,
    two, upper, low_a, low_b, held, w1, m1, v1, w2, m2, v2, d1, d2, in_sem, out_sem,
):
    inward = [
        pltpu.make_async_copy(src, dst, in_sem.at[i])
        for i, (src, dst) in enumerate(
            (
                (two_hbm, two), (upper_hbm, upper), (low_a_hbm, low_a), (low_b_hbm, low_b),
                (w1_hbm, w1), (m1_hbm, m1), (v1_hbm, v1), (w2_hbm, w2), (m2_hbm, m2), (v2_hbm, v2), (fresh_hbm, held),
            )
        )
    ]
    for copy in inward:
        copy.start()
    outward = []

    def leave(src, dst, rows=None):
        if rows is not None:
            src, dst = src.at[rows], dst.at[rows]
        outward.append(pltpu.make_async_copy(src, dst, out_sem.at[len(outward)]))
        outward[-1].start()

    def squares(values):
        return jnp.sum(jnp.sum(values * values, axis=0, keepdims=True), axis=1, keepdims=True)

    at_loss = z.at_bias + 2 * z.halves + 1
    for copy in inward[:4]:
        copy.wait()
    norm = jnp.sqrt(
        squares(two[...]) + squares(upper[0:at_loss, :]) + squares(low_a[...]) + squares(low_b[...])
    )
    o_norm[...] = norm
    o_loss[...] = upper[at_loss : at_loss + 1, 0:1]
    o_count[...] = misc[z.count_rows : z.count_rows + 1, 0:1]
    factor = jnp.minimum(1.0, CLIP / (norm + 1e-06))

    def step(grad, old, first, second):
        clipped = grad * factor
        moment = 0.5 * first + 0.5 * clipped
        squared = 0.5 * second + 0.5 * clipped * clipped
        below = jnp.sqrt(squared * (1.0 / CORRECT)) + EPSILON
        fresh = old * (1.0 - RATE * DECAY) - (moment * (RATE / CORRECT)) / below
        return fresh, moment, squared

    def renew(rows, lanes, grad, w, m, v):
        w[rows, lanes], m[rows, lanes], v[rows, lanes] = step(grad, w[rows, lanes], m[rows, lanes], v[rows, lanes])

    def lane_half(half):
        return slice(half * LANES, (half + 1) * LANES)

    low = z.fin - z.shift
    lows = (low_a, low_b)
    for copy in inward[4:7]:
        copy.wait()
    for half in range(z.halves):
        u0 = half * z.frows
        renew(slice(0, low), lane_half(half), upper[u0 : u0 + low, :], w1, m1, v1)
    for src, dst in ((w1, o1), (m1, n1), (v1, s1)):
        leave(src, dst, pl.ds(0, low))
    for half in range(z.halves):
        u0, lower, lanes = half * z.frows, lows[half], lane_half(half)
        if z.shift:
            renew(slice(low, low + 8), lanes, upper[u0 + low : u0 + low + 8, :] + lower[0:8, :], w1, m1, v1)
            renew(slice(low + 8, 2 * z.fin), lanes, lower[8 : z.fin + z.shift, :], w1, m1, v1)
        else:
            renew(slice(low, 2 * z.fin), lanes, lower[0 : z.fin, :], w1, m1, v1)
    for src, dst in ((w1, o1), (m1, n1), (v1, s1)):
        leave(src, dst, pl.ds(low, 2 * z.fin - low))
    d1[...] = w1[...].astype(BF16)
    leave(d1, c1)
    for copy in inward[7:10]:
        copy.wait()
    for half in range(z.halves):
        start = half * 2 * z.hid
        renew(slice(0, 2 * z.hid), lane_half(half), two[start : start + 2 * z.hid, :], w2, m2, v2)
    for src, dst in ((w2, o2), (m2, n2), (v2, s2)):
        leave(src, dst)
    d2[...] = w2[...].astype(BF16)
    leave(d2, c2)
    inward[10].wait()
    leave(held, o_fresh)
    packed = two[z.at_three : z.at_three + z.hid, :].T
    for half in range(2):
        grad = packed[half * (LANES // 2) : half * (LANES // 2) + z.cls, :]
        part = slice(half * z.hid, (half + 1) * z.hid)
        fresh, moment, squared = step(grad, w3[:, part], m3[:, part], v3[:, part])
        o3[:, part] = fresh
        n3[:, part] = moment
        s3[:, part] = squared
        c3[:, part] = fresh.astype(BF16)
    size = bs.shape[0]
    line = jnp.concatenate([upper[z.at_bias + k : z.at_bias + k + 1, :] for k in range(2 * z.halves + 1)], axis=1)
    flat = lambda ref: ref[...].reshape(1, size)
    fresh, moment, squared = step(line[:, 0:size], flat(bs), flat(mb), flat(vb))
    ob[...] = fresh.reshape(size)
    nb[...] = moment.reshape(size)
    sb[...] = squared.reshape(size)
    cb[...] = ob[...].astype(BF16)
    for copy in outward:
        copy.wait()


def update(z, *args):
    inside = pl.BlockSpec(memory_space=pltpu.VMEM)
    outside = pl.BlockSpec(memory_space=pl.ANY)
    shape = jax.ShapeDtypeStruct
    one, two, three_t, line = args[5].shape, args[8].shape, args[12].shape, args[15].shape

    def group(size):
        return [shape(size, F32)] * 3 + [shape(size, BF16)]

    shapes = [
        *group(one), *group(two), shape(args[4].shape, F32), *[shape((1, 1), F32)] * 3, *group(three_t), *group(line)
    ]
    return pl.pallas_call(
        functools.partial(update_kernel, z),
        out_shape=tuple(shapes),
        in_specs=[outside] * 11 + [inside] * 7,
        out_specs=tuple([outside] * 9 + [inside] * 11),
        scratch_shapes=[
            *[pltpu.VMEM(a.shape, F32) for a in args[:11]],
            pltpu.VMEM(one, BF16), pltpu.VMEM(two, BF16),
            pltpu.SemaphoreType.DMA((11,)), pltpu.SemaphoreType.DMA((12,)),
        ],
        compiler_params=pltpu.CompilerParams(vmem_limit_bytes=62 * 1024 * 1024),
        name="update",
    )(*args)


def solution(mesh):
    def local(
        features, hub_features, low_lists, low_masks, high_lists, high_masks, hub_lists, hub_masks, send_rows,
        labels, train_mask, stale_rows, weight_one, weight_two, weight_three, biases,
        mean_one, mean_two, mean_three, mean_biases, square_one, square_two, square_three, square_biases,
    ):
        z = Sizes(mesh, features, low_lists, high_lists, hub_lists, send_rows, weight_one, weight_three)
        three_t = weight_three.T
        two, upper, low_first, low_second, renewed, misc = train(
            z, features.T, hub_features.T, low_lists.T, low_masks.T, high_lists.T, high_masks.T,
            hub_lists[0].T, hub_masks[0].T, send_rows[0],
            labels.reshape(-1, LANES), train_mask.reshape(-1, LANES), stale_rows,
            weight_one, weight_two, three_t, biases,
        )
        o1, n1, s1, c1, o2, n2, s2, c2, renewed, norm, loss, count, o3, n3, s3, c3, ob, nb, sb, cb = update(
            z, two, upper, low_first, low_second, renewed, weight_one, mean_one, square_one,
            weight_two, mean_two, square_two, misc, three_t, mean_three.T, square_three.T,
            biases, mean_biases, square_biases,
        )
        return (
            norm[0, 0], loss[0, 0], count[0, 0],
            o1, o2, o3.T, ob, n1, n2, n3.T, nb, s1, s2, s3.T, sb, c1, c2, c3.T, cb, renewed,
        )

    spread = ("dom", "sub")
    rows, all_same, cube = P(spread, None), P(), P(spread, None, None)
    stale = P(None, spread, None)
    in_specs = (
        rows, all_same, rows, rows, rows, rows, cube, cube, cube, P(spread), P(spread), stale, *[all_same] * 12
    )
    out_specs = (*[all_same] * 19, stale)
    return jax.shard_map(local, mesh=mesh, in_specs=in_specs, out_specs=out_specs, check_vma=False)
```

```python
import functools

import jax
import jax.numpy as jnp
from jax import lax
from jax.experimental import pallas as pl
from jax.experimental.pallas import tpu as pltpu
from jax.sharding import PartitionSpec as P

MESH = pl.DeviceIdType.MESH
F32 = jnp.float32
BF16 = jnp.bfloat16

STEP = 5
KEEP = 0.95
SMOOTH = 0.1
CLIP = 0.02
RATE = 0.03
DECAY = 0.01
EPSILON = 1e-08
CORRECT = 1.0 - 0.5**STEP
GELU_A = 0.7978845608
GELU_B = 0.044715
LANES = 128
LIMIT = 4


def up(value, unit):
    return -(-value // unit) * unit


def split(values):
    high = values.astype(BF16)
    return high, (values - high.astype(F32)).astype(BF16)


def dot(left, right):
    return jnp.dot(left, right, preferred_element_type=F32)


def dot_nt(left, right):
    return lax.dot_general(left, right, (((1,), (1,)), ((), ())), preferred_element_type=F32)


def dot_tn(left, right):
    return lax.dot_general(left, right, (((0,), (0,)), ((), ())), preferred_element_type=F32)


def three(product, left, right):
    return (
        product(left[0], right[1]) + product(left[1], right[0])
    ) + product(left[0], right[0])


def gelu(v):
    return 0.5 * v * (1.0 + jnp.tanh(GELU_A * (v + GELU_B * (v * v * v))))


def gelu_slope(v):
    t = jnp.tanh(GELU_A * (v + GELU_B * (v * v * v)))
    return 0.5 * (1.0 + t) + (0.5 * GELU_A) * v * (1.0 - t * t) * (1.0 + (3.0 * GELU_B) * (v * v))


def tiles(total, step, body):
    if total // step <= LIMIT:
        for index in range(total // step):
            body(index * step)
        return

    @pl.loop(0, total // step)
    def _(index):
        body(pl.multiple_of(index * step, step))


class Sizes:
    def __init__(self, mesh, features, low_lists, high_lists, hub_lists, send_rows, weight_one, weight_three):
        self.dom, self.sub = mesh.shape["dom"], mesh.shape["sub"]
        self.devices = self.dom * self.sub
        self.nodes, self.fin = features.shape
        self.low, self.k_low = low_lists.shape
        self.high, self.k_high = high_lists.shape
        self.hubs, self.k_hub = hub_lists.shape[1:]
        self.blk = send_rows.shape[2]
        self.halo = self.devices * self.blk
        self.hid = weight_one.shape[1]
        self.halves = self.hid // LANES
        self.cls = weight_three.shape[1]
        self.rows = self.nodes + self.hubs
        self.table = self.nodes + self.halo + self.hubs
        self.fpad = up(self.fin, LANES)
        self.frows = up(self.fin, 8)
        self.shift = self.fin % 8
        self.brows = up(self.fin + self.shift, 8)
        self.part = self.hubs // self.dom
        self.count_rows = self.hubs // LANES
        self.paired = self.part % 16 == 0
        self.class_part = self.part // 2 if self.paired else self.part
        self.packed = self.blk % 16 == 0
        self.cblk = self.blk // 2 if self.packed else self.blk
        unit = 8 * self.devices
        self.at_three = self.halves * 2 * self.hid
        self.at_bias = self.halves * self.frows
        self.flat = (
            up(self.at_three + self.hid, unit),
            up(self.at_bias + 8, unit),
            *[up(self.brows, unit)] * self.halves,
        )
        three, four = (2, self.dom // 2, self.sub), (2, self.dom // 2, 2, self.sub // 2)
        self.levels = (four, four, *[three] * self.halves)


class HubSum:
    def __init__(self, z, place, remote, buffers, sems, index):
        self.z, self.place, self.remote = z, place, remote
        self.source, self.ra, self.rb, self.out = buffers
        self.sent, self.got = sems
        self.index = index

    def put(self, values):
        self.source[...] = values.reshape(self.source.shape)

    def sems(self, phase):
        return self.sent.at[self.index, phase], self.got.at[self.index, phase]

    def over_dom(self, start, phase):
        d, s = self.place

        @pl.loop(1, self.z.dom)
        def _(k):
            pd = lax.rem(d + k, self.z.dom)
            src, dst = start(pd)
            self.remote(src, dst, *self.sems(phase), pd, s).start()

    def dom_done(self, ref, phase):
        d, s = self.place
        some = ref.at[pl.ds(0, self.z.dom - 1)]
        copy = self.remote(some, some, *self.sems(phase), lax.rem(d + 1, self.z.dom), s)
        copy.wait_recv()
        copy.wait_send()

    def scatter(self):
        d, s = self.place
        self.over_dom(lambda pd: (self.source.at[pd], self.ra.at[d]), 0)

    def swap(self):
        d, s = self.place
        self.dom_done(self.ra, 0)
        total = self.source[d]
        for k in range(1, self.z.dom):
            total = total + self.ra[lax.rem(d + k, self.z.dom)]
        self.rb[s] = total

        @pl.loop(1, self.z.sub)
        def _(k):
            ps = lax.rem(s + k, self.z.sub)
            self.remote(self.rb.at[s], self.rb.at[s], *self.sems(1), d, ps).start()

    def gather(self):
        d, s = self.place
        some = self.rb.at[pl.ds(0, self.z.sub - 1)]
        copy = self.remote(some, some, *self.sems(1), d, lax.rem(s + 1, self.z.sub))
        copy.wait_recv()
        copy.wait_send()
        total = self.rb[0]
        for k in range(1, self.z.sub):
            total = total + self.rb[k]
        self.out[d] = total
        self.over_dom(lambda pd: (self.out.at[d], self.out.at[d]), 2)

    def finish(self):
        self.dom_done(self.out, 2)

    def end(self):
        self.finish()
        return self.out[:, 0 : self.z.part, :].reshape(self.z.hubs, self.out.shape[-1])


class FlatSum:
    def __init__(self, z, place, remote, buffers, sems, index):
        d, s = place
        self.remote, self.index = remote, index
        self.source, self.out = buffers[0], buffers[1]
        depth = len(z.levels[index])
        self.landed, self.parts = buffers[2 : 2 + depth], (buffers[0], *buffers[2 + depth :])
        self.sent, self.got = sems
        pair = lax.rem(d, 2)
        chip = d // 2
        self.levels = (
            (2, pair, lambda j: (chip * 2 + j, s)),
            (z.dom // 2, chip, lambda j: (j * 2 + pair, s)),
            (z.sub, s, lambda j: (d, j)),
        )
        if depth == 4:
            near, far = lax.rem(s, 2), s // 2
            self.levels = (
                *self.levels[:2],
                (2, near, lambda j: (d, far * 2 + j)),
                (z.sub // 2, far, lambda j: (d, j * 2 + near)),
            )
        self.first, offset, rows = [], 0, self.source.shape[0]
        for size, mine, _ in self.levels:
            rows = rows // size
            self.first.append((offset, rows))
            offset = offset + mine * rows

    def sems(self, phase):
        return self.sent.at[self.index, phase], self.got.at[self.index, phase]

    def rows(self, start, count):
        return pl.ds(pl.multiple_of(start, 8), count)

    def send(self, level):
        size, mine, peer = self.levels[level]
        count = self.first[level][1]

        @pl.loop(1, size)
        def _(k):
            j = lax.rem(mine + k, size)
            self.remote(
                self.parts[level].at[self.rows(j * count, count)],
                self.landed[level].at[mine],
                *self.sems(level),
                *peer(j),
            ).start()

    def receive(self, level):
        size, mine, peer = self.levels[level]
        offset, count = self.first[level]
        ref = self.landed[level]
        some = ref.at[pl.ds(0, size - 1)]
        copy = self.remote(some, some, *self.sems(level), *peer(lax.rem(mine + 1, size)))
        copy.wait_recv()
        copy.wait_send()
        total = self.parts[level][self.rows(mine * count, count), :]
        for k in range(1, size):
            total = total + ref[lax.rem(mine + k, size)]
        if level + 1 < len(self.levels):
            self.parts[level + 1][...] = total
        else:
            self.out[self.rows(offset + mine * count, count), :] = total

    def spread(self, level):
        size, mine, peer = self.levels[level]
        offset, count = self.first[level]
        held = self.out.at[self.rows(offset + mine * count, count)]

        @pl.loop(1, size)
        def _(k):
            j = lax.rem(mine + k, size)
            self.remote(held, held, *self.sems(4 + level), *peer(j)).start()

    def collect(self, level):
        size, mine, peer = self.levels[level]
        some = self.out.at[pl.ds(0, (size - 1) * self.first[level][1])]
        copy = self.remote(some, some, *self.sems(4 + level), *peer(lax.rem(mine + 1, size)))
        copy.wait_recv()
        copy.wait_send()


HUB_SUMS = (1, 1, 1, 1, 1, 2)


def train_kernel(
    z,
    feat, hubf, lowl, lowm, highl, highm, hubl, hubm, send, lab, tmask, stale_hbm, w1, w2, w3, bias,
    two_hbm, upper_hbm, lower_hbm, tail_hbm, fresh_hbm, misc,
    ab, abt, sel, selt, colb, keyt, keys, xh, xl, xth, xtl, w1h, w1l, w2h, w2l, w3t, w3h, w3l,
    tb, tc, inv, q, magg, h1h, h1l, m1h, m1l, h2h, h2l, dg0, dg1, dph, dpl, dmh, dml, eb, gown, gthree, stale,
    zst, pself, labc, trainw, brow,
    send_a, recv_a, send_b, recv_b, send_c, recv_c, send_d, recv_d, recv_e, recv_f, send_g, recv_g,
    *rest_refs,
):
    hub_refs, flat_refs = rest_refs[: 4 * len(HUB_SUMS)], rest_refs[4 * len(HUB_SUMS) : -7]
    xs, xr, hsem_s, hsem_r, gsem_s, gsem_r, lsem = rest_refs[-7:]
    send_e, send_f = send_a, send_b
    d = lax.axis_index("dom")
    s = lax.axis_index("sub")
    me = d * z.sub + s
    nd, halo, hubs, hid, fin = z.nodes, z.halo, z.hubs, z.hid, z.fin
    halo0, hub0 = nd, nd + halo
    own, halos, hubr = slice(0, nd), slice(halo0, hub0), slice(hub0, z.table)
    hubq = slice(nd, z.rows)
    up_rows, low_rows = slice(0, hid), slice(hid, 2 * hid)
    i32 = jnp.int32
    both = range(z.halves)

    def lanes(h):
        return slice(h * LANES, (h + 1) * LANES)

    barrier = pltpu.get_barrier_semaphore()

    @pl.loop(1, z.devices)
    def _(k):
        pl.semaphore_signal(
            barrier,
            inc=1,
            device_id=(lax.rem(d + k // z.sub, z.dom), lax.rem(s + k % z.sub, z.sub)),
            device_id_type=MESH,
        )

    stale_copy = pltpu.make_async_copy(stale_hbm, stale, lsem.at[0])
    stale_copy.start()

    def remote(src, dst, ssem, rsem, pd, ps):
        return pltpu.make_async_remote_copy(
            src_ref=src, dst_ref=dst, send_sem=ssem, recv_sem=rsem, device_id=(pd, ps), device_id_type=MESH
        )

    place = (d, s)
    sums = [
        HubSum(z, place, remote, hub_refs[4 * i : 4 * i + 4], (hsem_s, hsem_r), i) for i in range(len(HUB_SUMS))
    ]
    grads, start = [], 0
    for i in range(len(z.flat)):
        refs = flat_refs[start : start + 1 + 2 * len(z.levels[i])]
        grads.append(FlatSum(z, place, remote, refs, (gsem_s, gsem_r), i))
        start += len(refs)
    two, upper, *lowers = grads

    def part_of(portion):
        return 1 + (z.devices - 1) * portion // 8

    def exchange_start(src, dst, i, first=0, last=8):
        @pl.loop(part_of(first), part_of(last))
        def _(k):
            mixed = lax.rem(k * 5, z.devices)
            pd = lax.rem(d + mixed // z.sub, z.dom)
            ps = lax.rem(s + mixed % z.sub, z.sub)
            remote(src.at[pd * z.sub + ps], dst.at[me], xs.at[i], xr.at[i], pd, ps).start()

        if first == 0:
            dst[me] = src[me]

    def exchange_wait(src, dst, i):
        some = pl.ds(0, z.devices - 1)
        copy = remote(src.at[some], dst.at[some], xs.at[i], xr.at[i], lax.rem(d + 1, z.dom), s)
        copy.wait_recv()
        copy.wait_send()

    def put_split(ref, rows, values):
        width = values.shape[1]
        high, rest = split(values)
        ref[rows, 0:width] = high
        ref[rows, width : 2 * width] = rest

    def put_pair(high_ref, rest_ref, rows, columns, values):
        high, rest = split(values)
        high_ref[rows, columns] = high
        rest_ref[rows, columns] = rest
        return high, rest

    def added(product):
        return product[:, :LANES] + product[:, LANES:]

    per_tile = 256 // z.blk

    def turn(source, target, r_count, c_count, c_start=0, step=128):
        def body(r):
            for c in range(c_start, c_count, step):
                target[c : c + step, pl.ds(r, step)] = source[pl.ds(r, step), c : c + step].T

        tiles(r_count, step, body)

    pad0 = fin // 16 * 16
    xth[pad0 : z.fpad, :] = jnp.zeros((z.fpad - pad0, z.rows), BF16)
    xtl[pad0 : z.fpad, :] = jnp.zeros((z.fpad - pad0, z.rows), BF16)
    w1h[pad0 : z.fpad, :] = jnp.zeros((z.fpad - pad0, 2 * hid), BF16)
    w1l[pad0 : z.fpad, :] = jnp.zeros((z.fpad - pad0, 2 * hid), BF16)
    put_pair(xth, xtl, slice(0, fin), own, feat[...])
    turn(xth, xh, z.fpad, nd)
    turn(xtl, xl, z.fpad, nd)
    put_pair(w1h, w1l, slice(0, fin), low_rows, w1[fin : 2 * fin, :])

    def project(rows, columns):
        return three(dot, (xh[rows, :], xl[rows, :]), (w1h[:, columns], w1l[:, columns]))

    def put_halves(rows, values):
        for h in both:
            put_split(tb.at[h], rows, values[:, lanes(h)])

    tiles(nd, 256, lambda r: put_halves(pl.ds(r, 256), project(pl.ds(r, 256), low_rows)))

    colb[0 : z.devices, 0 : z.blk] = send[...]
    turned = colb[...].T

    for tile in range(halo // 256):
        first = tile * per_tile
        column = jnp.concatenate([turned[0 : z.blk, p : p + 1] for p in range(first, first + per_tile)], axis=0)
        hit = column == lax.broadcasted_iota(i32, (256, nd), 1)
        sel[tile * 256 : tile * 256 + 256, :] = jnp.where(hit, 1.0, 0.0).astype(BF16)

    def pick(source, target):
        def body(r):
            values = added(dot(sel[pl.ds(r, 256), :], source[own, :]))
            target[pl.ds(r // z.blk, per_tile)] = values.reshape(per_tile, z.blk, LANES)

        tiles(halo, 256, body)

    pick(tb.at[0], send_a.at[0])
    pl.semaphore_wait(barrier, z.devices - 1)
    for h in both:
        if h:
            pick(tb.at[h], send_a.at[h])
        exchange_start(send_a.at[h], recv_a.at[h], h)

    keyt[...] = jnp.full(keyt.shape, -1, i32)
    keyt[0 : z.k_low, 0 : z.low] = jnp.where(lowm[...] > 0, lowl[...], -1)
    keyt[0 : z.k_high, z.low : nd] = jnp.where(highm[...] > 0, highl[...], -1)
    keyt[0 : z.k_hub, hubq] = jnp.where(hubm[...] > 0, hubl[...], -1)
    for block in range(z.rows // LANES):
        keys[lanes(block), :] = keyt[:, lanes(block)].T
    counts = jnp.sum(jnp.where(keys[...] >= 0, 1.0, 0.0), axis=1, keepdims=True)
    inv[own, :] = 1.0 / jnp.maximum(counts[own, :], 1.0)
    train_local = jnp.sum(jnp.sum(tmask[...].astype(F32), axis=1, keepdims=True), axis=0, keepdims=True)
    used_slots = jnp.sum(jnp.where(keyt[0 : z.k_hub, hubq] >= 0, 1.0, 0.0), axis=0, keepdims=True)
    extra = [used_slots[:, lanes(c)] for c in range(z.count_rows)] + [jnp.broadcast_to(train_local, (1, LANES))]
    extra.append(jnp.zeros((8 - len(extra), LANES), F32))
    extra = jnp.concatenate(extra, axis=0)
    for block in range(z.dom):
        sums[0].source[block, z.part : z.part + 8, :] = extra

    def build(first, count, slots):
        def group(r):
            rows = pl.ds(first + r, 16)
            key = keys[rows, :].astype(jnp.int16)
            spot = lax.broadcasted_iota(i32, (16, z.table), 1).astype(jnp.int16)
            one, none = jnp.ones((16, z.table), BF16), jnp.zeros((16, z.table), BF16)
            total = none
            for k in range(slots):
                total = total + jnp.where(jnp.broadcast_to(key[:, k : k + 1], (16, z.table)) == spot, one, none)
            ab[rows, :] = total

        tiles(count, 16, group)

    build(0, z.low, z.k_low)
    build(nd, hubs, z.k_hub)
    build(z.low, z.high, z.k_high)

    put_pair(xth, xtl, slice(0, fin), hubq, hubf[...])
    turn(xth, xh, z.fpad, z.rows, nd)
    turn(xtl, xl, z.fpad, z.rows, nd)
    put_pair(w1h, w1l, slice(0, fin), up_rows, w1[0:fin, :])
    brow[...] = jnp.zeros(brow.shape, F32)
    line = bias[...].reshape(1, 2 * hid + z.cls)
    brow[0:1, :] = line[:, 0:hid]
    brow[1:2, :] = line[:, hid : 2 * hid]
    brow[2:3, 0 : z.cls] = line[:, 2 * hid : 2 * hid + z.cls]
    put_halves(hubr, project(hubq, low_rows))

    def own_tile(r):
        rows = pl.ds(r, 256)
        q[rows, :] = project(rows, up_rows) + brow[0:1, :]

    tiles(nd, 256, own_tile)

    def gather_local(h):
        def body(r):
            rows = pl.ds(r, 256)
            magg[rows, lanes(h)] = added(dot(ab[rows, own], tb[h, own, :]) + dot(ab[rows, hubr], tb[h, hubr, :]))

        tiles(z.rows, 256, body)

    gather_local(0)

    def with_halo(rows, h):
        return magg[rows, lanes(h)] + added(dot(ab[rows, halos], tb[h, halos, :]))

    def layer_one(h):
        def body(r):
            rows = pl.ds(r, 256)
            pre = q[rows, lanes(h)] + with_halo(rows, h) * inv[rows, :]
            q[rows, lanes(h)] = pre
            high, rest = put_pair(h1h, h1l, rows, lanes(h), gelu(pre))
            tb[h, rows, 0:LANES] = high
            tb[h, rows, LANES : 2 * LANES] = rest

        tiles(nd, 256, body)

    exchange_wait(send_a.at[0], recv_a.at[0], 0)
    put_split(tb.at[0], halos, recv_a[0].reshape(halo, LANES))
    sums[0].source[:, 0 : z.part, :] = with_halo(hubq, 0).reshape(z.dom, z.part, LANES)
    sums[0].scatter()
    layer_one(0)
    pick(tb.at[0], send_b.at[0])
    exchange_start(send_b.at[0], recv_b.at[0], 2, 0, 4)
    gather_local(1)
    own_tile(nd)
    turn(sel, selt, halo, nd)
    exchange_wait(send_a.at[1], recv_a.at[1], 1)
    put_split(tb.at[1], halos, recv_a[1].reshape(halo, LANES))
    sums[1].put(with_halo(hubq, 1))
    sums[1].scatter()
    exchange_start(send_b.at[0], recv_b.at[0], 2, 4, 8)
    layer_one(1)
    pick(tb.at[1], send_b.at[1])
    sums[0].swap()
    sums[1].swap()
    exchange_start(send_b.at[1], recv_b.at[1], 3, 0, 6)
    put_pair(w2h, w2l, slice(0, 2 * hid), slice(0, hid), w2[...])
    w3t[...] = jnp.zeros(w3t.shape, F32)
    w3t[0 : z.cls, :] = w3[...]
    put_pair(w3h, w3l, slice(0, 2 * hid), slice(0, LANES), w3t[...].T)
    turn(ab, abt, z.rows, z.table)
    sums[0].gather()
    sums[1].gather()
    exchange_start(send_b.at[1], recv_b.at[1], 3, 6, 8)
    for grad in grads:
        grad.source[...] = jnp.zeros(grad.source.shape, F32)

    stale_copy.wait()
    zst[...] = three(dot, split(KEEP * stale[1]), (w3h[low_rows, :], w3l[low_rows, :]))
    dg0[own, :] = gelu_slope(q[own, :])
    for block in range(nd // LANES):
        diag = lax.broadcasted_iota(i32, (LANES, LANES), 0) == lax.broadcasted_iota(i32, (LANES, LANES), 1)
        line = jnp.broadcast_to(lab[block : block + 1, :], (LANES, LANES))
        labc[lanes(block), :] = jnp.sum(jnp.where(diag, line, 0), axis=1, keepdims=True)
        line = jnp.broadcast_to(tmask[block : block + 1, :].astype(F32), (LANES, LANES))
        trainw[lanes(block), :] = jnp.sum(jnp.where(diag, line, 0.0), axis=1, keepdims=True)
    first_hub = sums[0].end()
    misc[...] = sums[0].out[0, z.part : z.part + 8, :]
    colb[0:8, :] = misc[...].astype(i32)
    turned_counts = colb[...].T
    for c in range(z.count_rows):
        inv[nd + c * LANES : nd + (c + 1) * LANES, :] = 1.0 / turned_counts[:, c : c + 1].astype(F32)
    hub_ends = (first_hub, sums[1].end())
    for h in both:
        pre = q[hubq, lanes(h)] + hub_ends[h] * inv[hubq, :]
        dg0[hubq, lanes(h)] = gelu_slope(pre)
        high, rest = put_pair(h1h, h1l, hubq, lanes(h), gelu(pre))
        tb[h, hubr, 0:LANES] = high
        tb[h, hubr, LANES : 2 * LANES] = rest

    for h in both:
        gather_local(h)

    def own_two(r):
        rows = pl.ds(r, 256)
        q[rows, :] = three(dot, (h1h[rows, :], h1l[rows, :]), (w2h[up_rows, :], w2l[up_rows, :])) + brow[1:2, :]

    tiles(z.rows, 256, own_two)

    def second(h):
        exchange_wait(send_b.at[h], recv_b.at[h], 2 + h)
        renewed = KEEP * stale[0, :, lanes(h)] + (1.0 - KEEP) * recv_b[h].reshape(halo, LANES)
        stale[0, :, lanes(h)] = renewed
        put_split(tb.at[h], halos, renewed)
        sums[2 + h].put(with_halo(hubq, h))
        sums[2 + h].scatter()

        def body(r):
            rows = pl.ds(r, 256)
            put_pair(m1h, m1l, rows, lanes(h), with_halo(rows, h) * inv[rows, :])

        tiles(nd, 256, body)

    second(0)
    second(1)
    sums[2].swap()

    def layer_two(r):
        rows = pl.ds(r, 256)
        pre = q[rows, :] + three(dot, (m1h[rows, :], m1l[rows, :]), (w2h[low_rows, :], w2l[low_rows, :]))
        q[rows, :] = pre
        high, rest = put_pair(h2h, h2l, rows, slice(0, hid), gelu(pre))
        put_split(tc, rows, three(dot, (high, rest), (w3h[low_rows, :], w3l[low_rows, :])))

    tiles(nd, 256, layer_two)
    class_lane = lax.broadcasted_iota(i32, (1, 1, LANES), 2) < LANES // 2

    def pack(values):
        blocks = values.reshape(values.shape[0] // z.blk, z.blk, LANES)
        if z.packed:
            return blocks[:, : z.cblk] + pltpu.roll(blocks[:, z.cblk :], LANES // 2, 2)
        return blocks

    def unpack(blocks):
        if z.packed:
            first = jnp.where(class_lane, blocks, 0.0)
            second = jnp.where(class_lane, pltpu.roll(blocks, LANES // 2, 2), 0.0)
            blocks = jnp.concatenate([first, second], axis=1)
        return blocks.reshape(halo, LANES)

    def pick_class(r):
        send_c[pl.ds(r // z.blk, per_tile)] = pack(added(dot(sel[pl.ds(r, 256), :], tc[own, :])))

    tiles(halo, 256, pick_class)
    sums[3].swap()
    sums[2].gather()
    exchange_start(send_c, recv_c, 4)

    def pick_wide(r):
        chosen = sel[pl.ds(r, 256), :]
        values = dot(chosen, h2l[own, :]) + dot(chosen, h2h[own, :])
        send_g[pl.ds(r // z.blk, per_tile)] = values.reshape(per_tile, z.blk, hid)


    def own_three(r):
        rows = pl.ds(r, 256)
        pself[rows, :] = three(dot, (h2h[rows, :], h2l[rows, :]), (w3h[up_rows, :], w3l[up_rows, :])) + brow[2:3, 0:LANES]

    tiles(nd, 256, own_three)

    def class_local(r):
        rows = pl.ds(r, 256)
        magg[rows, 0:LANES] = added(dot(ab[rows, own], tc[own, :]))

    tiles(nd, 256, class_local)
    sums[3].gather()
    tiles(halo, 256, pick_wide)
    exchange_start(send_g, recv_g, 5, 0, 3)
    dg1[own, :] = gelu_slope(q[own, :])
    for h in both:
        put_pair(m1h, m1l, hubq, lanes(h), sums[2 + h].end() * inv[hubq, :])
    pre = q[hubq, :] + three(dot, (m1h[hubq, :], m1l[hubq, :]), (w2h[low_rows, :], w2l[low_rows, :]))
    high, rest = put_pair(h2h, h2l, hubq, slice(0, hid), gelu(pre))
    put_split(tc, hubr, three(dot, (high, rest), (w3h[low_rows, :], w3l[low_rows, :])))
    q[hubq, :] = pre

    exchange_wait(send_c, recv_c, 4)
    put_split(tc, halos, zst[...] + (1.0 - KEEP) * unpack(recv_c[...]))
    used = lax.broadcasted_iota(i32, (256, LANES), 1)
    train_total = misc[z.count_rows : z.count_rows + 1, 0:1]
    at_bias = z.at_bias

    def head(r):
        rows = pl.ds(r, 256)
        logits = pself[rows, :] + (magg[rows, 0:LANES] + added(dot(ab[rows, halo0:], tc[halo0:, :]))) * inv[rows, :]
        valid = used < z.cls
        top = jnp.max(jnp.where(valid, logits, -1e30), axis=1, keepdims=True)
        shifted = logits - top
        powers = jnp.where(valid, jnp.exp(jnp.where(valid, shifted, 0.0)), 0.0)
        total = jnp.sum(powers, axis=1, keepdims=True)
        log_probs = jnp.where(valid, shifted - jnp.log(total), 0.0)
        target = jnp.where(used == labc[rows, :], 1.0 - SMOOTH, 0.0) + SMOOTH / z.cls
        weight = trainw[rows, :]
        losses = jnp.sum(jnp.where(valid, -target * log_probs, 0.0), axis=1, keepdims=True) * weight
        grad = jnp.where(valid, powers / total - target, 0.0) * weight / train_total
        at = at_bias + 2 * z.halves
        upper.source[at : at + 1, :] = upper.source[at : at + 1, :] + jnp.sum(grad, axis=0, keepdims=True)
        at = at + 1
        upper.source[at : at + 1, :] = upper.source[at : at + 1, :] + jnp.sum(losses, axis=0, keepdims=True)
        put_pair(dph, dpl, rows, slice(0, LANES), grad)
        put_split(eb.at[0], rows, grad * inv[rows, :])

    tiles(nd, 256, head)


    def pack_hubs(values):
        blocks = values.reshape(z.dom, z.part, LANES)
        if z.paired:
            return blocks[:, : z.class_part] + pltpu.roll(blocks[:, z.class_part :], LANES // 2, 2)
        return blocks

    def unpack_hubs(blocks):
        if z.paired:
            first = jnp.where(class_lane, blocks, 0.0)
            second = jnp.where(class_lane, pltpu.roll(blocks, LANES // 2, 2), 0.0)
            blocks = jnp.concatenate([first, second], axis=1)
        return blocks.reshape(hubs, LANES)

    sums[4].put(pack_hubs(added(dot(abt[hubr, own], eb[0, own, :]))))
    sums[4].scatter()

    def back_class(r):
        values = added(dot(abt[pl.ds(halo0 + r, 256), own], eb[0, own, :]))
        put_split(tc, pl.ds(halo0 + r, 256), values)
        send_d[pl.ds(r // z.blk, per_tile)] = pack((1.0 - KEEP) * values)

    tiles(halo, 256, back_class)
    sums[4].swap()
    exchange_start(send_d, recv_d, 6)
    gown[own, 0:LANES] = added(dot(abt[own, own], eb[0, own, :]))

    gthree[:, 0:LANES] = three(dot_tn, split(KEEP * stale[1]), (tc[halos, 0:LANES], tc[halos, LANES : 2 * LANES]))
    sums[4].gather()
    exchange_start(send_g, recv_g, 5, 3, 6)
    hub_class = split(unpack_hubs(sums[4].source[...]))
    gthree[:, 0:LANES] = gthree[:, 0:LANES] + three(dot_tn, (h2h[hubq, :], h2l[hubq, :]), hub_class)
    gthree[:, LANES : 2 * LANES] = three(dot_tn, (h2h[own, :], h2l[own, :]), (dph[own, 0:LANES], dpl[own, 0:LANES]))
    dg1[hubq, :] = gelu_slope(q[hubq, :])

    def self_two(r):
        rows = pl.ds(r, 256)
        magg[rows, :] = three(
            dot_nt, (dph[rows, 0:LANES], dpl[rows, 0:LANES]), (w3h[up_rows, :], w3l[up_rows, :])
        )

    tiles(nd, 256, self_two)

    def owned(values):
        row = lax.broadcasted_iota(i32, (hubs, 1), 0)
        share = hubs // z.devices
        mine = jnp.where(row >= me * share, 1.0, 0.0) * jnp.where(row < (me + 1) * share, 1.0, 0.0)
        return values * mine

    def column_sums(columns):
        return jnp.sum(dmh[:, columns].astype(F32) + dml[:, columns].astype(F32), axis=0, keepdims=True)

    sums[4].finish()
    node = three(dot_nt, split(unpack_hubs(sums[4].out[...])), (w3h[low_rows, :], w3l[low_rows, :])) * dg1[hubq, :]
    put_pair(dph, dpl, hubq, slice(0, hid), node)
    put_pair(dmh, dml, hubq, slice(0, hid), owned(node))

    def spread(rows):
        values = three(dot_nt, (dph[rows, :], dpl[rows, :]), (w2h[low_rows, :], w2l[low_rows, :])) * inv[rows, :]
        for h in both:
            put_split(eb.at[h], rows, values[:, lanes(h)])

    spread(hubq)
    exchange_wait(send_d, recv_d, 6)
    put_split(tc, halos, unpack(recv_d[...]))

    def back_two(r):
        rows = pl.ds(r, 256)
        own_class = gown[rows, 0:LANES] + added(dot(selt[rows, :], tc[halos, :]))
        gown[rows, 0:LANES] = own_class
        node = (
            three(dot_nt, split(own_class), (w3h[low_rows, :], w3l[low_rows, :])) + magg[rows, :]
        ) * dg1[rows, :]
        high, rest = put_pair(dph, dpl, rows, slice(0, hid), node)
        dmh[rows, :] = high
        dml[rows, :] = rest
        spread(rows)

    tiles(nd, 256, back_two)

    for h in both:
        sums[5].source[:, :, lanes(h)] = added(dot(abt[hubr, :], eb[h])).reshape(z.dom, z.part, LANES)
    sums[5].scatter()

    def send_halo(target, factor, h):
        def body(r):
            values = added(dot(abt[pl.ds(halo0 + r, 256), :], eb[h])) * factor
            target[pl.ds(r // z.blk, per_tile)] = values.reshape(per_tile, z.blk, LANES)

        tiles(halo, 256, body)

    send_halo(send_e.at[0], 1.0 - KEEP, 0)
    exchange_start(send_e.at[0], recv_e.at[0], 7, 0, 4)
    send_halo(send_e.at[1], 1.0 - KEEP, 1)
    sums[5].swap()
    exchange_start(send_e.at[0], recv_e.at[0], 7, 4, 8)

    def own_back(r):
        rows = pl.ds(r, 256)
        q[rows, :] = three(dot_nt, (dph[rows, :], dpl[rows, :]), (w2h[up_rows, :], w2l[up_rows, :]))

    tiles(z.rows, 256, own_back)

    def own_table(r):
        rows = pl.ds(r, 256)
        for h in both:
            q[rows, lanes(h)] = q[rows, lanes(h)] + added(dot(abt[rows, :], eb[h]))

    tiles(nd, 256, own_table)
    gthree[:, 0:LANES] = gthree[:, 0:LANES] + three(dot_tn, (h2h[own, :], h2l[own, :]), split(gown[own, 0:LANES]))
    two.source[z.at_three : z.at_three + hid, :] = gthree[:, LANES : 2 * LANES] + pltpu.roll(
        gthree[:, 0:LANES], LANES // 2, 1
    )
    for h in both:
        start = h * 2 * hid
        pair = (dmh[:, lanes(h)], dml[:, lanes(h)])
        two.source[start : start + hid, :] = three(dot_tn, (h1h[...], h1l[...]), pair)
        two.source[start + hid : start + 2 * hid, :] = three(dot_tn, (m1h[...], m1l[...]), pair)
        at = at_bias + z.halves + h
        upper.source[at : at + 1, :] = column_sums(lanes(h))
    sums[5].gather()
    exchange_start(send_e.at[1], recv_e.at[1], 8, 0, 4)
    node = (sums[5].end() + q[hubq, :]) * dg0[hubq, :]
    put_pair(dmh, dml, hubq, slice(0, hid), owned(node))
    node = node * inv[hubq, :]
    for h in both:
        put_split(eb.at[h], hubq, node[:, lanes(h)])
    two.send(0)
    exchange_start(send_e.at[1], recv_e.at[1], 8, 4, 8)

    def back_one(h):
        exchange_wait(send_e.at[h], recv_e.at[h], 7 + h)
        put_split(tb.at[h], halos, recv_e[h].reshape(halo, LANES))

        def body(r):
            rows = pl.ds(r, 256)
            node = (q[rows, lanes(h)] + added(dot(selt[rows, :], tb[h, halos, :]))) * dg0[rows, lanes(h)]
            put_pair(dmh, dml, rows, lanes(h), node)
            put_split(eb.at[h], rows, node * inv[rows, :])

        tiles(nd, 256, body)
        send_halo(send_f.at[h], 1.0, h)

    back_one(0)
    exchange_start(send_f.at[0], recv_f.at[0], 9, 0, 4)
    two.receive(0)
    two.send(1)
    exchange_start(send_f.at[0], recv_f.at[0], 9, 4, 8)
    back_one(1)
    two.receive(1)
    two.send(2)
    for h in both:
        top = three(dot, (xth[...], xtl[...]), (dmh[:, lanes(h)], dml[:, lanes(h)]))
        upper.source[h * z.frows : (h + 1) * z.frows, :] = top[0 : z.frows, :]
        upper.source[at_bias + h : at_bias + h + 1, :] = column_sums(lanes(h))
    upper.send(0)
    two.receive(2)
    two.send(3)
    exchange_start(send_f.at[1], recv_f.at[1], 10, 0, 4)

    def own_last(r):
        rows = pl.ds(r, 256)
        for h in both:
            gown[rows, lanes(h)] = added(dot(abt[rows, :], eb[h]))

    tiles(nd, 256, own_last)
    for h in both:
        put_pair(dmh, dml, hubq, lanes(h), added(dot(abt[hubr, :], eb[h])))
    upper.receive(0)
    upper.send(1)
    two.receive(3)
    two.spread(3)

    def last(h):
        exchange_wait(send_f.at[h], recv_f.at[h], 9 + h)
        put_split(tb.at[h], halos, recv_f[h].reshape(halo, LANES))

        def body(r):
            rows = pl.ds(r, 256)
            put_pair(dmh, dml, rows, lanes(h), gown[rows, lanes(h)] + added(dot(selt[rows, :], tb[h, halos, :])))

        tiles(nd, 256, body)
        bottom = three(dot, (xth[...], xtl[...]), (dmh[:, lanes(h)], dml[:, lanes(h)]))
        lowers[h].source[z.shift : z.shift + fin, :] = bottom[0:fin, :]

    last(0)
    low_first, low_second = lowers
    low_first.send(0)
    exchange_start(send_f.at[1], recv_f.at[1], 10, 4, 8)
    exchange_start(send_g, recv_g, 5, 6, 8)
    upper.receive(1)
    upper.send(2)
    two.collect(3)
    two.spread(2)
    low_first.receive(0)
    low_first.send(1)
    last(1)
    low_second.send(0)
    upper.receive(2)
    upper.send(3)
    two.collect(2)
    two.spread(1)
    low_first.receive(1)
    low_first.send(2)
    upper.receive(3)
    upper.spread(3)
    low_second.receive(0)
    low_second.send(1)
    two.collect(1)
    two.spread(0)
    two_copy = pltpu.make_async_copy(two.out, two_hbm, lsem.at[1])
    upper.collect(3)
    upper.spread(2)
    low_first.receive(2)
    low_first.spread(2)
    low_second.receive(1)
    low_second.send(2)
    low_first.collect(2)
    low_first.spread(1)
    upper.collect(2)
    upper.spread(1)
    low_second.receive(2)
    low_second.spread(2)
    exchange_wait(send_g, recv_g, 5)
    stale[1] = KEEP * stale[1] + (1.0 - KEEP) * recv_g[...].reshape(halo, hid)
    fresh_copy = pltpu.make_async_copy(stale, fresh_hbm, lsem.at[2])
    fresh_copy.start()
    low_first.collect(1)
    low_first.spread(0)
    low_second.collect(2)
    low_second.spread(1)
    upper.collect(1)
    upper.spread(0)
    two.collect(0)
    two_copy.start()
    low_first.collect(0)
    lower_copy = pltpu.make_async_copy(low_first.out, lower_hbm, lsem.at[4])
    lower_copy.start()
    upper.collect(0)
    upper_copy = pltpu.make_async_copy(upper.out, upper_hbm, lsem.at[3])
    upper_copy.start()
    low_second.collect(1)
    low_second.spread(0)
    low_second.collect(0)
    tail_copy = pltpu.make_async_copy(low_second.out, tail_hbm, lsem.at[5])
    tail_copy.start()
    two_copy.wait()
    fresh_copy.wait()
    upper_copy.wait()
    lower_copy.wait()
    tail_copy.wait()


def train(z, *args):
    b, f, i = BF16, F32, jnp.int32
    vmem = pltpu.VMEM
    n, rows, tab, hid, halo = z.nodes, z.rows, z.table, z.hid, z.halo
    wide = (z.halves, z.devices, z.blk, LANES)
    bulk = (z.devices, z.blk, hid)
    thin = (z.devices, z.cblk, LANES)

    def hub_buffers(count, more):
        width = count * LANES
        return [vmem((size, z.part + more, width), f) for size in (z.dom, z.dom, z.sub, z.dom)]

    def flat_buffers(total, levels):
        landed, parts, rest = [], [], total
        for size in levels:
            rest = rest // size
            landed.append(vmem((size, rest, LANES), f))
            parts.append(vmem((rest, LANES), f))
        return [vmem((total, LANES), f), vmem((total, LANES), f), *landed, *parts[:-1]]

    def pairs(count, *shape):
        return [vmem(shape, b) for _ in range(2 * count)]

    scratch = [
        vmem((rows, tab), b), vmem((tab, rows), b), vmem((halo, n), b), vmem((n, halo), b), vmem((LANES, LANES), i),
        vmem((LANES, rows), i), vmem((rows, LANES), i),
        *pairs(1, rows, z.fpad), *pairs(1, z.fpad, rows), *pairs(1, z.fpad, 2 * hid), *pairs(1, 2 * hid, hid),
        vmem((LANES, 2 * hid), f), *pairs(1, 2 * hid, LANES),
        vmem((z.halves, tab, 2 * LANES), b), vmem((tab, 2 * LANES), b), vmem((rows, 1), f), vmem((rows, hid), f),
        vmem((rows, hid), f),
        *pairs(3, rows, hid),
        vmem((rows, hid), f), vmem((rows, hid), f),
        *pairs(2, rows, hid),
        vmem((z.halves, rows, 2 * LANES), b), vmem((n, hid), f), vmem((hid, 2 * LANES), f),
        vmem((2, halo, hid), f),
        vmem((halo, LANES), f), vmem((n, LANES), f), vmem((n, 1), i), vmem((n, 1), f), vmem((8, hid), f),
        *[vmem(shape, f) for shape in (wide, wide, wide, wide, thin, thin, thin, thin, wide, wide, bulk, bulk)],
    ]
    for index, count in enumerate(HUB_SUMS):
        scratch += hub_buffers(count, {0: 8, 4: z.class_part - z.part}.get(index, 0))
    for total, levels in zip(z.flat, z.levels):
        scratch += flat_buffers(total, levels)
    dma = pltpu.SemaphoreType.DMA
    scratch += [
        dma((11,)), dma((11,)), dma((len(HUB_SUMS), 3)), dma((len(HUB_SUMS), 3)), dma((len(z.flat), 8)), dma((len(z.flat), 8)), dma((4 + z.halves,))
    ]
    inside = pl.BlockSpec(memory_space=pltpu.VMEM)
    outside = pl.BlockSpec(memory_space=pl.ANY)
    return pl.pallas_call(
        functools.partial(train_kernel, z),
        out_shape=(
            *[jax.ShapeDtypeStruct((total, LANES), f) for total in z.flat],
            jax.ShapeDtypeStruct((2, halo, hid), f),
            jax.ShapeDtypeStruct((8, LANES), f),
        ),
        in_specs=[inside] * 11 + [outside] + [inside] * 4,
        out_specs=(outside, outside, outside, outside, outside, inside),
        scratch_shapes=scratch,
        compiler_params=pltpu.CompilerParams(
            collective_id=0, has_side_effects=True, vmem_limit_bytes=62 * 1024 * 1024
        ),
        name="train",
    )(*args)


def update_kernel(
    z,
    two_hbm, upper_hbm, low_a_hbm, low_b_hbm, fresh_hbm, w1_hbm, m1_hbm, v1_hbm, w2_hbm, m2_hbm, v2_hbm,
    misc, w3, m3, v3, bs, mb, vb,
    o1, n1, s1, c1, o2, n2, s2, c2, o_fresh,
    o_norm, o_loss, o_count, o3, n3, s3, c3, ob, nb, sb, cb,
    two, upper, low_a, low_b, held, w1, m1, v1, w2, m2, v2, d1, d2, in_sem, out_sem,
):
    inward = [
        pltpu.make_async_copy(src, dst, in_sem.at[i])
        for i, (src, dst) in enumerate(
            (
                (two_hbm, two), (upper_hbm, upper), (low_a_hbm, low_a), (low_b_hbm, low_b),
                (w1_hbm, w1), (m1_hbm, m1), (v1_hbm, v1), (w2_hbm, w2), (m2_hbm, m2), (v2_hbm, v2), (fresh_hbm, held),
            )
        )
    ]
    for copy in inward:
        copy.start()
    outward = []

    def leave(src, dst, rows=None):
        if rows is not None:
            src, dst = src.at[rows], dst.at[rows]
        outward.append(pltpu.make_async_copy(src, dst, out_sem.at[len(outward)]))
        outward[-1].start()

    def squares(values):
        return jnp.sum(jnp.sum(values * values, axis=0, keepdims=True), axis=1, keepdims=True)

    at_loss = z.at_bias + 2 * z.halves + 1
    for copy in inward[:4]:
        copy.wait()
    norm = jnp.sqrt(
        squares(two[...]) + squares(upper[0:at_loss, :]) + squares(low_a[...]) + squares(low_b[...])
    )
    o_norm[...] = norm
    o_loss[...] = upper[at_loss : at_loss + 1, 0:1]
    o_count[...] = misc[z.count_rows : z.count_rows + 1, 0:1]
    factor = jnp.minimum(1.0, CLIP / (norm + 1e-06))

    def step(grad, old, first, second):
        clipped = grad * factor
        moment = 0.5 * first + 0.5 * clipped
        squared = 0.5 * second + 0.5 * clipped * clipped
        below = jnp.sqrt(squared * (1.0 / CORRECT)) + EPSILON
        fresh = old * (1.0 - RATE * DECAY) - (moment * (RATE / CORRECT)) / below
        return fresh, moment, squared

    def renew(rows, lanes, grad, w, m, v):
        w[rows, lanes], m[rows, lanes], v[rows, lanes] = step(grad, w[rows, lanes], m[rows, lanes], v[rows, lanes])

    def lane_half(half):
        return slice(half * LANES, (half + 1) * LANES)

    low = z.fin - z.shift
    lows = (low_a, low_b)
    for copy in inward[4:7]:
        copy.wait()
    for half in range(z.halves):
        u0 = half * z.frows
        renew(slice(0, low), lane_half(half), upper[u0 : u0 + low, :], w1, m1, v1)
    for src, dst in ((w1, o1), (m1, n1), (v1, s1)):
        leave(src, dst, pl.ds(0, low))
    for half in range(z.halves):
        u0, lower, lanes = half * z.frows, lows[half], lane_half(half)
        if z.shift:
            renew(slice(low, low + 8), lanes, upper[u0 + low : u0 + low + 8, :] + lower[0:8, :], w1, m1, v1)
            renew(slice(low + 8, 2 * z.fin), lanes, lower[8 : z.fin + z.shift, :], w1, m1, v1)
        else:
            renew(slice(low, 2 * z.fin), lanes, lower[0 : z.fin, :], w1, m1, v1)
    for src, dst in ((w1, o1), (m1, n1), (v1, s1)):
        leave(src, dst, pl.ds(low, 2 * z.fin - low))
    d1[...] = w1[...].astype(BF16)
    leave(d1, c1)
    for copy in inward[7:10]:
        copy.wait()
    for half in range(z.halves):
        start = half * 2 * z.hid
        renew(slice(0, 2 * z.hid), lane_half(half), two[start : start + 2 * z.hid, :], w2, m2, v2)
    for src, dst in ((w2, o2), (m2, n2), (v2, s2)):
        leave(src, dst)
    d2[...] = w2[...].astype(BF16)
    leave(d2, c2)
    inward[10].wait()
    leave(held, o_fresh)
    packed = two[z.at_three : z.at_three + z.hid, :].T
    for half in range(2):
        grad = packed[half * (LANES // 2) : half * (LANES // 2) + z.cls, :]
        part = slice(half * z.hid, (half + 1) * z.hid)
        fresh, moment, squared = step(grad, w3[:, part], m3[:, part], v3[:, part])
        o3[:, part] = fresh
        n3[:, part] = moment
        s3[:, part] = squared
        c3[:, part] = fresh.astype(BF16)
    size = bs.shape[0]
    line = jnp.concatenate([upper[z.at_bias + k : z.at_bias + k + 1, :] for k in range(2 * z.halves + 1)], axis=1)
    flat = lambda ref: ref[...].reshape(1, size)
    fresh, moment, squared = step(line[:, 0:size], flat(bs), flat(mb), flat(vb))
    ob[...] = fresh.reshape(size)
    nb[...] = moment.reshape(size)
    sb[...] = squared.reshape(size)
    cb[...] = ob[...].astype(BF16)
    for copy in outward:
        copy.wait()


def update(z, *args):
    inside = pl.BlockSpec(memory_space=pltpu.VMEM)
    outside = pl.BlockSpec(memory_space=pl.ANY)
    shape = jax.ShapeDtypeStruct
    one, two, three_t, line = args[5].shape, args[8].shape, args[12].shape, args[15].shape

    def group(size):
        return [shape(size, F32)] * 3 + [shape(size, BF16)]

    shapes = [
        *group(one), *group(two), shape(args[4].shape, F32), *[shape((1, 1), F32)] * 3, *group(three_t), *group(line)
    ]
    return pl.pallas_call(
        functools.partial(update_kernel, z),
        out_shape=tuple(shapes),
        in_specs=[outside] * 11 + [inside] * 7,
        out_specs=tuple([outside] * 9 + [inside] * 11),
        scratch_shapes=[
            *[pltpu.VMEM(a.shape, F32) for a in args[:11]],
            pltpu.VMEM(one, BF16), pltpu.VMEM(two, BF16),
            pltpu.SemaphoreType.DMA((11,)), pltpu.SemaphoreType.DMA((12,)),
        ],
        compiler_params=pltpu.CompilerParams(vmem_limit_bytes=62 * 1024 * 1024),
        name="update",
    )(*args)


def solution(mesh):
    def local(
        features, hub_features, low_lists, low_masks, high_lists, high_masks, hub_lists, hub_masks, send_rows,
        labels, train_mask, stale_rows, weight_one, weight_two, weight_three, biases,
        mean_one, mean_two, mean_three, mean_biases, square_one, square_two, square_three, square_biases,
    ):
        z = Sizes(mesh, features, low_lists, high_lists, hub_lists, send_rows, weight_one, weight_three)
        three_t = weight_three.T
        two, upper, low_first, low_second, renewed, misc = train(
            z, features.T, hub_features.T, low_lists.T, low_masks.T, high_lists.T, high_masks.T,
            hub_lists[0].T, hub_masks[0].T, send_rows[0],
            labels.reshape(-1, LANES), train_mask.reshape(-1, LANES), stale_rows,
            weight_one, weight_two, three_t, biases,
        )
        o1, n1, s1, c1, o2, n2, s2, c2, renewed, norm, loss, count, o3, n3, s3, c3, ob, nb, sb, cb = update(
            z, two, upper, low_first, low_second, renewed, weight_one, mean_one, square_one,
            weight_two, mean_two, square_two, misc, three_t, mean_three.T, square_three.T,
            biases, mean_biases, square_biases,
        )
        return (
            norm[0, 0], loss[0, 0], count[0, 0],
            o1, o2, o3.T, ob, n1, n2, n3.T, nb, s1, s2, s3.T, sb, c1, c2, c3.T, cb, renewed,
        )

    spread = ("dom", "sub")
    rows, all_same, cube = P(spread, None), P(), P(spread, None, None)
    stale = P(None, spread, None)
    in_specs = (
        rows, all_same, rows, rows, rows, rows, cube, cube, cube, P(spread), P(spread), stale, *[all_same] * 12
    )
    out_specs = (*[all_same] * 19, stale)
    return jax.shard_map(local, mesh=mesh, in_specs=in_specs, out_specs=out_specs, check_vma=False)
```
